32 devices in a mesh: rep: 8 (over y, x, core), exp: 4 (over z).
Axes of the slice: x: 2, y: 2, z: 4, core: 2. Of those that a mesh axis runs over, the one named last changes fastest.
Arguments:
- grad_out: bfloat16 [4096, 3584], P(('rep', 'exp')), may hold values from -6 to 6
- routes: int32 [4096, 4], P(('rep', 'exp')), may hold values from 0 to 15, as said below
- affinity: float32 [4096, 4], P(('rep', 'exp')), may hold values from 0.02 to 0.98
- saved_hidden: bfloat16 [8, 16, 4, 60, 1024], P('rep', 'exp'), may hold values from -0.29882812 to 0.29882812
- down_proj: bfloat16 [1024, 16, 3584], P('rep', 'exp'), may hold values from -0.1875 to 0.1875
Outputs:
- affinity_grad: float32 [4096, 4], P(('rep', 'exp'))
- hidden_grad: bfloat16 [8, 16, 4, 60, 1024], P('rep', 'exp')
- down_grad: float32 [1024, 16, 3584], P('rep', 'exp')
The draws below stay inside these ranges and needn't reach their ends.
Inputs may be any that keep to these rules, and one draw needn't show every extreme that they name: `routes`: each row names 4 different experts. Among the tokens of one device no expert is named more than 60 times; in every replica group one expert is named exactly 60 times by the tokens of each device of the group.
All inputs are finite; a program needn't handle non-finite values.
Results may differ from the reference program's by a relative error of at most 0.02.
Values may be sent and summed in bfloat16 or wider, within the bound.
No kernel may reach another device: no remote copies, remote signals or barrier semaphores. Data moves between devices by JAX's collectives and lax.ppermute only.
A program may use at most 192 MiB of HBM per device.

```python
import math
from functools import partial
import jax
import jax.numpy as jnp
from jax import lax

D = 3584
H = 1024
EXPERTS = 16
TOPK = 4
TOK_DEV = 128
MOST = 60
TOKENS = 4096
N_REP = 8
N_EXP = 4


def device_routes(dev_key, busy_expert):
    key_shuffle, key_space, key_open, key_other, key_rotate = jax.random.split(dev_key, 5)
    shuffle = jax.random.permutation(key_shuffle, TOK_DEV)
    leading = (jnp.arange(TOK_DEV) < MOST).astype(jnp.int32)
    is_busy = jnp.zeros((TOK_DEV,), jnp.int32).at[shuffle].set(leading)
    needed = TOPK - is_busy
    spacing = jax.random.randint(key_space, (TOK_DEV,), 0, 3)
    advance = needed + spacing
    opening = jnp.cumsum(advance) - advance + jax.random.randint(key_open, (), 0, EXPERTS - 1)
    others = jax.random.permutation(key_other, EXPERTS - 1).astype(jnp.int32)
    others = others + (others >= busy_expert).astype(jnp.int32)
    window = (opening[:, None] + jnp.arange(TOPK)[None, :]) % (EXPERTS - 1)
    chosen = others[window]
    with_busy = jnp.concatenate([jnp.broadcast_to(busy_expert, (TOK_DEV, 1)).astype(jnp.int32), chosen[:, :TOPK - 1]], axis=1)
    merged = jnp.where(is_busy[:, None] > 0, with_busy, chosen)
    rotation = jax.random.randint(key_rotate, (TOK_DEV, 1), 0, TOPK)
    column = (jnp.arange(TOPK)[None, :] + rotation) % TOPK
    return jnp.take_along_axis(merged, column, axis=1)


def draw_routes(key, part):
    key_busy, key_rest = jax.random.split(key)
    busiest = jax.random.randint(key_busy, (N_REP,), 0, EXPERTS).astype(jnp.int32)
    busy_devices = jnp.repeat(busiest, N_EXP)
    device_keys = jax.random.split(key_rest, N_REP * N_EXP)
    drawn = jax.vmap(device_routes)(device_keys, busy_devices)
    return drawn.reshape(TOKENS, TOPK).astype(jnp.int32)


def with_spikes(entries, own_key, source, target, blocks, factor):
    def block_of(axis_at):
        return (jnp.arange(entries.shape[axis_at]) // (entries.shape[axis_at] // blocks)).reshape((-1,) + (1,) * (entries.ndim - 1 - axis_at))

    first = jax.random.permutation(own_key, blocks)[block_of(target)]
    other_side = (block_of(target) + blocks // 2) % blocks
    return jnp.where((block_of(source) == first) | (block_of(source) == other_side), factor * entries, entries)


def block_levels(key, shape, cuts, least, high):
    level = 1.0
    for position, blocks in cuts:
        heights = jax.random.uniform(jax.random.fold_in(jax.random.fold_in(key, 6), position), (blocks,), jnp.float32, least / len(cuts), high / len(cuts))
        level = level * jnp.repeat(jnp.exp(heights), shape[position] // blocks).reshape((-1,) + (1,) * (len(shape) - 1 - position))
    return level


def bell_draw(own_key, extent, width, limit, cuts=(), held_as=jnp.bfloat16):
    loudness = block_levels(own_key, extent, cuts, -0.22, 0.18) if cuts else 1.0
    result = jax.random.normal(own_key, extent, jnp.float32) * width * loudness
    return jnp.minimum(jnp.maximum(result, -limit), limit).astype(held_as)


def bell_draw_with(rng, extent, spread, bound, shards, heavy, kind=jnp.bfloat16):
    values = spread * jax.random.normal(rng, extent, jnp.float32)
    if shards:
        values = values * block_levels(rng, extent, shards, -0.22, 0.18)
    return jnp.clip(with_spikes(values, jax.random.fold_in(rng, 3), *heavy), -bound, bound).astype(kind)


def setup_inputs(seed: int = 0) -> dict:
    splits = jax.random.split(jax.random.key(seed), 6)
    grad_out = bell_draw(splits[0], (TOKENS, D), 1.0, 6.0, ((0, 32),))
    routes = draw_routes(jax.random.fold_in(splits[5], 71), 0)
    affinity = jnp.clip(jnp.exp(math.log(0.98) - 3.89182034 * jax.random.uniform(splits[2], (TOKENS, TOPK), jnp.float32) ** block_levels(splits[2], (TOKENS, TOPK), ((0, 32),), -0.2, 0.2)), 0.02, 0.98)
    saved_hidden = bell_draw_with(splits[3], (N_REP, EXPERTS, N_EXP, MOST, H), 0.05, 0.29882812, ((0, 8), (1, 4)), (0, 4, 8, 2.0))
    down_proj = bell_draw(splits[4], (H, EXPERTS, D), H ** -0.5, 0.1875, ((0, 8), (1, 4)))
    return {"grad_out": grad_out, "routes": routes, "affinity": affinity, "saved_hidden": saved_hidden, "down_proj": down_proj}


ROUTE_SCALE = 2.5


def pack_routes(grad_rows, route_ids, route_weight, expert_count, most):
    expert_ids = jnp.arange(expert_count, dtype=jnp.int32)
    naming = jnp.sum((route_ids[:, :, None] == expert_ids[None, None, :]).astype(jnp.int32), axis=1)
    before = jnp.cumsum(naming, axis=0) - naming
    slot_ids = jnp.take_along_axis(before, route_ids, axis=1).astype(jnp.int32)
    placed = (route_ids * most + slot_ids).reshape(-1).astype(jnp.int32)
    token_ids = jnp.repeat(jnp.arange(grad_rows.shape[0], dtype=jnp.int32), route_ids.shape[1])
    source = jnp.zeros((expert_count * most,), jnp.int32).at[placed].set(token_ids)
    filled = jnp.zeros((expert_count * most,), jnp.int32).at[placed].set(1)
    weights = jnp.zeros((expert_count * most,), route_weight.dtype).at[placed].set(route_weight.reshape(-1))
    fetched = jnp.take(grad_rows, source, axis=0)
    packed = jnp.where(filled[:, None] > 0, fetched, jnp.zeros_like(fetched))
    return packed.reshape(expert_count, most, grad_rows.shape[1]), weights.reshape(expert_count, most), placed


def reference(grad_out, routes, affinity, saved_hidden, down_proj):
    grad_grid = grad_out.reshape(N_REP, N_EXP, TOK_DEV, D)
    route_grid = routes.reshape(N_REP, N_EXP, TOK_DEV, TOPK)
    affinity_grid = affinity.reshape(N_REP, N_EXP, TOK_DEV, TOPK)
    weights_wide = down_proj.astype(jnp.float32)
    packer = jax.vmap(partial(pack_routes, expert_count=EXPERTS, most=MOST))

    def per_group(running, inputs):
        grad_group, route_group, affinity_group, hidden_group = inputs
        totals = jnp.sum(affinity_group, axis=-1, keepdims=True)
        shares = affinity_group / totals
        route_weight = (ROUTE_SCALE * shares).astype(jnp.bfloat16)
        packed, packed_weight, placed = packer(grad_group, route_group, route_weight)
        received = jnp.transpose(packed, (1, 0, 2, 3)).reshape(EXPERTS, N_EXP * MOST, D).astype(jnp.float32)
        row_scale = jnp.transpose(packed_weight, (1, 0, 2)).reshape(EXPERTS, N_EXP * MOST).astype(jnp.float32)
        hidden = hidden_group.reshape(EXPERTS, N_EXP * MOST, H).astype(jnp.float32)
        projected = jnp.einsum('erd,hed->erh', received, weights_wide)
        hidden_grad = (row_scale[:, :, None] * projected).astype(jnp.bfloat16)
        combine_grad = ROUTE_SCALE * jnp.sum(hidden * projected, axis=-1)
        scaled = lax.optimization_barrier((row_scale[:, :, None] * received).astype(jnp.bfloat16)).astype(jnp.float32)
        partial_grad = jnp.einsum('erh,erd->hed', hidden, scaled)
        partial_grad = lax.optimization_barrier(partial_grad.astype(jnp.bfloat16)).astype(jnp.float32)
        running = running + partial_grad
        returned = jnp.transpose(combine_grad.reshape(EXPERTS, N_EXP, MOST), (1, 0, 2)).reshape(N_EXP, EXPERTS * MOST)
        route_grad = jnp.take_along_axis(returned, placed, axis=1).reshape(N_EXP, TOK_DEV, TOPK)
        affinity_grad = (route_grad - jnp.sum(route_grad * shares, axis=-1, keepdims=True)) / totals
        return running, (affinity_grad, hidden_grad.reshape(EXPERTS, N_EXP, MOST, H))

    zero_grad = jnp.zeros((H, EXPERTS, D), jnp.float32)
    down_grad, outputs = lax.scan(per_group, zero_grad, (grad_grid, route_grid, affinity_grid, saved_hidden))
    affinity_grad, hidden_grad = outputs
    return affinity_grad.reshape(TOKENS, TOPK), hidden_grad, down_grad
```

```python
import functools
import jax
import jax.numpy as jnp
from jax import lax
from jax.experimental import pallas as pl
from jax.experimental.pallas import tpu as pltpu
from jax.sharding import PartitionSpec as P

ROUTE_SCALE = 2.5


def pack_routes(grad_rows, route_ids, route_weight, expert_count, most):
    expert_ids = jnp.arange(expert_count, dtype=jnp.int32)
    naming = jnp.sum((route_ids[:, :, None] == expert_ids[None, None, :]).astype(jnp.int32), axis=1)
    before = jnp.cumsum(naming, axis=0) - naming
    slot_ids = jnp.take_along_axis(before, route_ids, axis=1)
    placed = (route_ids * most + slot_ids).reshape(-1)
    token_ids = jnp.repeat(jnp.arange(grad_rows.shape[0], dtype=jnp.int32), route_ids.shape[1])
    source = jnp.zeros((expert_count * most,), jnp.int32).at[placed].set(token_ids)
    filled = jnp.zeros((expert_count * most,), jnp.int32).at[placed].set(1)
    weights = (
        jnp.zeros((expert_count * most,), route_weight.dtype)
        .at[placed]
        .set(route_weight.reshape(-1))
    )
    fetched = jnp.take(grad_rows, source, axis=0)
    packed = jnp.where(filled[:, None] > 0, fetched, jnp.zeros_like(fetched))
    return (packed, weights, placed)


def on_device_weights(grad_out, routes, affinity, saved_hidden, down_proj):
    exp_devices = lax.axis_size("exp")
    local_experts = down_proj.shape[1]
    expert_count = exp_devices * local_experts
    most = saved_hidden.shape[3]
    width = grad_out.shape[1]
    hidden_units = saved_hidden.shape[4]
    row_count = exp_devices * most
    totals = jnp.sum(affinity, axis=-1, keepdims=True)
    shares = affinity / totals
    route_weight = (ROUTE_SCALE * shares).astype(jnp.bfloat16)
    packed, weights, placed = pack_routes(grad_out, routes, route_weight, expert_count, most)
    outgoing = packed.reshape(exp_devices, local_experts, 1, most, width)
    outgoing_weight = weights.reshape(exp_devices, local_experts, 1, most)
    received, received_weight = (
        lax.all_to_all(outgoing, "exp", split_axis=0, concat_axis=2, tiled=True),
        lax.all_to_all(outgoing_weight, "exp", split_axis=0, concat_axis=2, tiled=True),
    )
    received = received.reshape(local_experts, row_count, width)
    row_scale = received_weight.reshape(local_experts, row_count).astype(jnp.float32)
    hidden = saved_hidden.reshape(local_experts, row_count, hidden_units)
    gathered = lax.all_gather(down_proj, "rep", axis=0, tiled=True)
    projected = jnp.einsum("erd,hed->erh", received, gathered, preferred_element_type=jnp.float32)
    hidden_grad = (row_scale[:, :, None] * projected).astype(jnp.bfloat16)
    combine_grad = ROUTE_SCALE * jnp.sum(hidden.astype(jnp.float32) * projected, axis=-1)
    scaled = (row_scale[:, :, None] * received.astype(jnp.float32)).astype(jnp.bfloat16)
    grad_term = jnp.einsum("erh,erd->hed", hidden, scaled, preferred_element_type=jnp.float32)
    down_grad = lax.psum_scatter(
        grad_term.astype(jnp.bfloat16), "rep", scatter_dimension=0, tiled=True
    ).astype(jnp.float32)
    returned = lax.all_to_all(
        combine_grad.reshape(local_experts, exp_devices, most),
        "exp",
        split_axis=1,
        concat_axis=0,
        tiled=True,
    )
    route_grad = jnp.take(returned.reshape(-1), placed).reshape(routes.shape)
    affinity_grad = (route_grad - jnp.sum(route_grad * shares, axis=-1, keepdims=True)) / totals
    return (affinity_grad, hidden_grad.reshape(saved_hidden.shape), down_grad)


SLOT_PAD = 64
F32 = jnp.float32
BF16 = jnp.bfloat16


def nt_dot(a, b):
    return lax.dot_general(a, b, (((1,), (1,)), ((), ())), preferred_element_type=F32)


def tn_dot(a, b):
    return lax.dot_general(a, b, (((0,), (0,)), ((), ())), preferred_element_type=F32)


def project_kernel(
    top_k, idx_ref, rows_ref, weight_ref, hidden_ref, meta_ref, grad_ref, combine_ref, scatter_ref, terms
):
    reps, experts, slots, block = grad_ref.shape
    tokens = rows_ref.shape[0] // reps
    base = idx_ref[1].astype(F32)
    projected = nt_dot(rows_ref[...], weight_ref[...])
    earlier = (
        lax.broadcasted_iota(jnp.int32, (tokens, tokens), 0)
        < lax.broadcasted_iota(jnp.int32, (tokens, tokens), 1)
    ).astype(BF16)
    expert_ids = lax.broadcasted_iota(jnp.int32, (8, tokens), 0).astype(F32) + base
    slot_ids = lax.broadcasted_iota(jnp.int32, (slots, tokens), 0).astype(F32)
    ones = jnp.ones((8, block), BF16)
    for rep in range(reps):
        meta = meta_ref[rep, 0]
        named = jnp.zeros((8, tokens), F32)
        scale = jnp.zeros((8, tokens), F32)
        for k in range(top_k):
            hit = meta[k : k + 1, :] == expert_ids
            named = jnp.where(hit, 1.0, named)
            scale = jnp.where(hit, meta[top_k + k : top_k + k + 1, :], scale)
        before = jnp.dot(named.astype(BF16), earlier, preferred_element_type=F32)
        slot = jnp.where(named > 0, before, -1.0)
        scale_columns = jnp.transpose(scale)
        span = slice(rep * tokens, (rep + 1) * tokens)
        for e in range(experts):
            pick = (slot[e : e + 1, :] == slot_ids).astype(BF16)
            column = scale_columns[:, e : e + 1]
            own = projected[span, e * block : (e + 1) * block]
            hidden = tn_dot(pick, hidden_ref[rep, e, 0])
            grad_ref[rep, e] = jnp.dot(
                pick, (column * own).astype(BF16), preferred_element_type=F32
            ).astype(BF16)
            product = hidden * own
            high = product.astype(BF16)
            low = (product - high.astype(F32)).astype(BF16)
            combine_ref[rep, e : e + 1] = (nt_dot(ones, high) + nt_dot(ones, low))[0:1]
            terms[span, e * block : (e + 1) * block] = (column * hidden).astype(BF16)
    width = experts * block
    row = lax.broadcasted_iota(jnp.int32, (width, width), 0)
    col = lax.broadcasted_iota(jnp.int32, (width, width), 1)
    order = (col == lax.rem(row, experts) * block + lax.div(row, experts)).astype(BF16)
    scatter_ref[...] = nt_dot(order, terms[...]).astype(BF16)


def project(index, rows, weight, hidden, meta, top_k, step_reps):
    reps, experts, sources, slots, block = hidden.shape
    tokens = rows.shape[0] // reps
    width = rows.shape[1]
    count = step_reps * tokens
    return pl.pallas_call(
        functools.partial(project_kernel, top_k),
        grid_spec=pltpu.PrefetchScalarGridSpec(
            num_scalar_prefetch=1,
            grid=(reps // step_reps,),
            in_specs=[
                pl.BlockSpec((count, width), lambda i, idx: (i, 0)),
                pl.BlockSpec((experts * block, width), lambda i, idx: (0, 0)),
                pl.BlockSpec((step_reps, experts, 1, slots, block), lambda i, idx: (i, 0, idx[0], 0, 0)),
                pl.BlockSpec((step_reps, 1, 2 * top_k, tokens), lambda i, idx: (i, idx[0], 0, 0)),
            ],
            out_specs=[
                pl.BlockSpec((step_reps, experts, slots, block), lambda i, idx: (i, 0, 0, 0)),
                pl.BlockSpec((step_reps, experts, tokens), lambda i, idx: (i, 0, 0)),
                pl.BlockSpec((experts * block, count), lambda i, idx: (0, i)),
            ],
            scratch_shapes=[pltpu.VMEM((count, experts * block), BF16)],
        ),
        out_shape=[
            jax.ShapeDtypeStruct((reps, experts, slots, block), BF16),
            jax.ShapeDtypeStruct((reps, experts, tokens), F32),
            jax.ShapeDtypeStruct((experts * block, reps * tokens), BF16),
        ],
        compiler_params=pltpu.CompilerParams(vmem_limit_bytes=40 * 2**20),
        cost_estimate=pl.CostEstimate(
            flops=2 * reps * tokens * width * experts * block,
            bytes_accessed=2 * (rows.size + weight.size),
            transcendentals=0,
        ),
    )(index, rows, weight, hidden, meta)


def weight_grad_kernel(first, last, *refs):
    if first:
        scatter_ref, rows_ref, out_ref = refs
        total = jnp.dot(scatter_ref[...], rows_ref[...], preferred_element_type=F32)
    else:
        scatter_ref, rows_ref, before_ref, out_ref = refs[:4]
        total = before_ref[...] + jnp.dot(scatter_ref[...], rows_ref[...], preferred_element_type=F32)
    if not last:
        out_ref[...] = total
        return
    held = refs[4]
    held[...] = total
    experts = out_ref.shape[1]

    group = 8 // experts

    def move(i, carry):
        both = held[pl.ds(pl.multiple_of(i * 8, 8), 8), :]
        for j in range(group):
            out_ref[i * group + j] = both[j * experts : (j + 1) * experts]
        return carry

    lax.fori_loop(0, out_ref.shape[0] // group, move, 0, unroll=4)


def weight_grad(scatter, rows, before, last, experts, tile):
    height, count = scatter.shape
    width = rows.shape[1]
    block = height // experts
    first = before is None
    in_specs = [
        pl.BlockSpec((height, count), lambda i: (0, 0)),
        pl.BlockSpec((count, tile), lambda i: (0, i)),
    ]
    args = [scatter, rows]
    if not first:
        in_specs.append(pl.BlockSpec((height, tile), lambda i: (0, i)))
        args.append(before)
    if last:
        out_spec = pl.BlockSpec((block, experts, tile), lambda i: (0, 0, i))
        out_shape = jax.ShapeDtypeStruct((block, experts, width), F32)
        scratch = [pltpu.VMEM((height, tile), F32)]
    else:
        out_spec = pl.BlockSpec((height, tile), lambda i: (0, i))
        out_shape = jax.ShapeDtypeStruct((height, width), F32)
        scratch = []
    return pl.pallas_call(
        functools.partial(weight_grad_kernel, first, last),
        grid=(width // tile,),
        in_specs=in_specs,
        out_specs=out_spec,
        out_shape=out_shape,
        scratch_shapes=scratch,
        input_output_aliases={2: 0} if not first and not last else {},
        compiler_params=pltpu.CompilerParams(vmem_limit_bytes=40 * 2**20),
        cost_estimate=pl.CostEstimate(
            flops=2 * height * count * width,
            bytes_accessed=2 * (scatter.size + rows.size) + 8 * height * width,
            transcendentals=0,
        ),
    )(*args)


def on_device_tokens(grad_out, routes, affinity, saved_hidden, down_proj):
    reps, sources = lax.axis_size("rep"), lax.axis_size("exp")
    block, experts, width = down_proj.shape
    tokens, top_k = routes.shape
    most, hidden_units = saved_hidden.shape[3:]
    me = lax.axis_index("exp")
    totals = jnp.sum(affinity, axis=-1, keepdims=True)
    shares = affinity / totals
    route_weight = (ROUTE_SCALE * shares).astype(BF16).astype(F32)
    meta = jnp.concatenate([routes.astype(F32).T, route_weight.T], axis=0)
    meta = lax.all_gather(meta, ("rep", "exp"), axis=0).reshape(reps, sources, 2 * top_k, tokens)
    weight = jnp.transpose(down_proj, (1, 0, 2)).reshape(experts * block, width)
    pieces = saved_hidden.reshape(experts, sources, most, reps, block)
    pieces = jnp.transpose(pieces, (3, 0, 1, 2, 4))
    pieces = jnp.pad(pieces, ((0, 0), (0, 0), (0, 0), (0, SLOT_PAD - most), (0, 0)))
    hidden = lax.all_to_all(pieces, "rep", split_axis=0, concat_axis=0, tiled=True)
    ring = [(i, (i + 1) % sources) for i in range(sources)]
    carried = grad_out
    total = None
    grads, combines = [], []
    for step in range(sources):
        rows = lax.all_gather(carried, "rep", axis=0, tiled=True)
        if step < sources - 1:
            carried = lax.ppermute(carried, "exp", ring)
        source = lax.rem(me - step + sources, sources)
        index = jnp.stack([source, me * experts]).astype(jnp.int32)
        grad, combine, scatter = project(index, rows, weight, hidden, meta, top_k, 2)
        total = weight_grad(scatter, rows, total, step == sources - 1, experts, 512)
        grads.append(lax.all_to_all(grad, "rep", split_axis=0, concat_axis=0, tiled=True))
        combines.append(combine)
    at_source = lax.rem(me - jnp.arange(sources) + sources, sources)
    grads = jnp.take(jnp.stack(grads), at_source, axis=0)[:, :, :, :most]
    hidden_grad = jnp.transpose(grads, (2, 0, 3, 1, 4)).reshape(saved_hidden.shape)
    combine = jnp.take(jnp.stack(combines, axis=1), at_source, axis=1)
    combine = combine.reshape(reps * sources, experts, tokens)
    combine = lax.all_to_all(combine, ("rep", "exp"), split_axis=0, concat_axis=0, tiled=True)
    combine = jnp.sum(combine.reshape(reps, sources * experts, tokens), axis=0)
    expert_ids = jnp.arange(sources * experts, dtype=routes.dtype)
    named = routes.T[:, None, :] == expert_ids[None, :, None]
    route_grad = ROUTE_SCALE * jnp.sum(jnp.where(named, combine[None], 0.0), axis=1).T
    affinity_grad = (route_grad - jnp.sum(route_grad * shares, axis=-1, keepdims=True)) / totals
    return (affinity_grad, hidden_grad, total)


def on_device(grad_out, routes, affinity, saved_hidden, down_proj):
    reps, sources = lax.axis_size("rep"), lax.axis_size("exp")
    block, experts, width = down_proj.shape
    tokens = grad_out.shape[0]
    most = saved_hidden.shape[3]
    fits = block % 128 == 0 and tokens % 128 == 0 and width % 512 == 0 and 8 % experts == 0
    fits = fits and most <= SLOT_PAD and reps % 2 == 0 and routes.shape[1] == 4
    if fits and reps * sources * tokens <= 2 * reps * block * experts:
        return on_device_tokens(grad_out, routes, affinity, saved_hidden, down_proj)
    return on_device_weights(grad_out, routes, affinity, saved_hidden, down_proj)


def solution(mesh):
    return jax.shard_map(
        on_device,
        mesh=mesh,
        in_specs=(
            P(("rep", "exp"), None),
            P(("rep", "exp"), None),
            P(("rep", "exp"), None),
            P("rep", "exp", None, None, None),
            P("rep", "exp", None),
        ),
        out_specs=(
            P(("rep", "exp"), None),
            P("rep", "exp", None, None, None),
            P("rep", "exp", None),
        ),
        check_vma=False,
    )
```

```python
import functools
import jax
import jax.numpy as jnp
from jax import lax
from jax.experimental import pallas as pl
from jax.experimental.pallas import tpu as pltpu
from jax.sharding import PartitionSpec as P

ROUTE_SCALE = 2.5


def pack_routes(grad_rows, route_ids, route_weight, expert_count, most):
    expert_ids = jnp.arange(expert_count, dtype=jnp.int32)
    naming = jnp.sum((route_ids[:, :, None] == expert_ids[None, None, :]).astype(jnp.int32), axis=1)
    before = jnp.cumsum(naming, axis=0) - naming
    slot_ids = jnp.take_along_axis(before, route_ids, axis=1)
    placed = (route_ids * most + slot_ids).reshape(-1)
    token_ids = jnp.repeat(jnp.arange(grad_rows.shape[0], dtype=jnp.int32), route_ids.shape[1])
    source = jnp.zeros((expert_count * most,), jnp.int32).at[placed].set(token_ids)
    filled = jnp.zeros((expert_count * most,), jnp.int32).at[placed].set(1)
    weights = (
        jnp.zeros((expert_count * most,), route_weight.dtype)
        .at[placed]
        .set(route_weight.reshape(-1))
    )
    fetched = jnp.take(grad_rows, source, axis=0)
    packed = jnp.where(filled[:, None] > 0, fetched, jnp.zeros_like(fetched))
    return (packed, weights, placed)


def on_device_weights(grad_out, routes, affinity, saved_hidden, down_proj):
    exp_devices = lax.axis_size("exp")
    local_experts = down_proj.shape[1]
    expert_count = exp_devices * local_experts
    most = saved_hidden.shape[3]
    width = grad_out.shape[1]
    hidden_units = saved_hidden.shape[4]
    row_count = exp_devices * most
    totals = jnp.sum(affinity, axis=-1, keepdims=True)
    shares = affinity / totals
    route_weight = (ROUTE_SCALE * shares).astype(jnp.bfloat16)
    packed, weights, placed = pack_routes(grad_out, routes, route_weight, expert_count, most)
    outgoing = packed.reshape(exp_devices, local_experts, 1, most, width)
    outgoing_weight = weights.reshape(exp_devices, local_experts, 1, most)
    received, received_weight = (
        lax.all_to_all(outgoing, "exp", split_axis=0, concat_axis=2, tiled=True),
        lax.all_to_all(outgoing_weight, "exp", split_axis=0, concat_axis=2, tiled=True),
    )
    received = received.reshape(local_experts, row_count, width)
    row_scale = received_weight.reshape(local_experts, row_count).astype(jnp.float32)
    hidden = saved_hidden.reshape(local_experts, row_count, hidden_units)
    gathered = lax.all_gather(down_proj, "rep", axis=0, tiled=True)
    projected = jnp.einsum("erd,hed->erh", received, gathered, preferred_element_type=jnp.float32)
    hidden_grad = (row_scale[:, :, None] * projected).astype(jnp.bfloat16)
    combine_grad = ROUTE_SCALE * jnp.sum(hidden.astype(jnp.float32) * projected, axis=-1)
    scaled = (row_scale[:, :, None] * received.astype(jnp.float32)).astype(jnp.bfloat16)
    grad_term = jnp.einsum("erh,erd->hed", hidden, scaled, preferred_element_type=jnp.float32)
    down_grad = lax.psum_scatter(
        grad_term.astype(jnp.bfloat16), "rep", scatter_dimension=0, tiled=True
    ).astype(jnp.float32)
    returned = lax.all_to_all(
        combine_grad.reshape(local_experts, exp_devices, most),
        "exp",
        split_axis=1,
        concat_axis=0,
        tiled=True,
    )
    route_grad = jnp.take(returned.reshape(-1), placed).reshape(routes.shape)
    affinity_grad = (route_grad - jnp.sum(route_grad * shares, axis=-1, keepdims=True)) / totals
    return (affinity_grad, hidden_grad.reshape(saved_hidden.shape), down_grad)


SLOT_PAD = 64
F32 = jnp.float32
BF16 = jnp.bfloat16
VMEM_BYTES = 40 * 2**20


def nt_dot(a, b):
    return lax.dot_general(a, b, (((1,), (1,)), ((), ())), preferred_element_type=F32)


def tn_dot(a, b):
    return lax.dot_general(a, b, (((0,), (0,)), ((), ())), preferred_element_type=F32)


def project_kernel(top_k, sizes, idx_ref, *refs):
    parts = len(sizes)
    pieces, (weight_ref,) = refs[:parts], refs[parts : parts + 1]
    hidden_refs = refs[parts + 1 : parts + 5]
    grad_refs = refs[parts + 5 : parts + 9]
    scatter_ref, rows_out, rows, sems, out_sem = refs[parts + 9 :]
    e = pl.program_id(0)
    slots, pair = grad_refs[0].shape[1:]
    tokens = rows.shape[0] // 4
    spare = slots - 8
    store = pltpu.make_async_copy(rows, rows_out, out_sem)

    @pl.when(e == 0)
    def _():
        copies, at = [], 0
        for i, size in enumerate(sizes):
            copies.append(pltpu.make_async_copy(pieces[i], rows.at[at : at + size], sems.at[i]))
            at += size
        for copy in copies:
            copy.start()
        for copy in copies:
            copy.wait()
        store.start()

    projected = nt_dot(weight_ref[...], rows[...])
    earlier = (
        lax.broadcasted_iota(jnp.int32, (tokens, tokens), 0)
        < lax.broadcasted_iota(jnp.int32, (tokens, tokens), 1)
    ).astype(BF16)
    slot_ids = lax.broadcasted_iota(jnp.int32, (slots, tokens), 0).astype(F32)
    slot_rows = lax.broadcasted_iota(jnp.int32, (slots, pair), 0)
    expert = (idx_ref[1] + e).astype(F32)
    for m in range(4):
        held = hidden_refs[m][0, 0]
        meta = held[spare:].astype(F32)[8 - top_k :]
        named = jnp.zeros((1, tokens), F32)
        scale = jnp.zeros((1, tokens), F32)
        for k in range(top_k):
            hit = meta[k : k + 1, :tokens] == expert
            named = jnp.where(hit, 1.0, named)
            scale = jnp.where(hit, meta[k : k + 1, tokens:], scale)
        before = jnp.dot(
            jnp.broadcast_to(named, (8, tokens)).astype(BF16), earlier, preferred_element_type=F32
        )[0:1]
        slot = jnp.where(named > 0, before, -1.0)
        pick = (slot == slot_ids).astype(BF16)
        own = projected[:, m * tokens : (m + 1) * tokens]
        hidden = tn_dot(held, pick)
        grad = nt_dot(pick, (scale * own).astype(BF16))
        combine = jnp.sum(hidden * own, axis=0, keepdims=True)
        high = combine.astype(BF16).astype(F32)
        partial = jnp.concatenate([high, combine - high], axis=1)
        grad_refs[m][0] = jnp.where(slot_rows == slots - top_k, partial, grad).astype(BF16)
        scatter = (scale * hidden).astype(BF16)
        for half in range(2):
            scatter_ref[half, :, m * tokens : (m + 1) * tokens] = scatter[
                half * (pair // 2) : (half + 1) * (pair // 2)
            ]

    @pl.when(e == pl.num_programs(0) - 1)
    def _():
        store.wait()


def project(index, pieces, weight, hidden, top_k):
    experts, sources, slots, pair = hidden[0].shape
    width = weight.shape[1]
    sizes = [p.shape[0] for p in pieces]
    count = sum(sizes)
    block = pair // 2
    return pl.pallas_call(
        functools.partial(project_kernel, top_k, sizes),
        grid_spec=pltpu.PrefetchScalarGridSpec(
            num_scalar_prefetch=1,
            grid=(experts,),
            in_specs=[pl.BlockSpec(memory_space=pl.ANY)] * len(sizes)
            + [pl.BlockSpec((pair, width), lambda e, idx: (e, 0))]
            + [pl.BlockSpec((1, 1, slots, pair), lambda e, idx: (e, idx[0], 0, 0))] * 4,
            out_specs=[pl.BlockSpec((1, slots, pair), lambda e, idx: (e, 0, 0))] * 4
            + [
                pl.BlockSpec((2, block, count), lambda e, idx: (0, e, 0)),
                pl.BlockSpec(memory_space=pl.ANY),
            ],
            scratch_shapes=[
                pltpu.VMEM((count, width), BF16),
                pltpu.SemaphoreType.DMA((len(sizes),)),
                pltpu.SemaphoreType.DMA,
            ],
        ),
        out_shape=[jax.ShapeDtypeStruct((experts, slots, pair), BF16)] * 4
        + [
            jax.ShapeDtypeStruct((2, experts * block, count), BF16),
            jax.ShapeDtypeStruct((count, width), BF16),
        ],
        compiler_params=pltpu.CompilerParams(vmem_limit_bytes=VMEM_BYTES),
        cost_estimate=pl.CostEstimate(
            flops=4 * count * width * experts * pair,
            bytes_accessed=2 * (2 * count * width + weight.size),
            transcendentals=0,
        ),
    )(index, *pieces, weight, *hidden)


def early_grad_kernel(terms, *refs):
    out_ref = refs[-1]
    for half in range(2):
        total = jnp.dot(refs[0][half], refs[terms][...], preferred_element_type=F32)
        for i in range(1, terms):
            total += jnp.dot(refs[i][half], refs[terms + i][...], preferred_element_type=F32)
        out_ref[half] = total


def early_grad(scatters, rows, tile):
    _, height, count = scatters[0].shape
    width = rows[0].shape[1]
    terms = len(rows)
    return pl.pallas_call(
        functools.partial(early_grad_kernel, terms),
        grid=(width // tile,),
        in_specs=[pl.BlockSpec((2, height, count), lambda i: (0, 0, 0))] * terms
        + [pl.BlockSpec((count, tile), lambda i: (0, i))] * terms,
        out_specs=pl.BlockSpec((2, height, tile), lambda i: (0, 0, i)),
        out_shape=jax.ShapeDtypeStruct((2, height, width), F32),
        compiler_params=pltpu.CompilerParams(vmem_limit_bytes=VMEM_BYTES),
        cost_estimate=pl.CostEstimate(
            flops=4 * height * count * width * terms,
            bytes_accessed=2 * terms * (rows[0].size + scatters[0].size) + 8 * height * width,
            transcendentals=0,
        ),
    )(*scatters, *rows)


def partner_grad_kernel(idx_ref, scatter_ref, rows_ref, before_ref, out_ref):
    total = before_ref[0] + jnp.dot(scatter_ref[0], rows_ref[...], preferred_element_type=F32)
    out_ref[...] = total.astype(BF16)


def own_grad_kernel(idx_ref, scatter_ref, rows_ref, before_ref, arrived_ref, out_ref, held):
    total = before_ref[0] + jnp.dot(scatter_ref[0], rows_ref[...], preferred_element_type=F32)
    total += arrived_ref[...].astype(F32)
    block, experts, _ = out_ref.shape
    held[...] = total

    def move(h, carry):
        out_ref[h] = jnp.concatenate([held[pl.ds(e * block + h, 1), :] for e in range(experts)], axis=0)
        return carry

    lax.fori_loop(0, block, move, 0, unroll=8)


def late_grad(index, scatter, rows, before, arrived, experts, tile):
    _, height, count = scatter.shape
    width = rows.shape[1]
    in_specs = [
        pl.BlockSpec((1, height, count), lambda i, idx: (idx[0], 0, 0)),
        pl.BlockSpec((count, tile), lambda i, idx: (0, i)),
        pl.BlockSpec((1, height, tile), lambda i, idx: (idx[0], 0, i)),
    ]
    args = [scatter, rows, before]
    if arrived is None:
        kernel, scratch = partner_grad_kernel, []
        out_spec = pl.BlockSpec((height, tile), lambda i, idx: (0, i))
        out_shape = jax.ShapeDtypeStruct((height, width), BF16)
    else:
        kernel, scratch = own_grad_kernel, [pltpu.VMEM((height, tile), F32)]
        in_specs.append(pl.BlockSpec((height, tile), lambda i, idx: (0, i)))
        args.append(arrived)
        out_spec = pl.BlockSpec((height // experts, experts, tile), lambda i, idx: (0, 0, i))
        out_shape = jax.ShapeDtypeStruct((height // experts, experts, width), F32)
    return pl.pallas_call(
        kernel,
        grid_spec=pltpu.PrefetchScalarGridSpec(
            num_scalar_prefetch=1,
            grid=(width // tile,),
            in_specs=in_specs,
            out_specs=out_spec,
            scratch_shapes=scratch,
        ),
        out_shape=out_shape,
        compiler_params=pltpu.CompilerParams(vmem_limit_bytes=VMEM_BYTES),
        cost_estimate=pl.CostEstimate(
            flops=2 * height * count * width,
            bytes_accessed=2 * (rows.size + scatter.size) + 8 * height * width,
            transcendentals=0,
        ),
    )(index, *args)


def place_kernel(top_k, first, idx_ref, *refs):
    pieces = refs[:4]
    out_ref, sum_ref = refs[-2:]
    experts, slots, pair = pieces[0].shape
    m = pl.program_id(0)

    @pl.when(m == 0)
    def _():
        sum_ref[...] = jnp.zeros_like(sum_ref)

    for i in range(4):

        @pl.when(m == i)
        def _():
            out_ref[0] = pieces[i][...]
            for e in range(experts):
                row = pieces[i][e, slots - 8 :].astype(F32)[8 - top_k : 9 - top_k]
                sum_ref[e : e + 1] += row[:, : pair // 2] + row[:, pair // 2 :]


def place(index, pieces, before, sources, top_k):
    experts, slots, pair = pieces[0].shape
    first = before is None
    shape = (sources, experts, slots, 4 * pair)
    return pl.pallas_call(
        functools.partial(place_kernel, top_k, first),
        grid_spec=pltpu.PrefetchScalarGridSpec(
            num_scalar_prefetch=1,
            grid=(4,),
            in_specs=[pl.BlockSpec((experts, slots, pair), lambda m, idx: (0, 0, 0))] * 4
            + ([] if first else [pl.BlockSpec(memory_space=pl.ANY)]),
            out_specs=[
                pl.BlockSpec((1, experts, slots, pair), lambda m, idx: (idx[0], 0, 0, idx[1 + m])),
                pl.BlockSpec((experts, pair // 2), lambda m, idx: (0, 0)),
            ],
        ),
        out_shape=[
            jax.ShapeDtypeStruct(shape, BF16),
            jax.ShapeDtypeStruct((experts, pair // 2), F32),
        ],
        input_output_aliases={} if first else {5: 0},
        compiler_params=pltpu.CompilerParams(vmem_limit_bytes=VMEM_BYTES),
        cost_estimate=pl.CostEstimate(
            flops=0, bytes_accessed=16 * experts * slots * pair, transcendentals=0
        ),
    )(index, *pieces, *([] if first else [before]))


def on_device_tokens(grad_out, routes, affinity, saved_hidden, down_proj):
    reps, sources = lax.axis_size("rep"), lax.axis_size("exp")
    block, experts, width = down_proj.shape
    tokens, top_k = routes.shape
    most, hidden_units = saved_hidden.shape[3:]
    pair = 2 * block
    me = lax.axis_index("exp")
    rep = lax.axis_index("rep")
    chip, core = lax.div(rep, 2), lax.rem(rep, 2)
    chips = [jnp.bitwise_xor(chip, m) for m in range(4)]

    def across(array, bits):
        return lax.ppermute(array, "rep", [(i, i ^ bits) for i in range(reps)])

    def around(array, shift):
        return lax.ppermute(array, "exp", [(i, (i + shift) % sources) for i in range(sources)])

    totals = jnp.sum(affinity, axis=-1, keepdims=True)
    shares = affinity / totals
    route_weight = (ROUTE_SCALE * shares).astype(BF16)
    meta = jnp.concatenate([routes.astype(BF16).T, route_weight.T], axis=1)
    metas = jnp.stack([meta] + [around(meta, shift) for shift in range(1, sources)])
    metas = jnp.take(metas, lax.rem(me - jnp.arange(sources) + sources, sources), axis=0)
    blank = jnp.zeros((experts, sources, SLOT_PAD - most - top_k, pair), BF16)
    metas = jnp.broadcast_to(metas[None], (experts, sources, top_k, pair))

    held = saved_hidden.reshape(experts, sources, most, 4, pair)
    held = jnp.transpose(held, (3, 0, 1, 2, 4))
    hidden = []
    for m in range(4):
        piece = lax.dynamic_index_in_dim(held, chips[m], axis=0, keepdims=False)
        piece = jnp.concatenate([piece, blank, metas], axis=2)
        hidden.append(across(piece, 2 * m) if m else piece)

    own_weight = jnp.transpose(down_proj, (1, 0, 2))
    partner_weight = across(own_weight, 1)
    weight = jnp.concatenate(
        [
            jnp.where(core == 0, own_weight, partner_weight),
            jnp.where(core == 0, partner_weight, own_weight),
        ],
        axis=1,
    ).reshape(experts * pair, width)

    carried = grad_out
    half = tokens // 2
    scatters, rows, returned, indices = [], [], [], []
    before = None
    for step in range(sources):
        from_x, from_y = across(carried, 2), across(carried, 4)
        own = carried
        if step < sources - 1:
            carried = around(carried, 1)
        top, bottom = across(from_x[:half], 4), across(from_y[half:], 2)
        source = lax.rem(me - step + sources, sources)
        index = jnp.stack([source, me * experts]).astype(jnp.int32)
        *grads, scatter, row = project(
            index, [own, from_x, from_y, top, bottom], weight, hidden, top_k
        )
        scatters.append(scatter)
        rows.append(row)
        returned.append([grads[0]] + [across(grads[m], 2 * m) for m in range(1, 4)])
        indices.append(jnp.stack([source] + chips).astype(jnp.int32))
        if step == sources - 2:
            before = early_grad(scatters, rows, 512)
    partner = late_grad((1 - core).reshape(1), scatters[-1], rows[-1], before, None, experts, 512)
    partner = across(partner, 1)
    placed, route_grad = None, 0.0
    expert_ids = jnp.arange(experts, dtype=routes.dtype)
    for step in range(sources):
        placed, combine = place(indices[step], returned[step], placed, sources, top_k)
        if step:
            combine = around(combine, -step)
        ids = lax.rem(me + step, sources) * experts + expert_ids
        named = routes.T[:, None, :] == ids[None, :, None]
        route_grad += jnp.sum(jnp.where(named, combine[None], 0.0), axis=1)
    hidden_grad = jnp.transpose(placed[:, :, :most], (1, 0, 2, 3)).reshape(saved_hidden.shape)
    route_grad = ROUTE_SCALE * route_grad.T
    affinity_grad = (route_grad - jnp.sum(route_grad * shares, axis=-1, keepdims=True)) / totals
    down_grad = late_grad(core.reshape(1), scatters[-1], rows[-1], before, partner, experts, 512)
    return (affinity_grad, hidden_grad, down_grad)


def on_device(grad_out, routes, affinity, saved_hidden, down_proj):
    reps, sources = lax.axis_size("rep"), lax.axis_size("exp")
    block, experts, width = down_proj.shape
    tokens, top_k = routes.shape
    most = saved_hidden.shape[3]
    fits = block == 128 and tokens == 128 and width % 512 == 0 and reps == 8
    fits = fits and sources > 1 and most + top_k <= SLOT_PAD and top_k <= 8
    if fits and sources * tokens <= 2 * block * experts:
        return on_device_tokens(grad_out, routes, affinity, saved_hidden, down_proj)
    return on_device_weights(grad_out, routes, affinity, saved_hidden, down_proj)


def solution(mesh):
    return jax.shard_map(
        on_device,
        mesh=mesh,
        in_specs=(
            P(("rep", "exp"), None),
            P(("rep", "exp"), None),
            P(("rep", "exp"), None),
            P("rep", "exp", None, None, None),
            P("rep", "exp", None),
        ),
        out_specs=(
            P(("rep", "exp"), None),
            P("rep", "exp", None, None, None),
            P("rep", "exp", None),
        ),
        check_vma=False,
    )
```

```python
import functools
import jax
import jax.numpy as jnp
from jax import lax
from jax.experimental import pallas as pl
from jax.experimental.pallas import tpu as pltpu
from jax.sharding import PartitionSpec as P

ROUTE_SCALE = 2.5


def pack_routes(grad_rows, route_ids, route_weight, expert_count, most):
    expert_ids = jnp.arange(expert_count, dtype=jnp.int32)
    naming = jnp.sum((route_ids[:, :, None] == expert_ids[None, None, :]).astype(jnp.int32), axis=1)
    before = jnp.cumsum(naming, axis=0) - naming
    slot_ids = jnp.take_along_axis(before, route_ids, axis=1)
    placed = (route_ids * most + slot_ids).reshape(-1)
    token_ids = jnp.repeat(jnp.arange(grad_rows.shape[0], dtype=jnp.int32), route_ids.shape[1])
    source = jnp.zeros((expert_count * most,), jnp.int32).at[placed].set(token_ids)
    filled = jnp.zeros((expert_count * most,), jnp.int32).at[placed].set(1)
    weights = (
        jnp.zeros((expert_count * most,), route_weight.dtype)
        .at[placed]
        .set(route_weight.reshape(-1))
    )
    fetched = jnp.take(grad_rows, source, axis=0)
    packed = jnp.where(filled[:, None] > 0, fetched, jnp.zeros_like(fetched))
    return (packed, weights, placed)


def on_device_weights(grad_out, routes, affinity, saved_hidden, down_proj):
    exp_devices = lax.axis_size("exp")
    local_experts = down_proj.shape[1]
    expert_count = exp_devices * local_experts
    most = saved_hidden.shape[3]
    width = grad_out.shape[1]
    hidden_units = saved_hidden.shape[4]
    row_count = exp_devices * most
    totals = jnp.sum(affinity, axis=-1, keepdims=True)
    shares = affinity / totals
    route_weight = (ROUTE_SCALE * shares).astype(jnp.bfloat16)
    packed, weights, placed = pack_routes(grad_out, routes, route_weight, expert_count, most)
    outgoing = packed.reshape(exp_devices, local_experts, 1, most, width)
    outgoing_weight = weights.reshape(exp_devices, local_experts, 1, most)
    received, received_weight = (
        lax.all_to_all(outgoing, "exp", split_axis=0, concat_axis=2, tiled=True),
        lax.all_to_all(outgoing_weight, "exp", split_axis=0, concat_axis=2, tiled=True),
    )
    received = received.reshape(local_experts, row_count, width)
    row_scale = received_weight.reshape(local_experts, row_count).astype(jnp.float32)
    hidden = saved_hidden.reshape(local_experts, row_count, hidden_units)
    gathered = lax.all_gather(down_proj, "rep", axis=0, tiled=True)
    projected = jnp.einsum("erd,hed->erh", received, gathered, preferred_element_type=jnp.float32)
    hidden_grad = (row_scale[:, :, None] * projected).astype(jnp.bfloat16)
    combine_grad = ROUTE_SCALE * jnp.sum(hidden.astype(jnp.float32) * projected, axis=-1)
    scaled = (row_scale[:, :, None] * received.astype(jnp.float32)).astype(jnp.bfloat16)
    grad_term = jnp.einsum("erh,erd->hed", hidden, scaled, preferred_element_type=jnp.float32)
    down_grad = lax.psum_scatter(
        grad_term.astype(jnp.bfloat16), "rep", scatter_dimension=0, tiled=True
    ).astype(jnp.float32)
    returned = lax.all_to_all(
        combine_grad.reshape(local_experts, exp_devices, most),
        "exp",
        split_axis=1,
        concat_axis=0,
        tiled=True,
    )
    route_grad = jnp.take(returned.reshape(-1), placed).reshape(routes.shape)
    affinity_grad = (route_grad - jnp.sum(route_grad * shares, axis=-1, keepdims=True)) / totals
    return (affinity_grad, hidden_grad.reshape(saved_hidden.shape), down_grad)


SLOT_PAD = 64
F32 = jnp.float32
BF16 = jnp.bfloat16
VMEM_BYTES = 24 * 2**20


def nt_dot(a, b):
    return lax.dot_general(a, b, (((1,), (1,)), ((), ())), preferred_element_type=F32)


def tn_dot(a, b):
    return lax.dot_general(a, b, (((0,), (0,)), ((), ())), preferred_element_type=F32)


def project_kernel(top_k, sizes, idx_ref, *refs):
    parts = len(sizes)
    pieces, (own_weight, partner_weight) = refs[:parts], refs[parts : parts + 2]
    hidden_refs = refs[parts + 2 : parts + 6]
    grad_refs = refs[parts + 6 : parts + 10]
    scatter_ref, rows_out, rows, weight, terms, sems, out_sem = refs[parts + 10 :]
    e = pl.program_id(0)
    slots, pair = grad_refs[0].shape[1:]
    tokens = rows.shape[0] // 4
    spare = slots - 8
    store = pltpu.make_async_copy(rows, rows_out, out_sem)

    @pl.when(e == 0)
    def _():
        copies, at = [], 0
        for i, size in enumerate(sizes):
            copies.append(pltpu.make_async_copy(pieces[i], rows.at[at : at + size], sems.at[i]))
            at += size
        for copy in copies:
            copy.start()
        for copy in copies:
            copy.wait()
        store.start()

    block = pair // 2
    core = idx_ref[2]
    weight[pl.ds(pl.multiple_of(core * block, block), block), :] = own_weight[...]
    weight[pl.ds(pl.multiple_of((1 - core) * block, block), block), :] = partner_weight[...]
    projected = nt_dot(weight[...], rows[...])
    earlier = (
        lax.broadcasted_iota(jnp.int32, (tokens, tokens), 0)
        < lax.broadcasted_iota(jnp.int32, (tokens, tokens), 1)
    ).astype(BF16)
    slot_ids = lax.broadcasted_iota(jnp.int32, (slots, tokens), 0).astype(F32)
    slot_rows = lax.broadcasted_iota(jnp.int32, (slots, pair), 0)
    expert = (idx_ref[1] + e).astype(F32)
    for m in range(4):
        held = hidden_refs[m][0, 0]
        meta = held[spare:].astype(F32)[8 - top_k :]
        named = jnp.zeros((1, tokens), F32)
        scale = jnp.zeros((1, tokens), F32)
        for k in range(top_k):
            hit = meta[k : k + 1, :tokens] == expert
            named = jnp.where(hit, 1.0, named)
            scale = jnp.where(hit, meta[k : k + 1, tokens:], scale)
        before = jnp.dot(
            jnp.broadcast_to(named, (8, tokens)).astype(BF16), earlier, preferred_element_type=F32
        )[0:1]
        slot = jnp.where(named > 0, before, -1.0)
        pick = (slot == slot_ids).astype(BF16)
        own = projected[:, m * tokens : (m + 1) * tokens]
        hidden = tn_dot(held, pick)
        grad = nt_dot(pick, (scale * own).astype(BF16))
        combine = jnp.sum(hidden * own, axis=0, keepdims=True)
        high = combine.astype(BF16).astype(F32)
        partial = jnp.concatenate([high, combine - high], axis=1)
        grad_refs[m][0] = jnp.where(slot_rows == slots - top_k, partial, grad).astype(BF16)
        scatter = (scale * hidden).astype(BF16)
        for half in range(2):
            terms[half, pl.ds(pl.multiple_of(e * block, block), block), m * tokens : (m + 1) * tokens] = (
                scatter[half * block : (half + 1) * block]
            )

    @pl.when(e == pl.num_programs(0) - 1)
    def _():
        height = terms.shape[1]
        experts = height // block
        row = lax.broadcasted_iota(jnp.int32, (height, height), 0)
        col = lax.broadcasted_iota(jnp.int32, (height, height), 1)
        order = (col == lax.rem(row, experts) * block + lax.div(row, experts)).astype(BF16)
        for half in range(2):
            scatter_ref[half] = jnp.dot(order, terms[half], preferred_element_type=F32).astype(BF16)
        store.wait()


def project(index, pieces, own_weight, partner_weight, hidden, top_k):
    experts, sources, slots, pair = hidden[0].shape
    width = own_weight.shape[1]
    sizes = [p.shape[0] for p in pieces]
    count = sum(sizes)
    block = pair // 2
    return pl.pallas_call(
        functools.partial(project_kernel, top_k, sizes),
        grid_spec=pltpu.PrefetchScalarGridSpec(
            num_scalar_prefetch=1,
            grid=(experts,),
            in_specs=[pl.BlockSpec(memory_space=pl.ANY)] * len(sizes)
            + [pl.BlockSpec((block, width), lambda e, idx: (e, 0))] * 2
            + [pl.BlockSpec((1, 1, slots, pair), lambda e, idx: (e, idx[0], 0, 0))] * 4,
            out_specs=[pl.BlockSpec((1, slots, pair), lambda e, idx: (e, 0, 0))] * 4
            + [
                pl.BlockSpec((2, experts * block, count), lambda e, idx: (0, 0, 0)),
                pl.BlockSpec(memory_space=pl.ANY),
            ],
            scratch_shapes=[
                pltpu.VMEM((count, width), BF16),
                pltpu.VMEM((pair, width), BF16),
                pltpu.VMEM((2, experts * block, count), BF16),
                pltpu.SemaphoreType.DMA((len(sizes),)),
                pltpu.SemaphoreType.DMA,
            ],
        ),
        out_shape=[jax.ShapeDtypeStruct((experts, slots, pair), BF16)] * 4
        + [
            jax.ShapeDtypeStruct((2, experts * block, count), BF16),
            jax.ShapeDtypeStruct((count, width), BF16),
        ],
        compiler_params=pltpu.CompilerParams(vmem_limit_bytes=VMEM_BYTES),
        cost_estimate=pl.CostEstimate(
            flops=4 * count * width * experts * pair,
            bytes_accessed=2 * (2 * count * width + 2 * own_weight.size),
            transcendentals=0,
        ),
    )(index, *pieces, own_weight, partner_weight, *hidden)


def early_grad_kernel(terms, *refs):
    out_ref = refs[-1]
    for half in range(2):
        total = jnp.dot(refs[0][half], refs[terms][...], preferred_element_type=F32)
        for i in range(1, terms):
            total += jnp.dot(refs[i][half], refs[terms + i][...], preferred_element_type=F32)
        out_ref[half] = total


def early_grad(scatters, rows, tile):
    _, height, count = scatters[0].shape
    width = rows[0].shape[1]
    terms = len(rows)
    return pl.pallas_call(
        functools.partial(early_grad_kernel, terms),
        grid=(width // tile,),
        in_specs=[pl.BlockSpec((2, height, count), lambda i: (0, 0, 0))] * terms
        + [pl.BlockSpec((count, tile), lambda i: (0, i))] * terms,
        out_specs=pl.BlockSpec((2, height, tile), lambda i: (0, 0, i)),
        out_shape=jax.ShapeDtypeStruct((2, height, width), F32),
        compiler_params=pltpu.CompilerParams(vmem_limit_bytes=VMEM_BYTES),
        cost_estimate=pl.CostEstimate(
            flops=4 * height * count * width * terms,
            bytes_accessed=2 * terms * (rows[0].size + scatters[0].size) + 8 * height * width,
            transcendentals=0,
        ),
    )(*scatters, *rows)


def partner_grad_kernel(idx_ref, scatter_ref, rows_ref, before_ref, out_ref):
    total = before_ref[0] + jnp.dot(scatter_ref[0], rows_ref[...], preferred_element_type=F32)
    out_ref[...] = total.astype(BF16)


def own_grad_kernel(idx_ref, scatter_ref, rows_ref, before_ref, arrived_ref, out_ref, held):
    total = before_ref[0] + jnp.dot(scatter_ref[0], rows_ref[...], preferred_element_type=F32)
    total += arrived_ref[...].astype(F32)
    block, experts, _ = out_ref.shape
    held[...] = total
    group = 8 // experts

    def move(i, carry):
        both = held[pl.ds(pl.multiple_of(i * 8, 8), 8), :]
        for j in range(group):
            out_ref[i * group + j] = both[j * experts : (j + 1) * experts]
        return carry

    lax.fori_loop(0, block // group, move, 0, unroll=4)


def late_grad(index, scatter, rows, before, arrived, experts, tile):
    _, height, count = scatter.shape
    width = rows.shape[1]
    in_specs = [
        pl.BlockSpec((1, height, count), lambda i, idx: (idx[0], 0, 0)),
        pl.BlockSpec((count, tile), lambda i, idx: (0, i)),
        pl.BlockSpec((1, height, tile), lambda i, idx: (idx[0], 0, i)),
    ]
    args = [scatter, rows, before]
    if arrived is None:
        kernel, scratch = partner_grad_kernel, []
        out_spec = pl.BlockSpec((height, tile), lambda i, idx: (0, i))
        out_shape = jax.ShapeDtypeStruct((height, width), BF16)
    else:
        kernel, scratch = own_grad_kernel, [pltpu.VMEM((height, tile), F32)]
        in_specs.append(pl.BlockSpec((height, tile), lambda i, idx: (0, i)))
        args.append(arrived)
        out_spec = pl.BlockSpec((height // experts, experts, tile), lambda i, idx: (0, 0, i))
        out_shape = jax.ShapeDtypeStruct((height // experts, experts, width), F32)
    return pl.pallas_call(
        kernel,
        grid_spec=pltpu.PrefetchScalarGridSpec(
            num_scalar_prefetch=1,
            grid=(width // tile,),
            in_specs=in_specs,
            out_specs=out_spec,
            scratch_shapes=scratch,
        ),
        out_shape=out_shape,
        compiler_params=pltpu.CompilerParams(vmem_limit_bytes=VMEM_BYTES),
        cost_estimate=pl.CostEstimate(
            flops=2 * height * count * width,
            bytes_accessed=2 * (rows.size + scatter.size) + 8 * height * width,
            transcendentals=0,
        ),
    )(index, *args)


def place_kernel(top_k, first, idx_ref, *refs):
    pieces = refs[:4]
    out_ref, sum_ref = refs[-2:]
    experts, slots, pair = pieces[0].shape
    m = pl.program_id(0)

    @pl.when(m == 0)
    def _():
        sum_ref[...] = jnp.zeros_like(sum_ref)

    for i in range(4):

        @pl.when(m == i)
        def _():
            out_ref[0] = pieces[i][...]
            for e in range(experts):
                row = pieces[i][e, slots - 8 :].astype(F32)[8 - top_k : 9 - top_k]
                sum_ref[e : e + 1] += row[:, : pair // 2] + row[:, pair // 2 :]


def place(index, pieces, before, sources, top_k):
    experts, slots, pair = pieces[0].shape
    first = before is None
    shape = (sources, experts, slots, 4 * pair)
    return pl.pallas_call(
        functools.partial(place_kernel, top_k, first),
        grid_spec=pltpu.PrefetchScalarGridSpec(
            num_scalar_prefetch=1,
            grid=(4,),
            in_specs=[pl.BlockSpec((experts, slots, pair), lambda m, idx: (0, 0, 0))] * 4
            + ([] if first else [pl.BlockSpec(memory_space=pl.ANY)]),
            out_specs=[
                pl.BlockSpec((1, experts, slots, pair), lambda m, idx: (idx[0], 0, 0, idx[1 + m])),
                pl.BlockSpec((experts, pair // 2), lambda m, idx: (0, 0)),
            ],
        ),
        out_shape=[
            jax.ShapeDtypeStruct(shape, BF16),
            jax.ShapeDtypeStruct((experts, pair // 2), F32),
        ],
        input_output_aliases={} if first else {5: 0},
        compiler_params=pltpu.CompilerParams(vmem_limit_bytes=VMEM_BYTES),
        cost_estimate=pl.CostEstimate(
            flops=0, bytes_accessed=16 * experts * slots * pair, transcendentals=0
        ),
    )(index, *pieces, *([] if first else [before]))


def on_device_tokens(grad_out, routes, affinity, saved_hidden, down_proj):
    reps, sources = lax.axis_size("rep"), lax.axis_size("exp")
    block, experts, width = down_proj.shape
    tokens, top_k = routes.shape
    most, hidden_units = saved_hidden.shape[3:]
    pair = 2 * block
    me = lax.axis_index("exp")
    rep = lax.axis_index("rep")
    chip, core = lax.div(rep, 2), lax.rem(rep, 2)
    chips = [jnp.bitwise_xor(chip, m) for m in range(4)]

    def across(array, bits):
        return lax.ppermute(array, "rep", [(i, i ^ bits) for i in range(reps)])

    def around(array, shift):
        return lax.ppermute(array, "exp", [(i, (i + shift) % sources) for i in range(sources)])

    def after(array, other):
        return lax.optimization_barrier((array, other))[0]

    totals = jnp.sum(affinity, axis=-1, keepdims=True)
    shares = affinity / totals
    route_weight = (ROUTE_SCALE * shares).astype(BF16)
    meta = jnp.concatenate([routes.astype(BF16).T, route_weight.T], axis=1)
    metas = jnp.stack([meta] + [around(meta, shift) for shift in range(1, sources)])
    carried = after(grad_out, metas)
    metas = jnp.take(metas, lax.rem(me - jnp.arange(sources) + sources, sources), axis=0)
    blank = jnp.zeros((experts, sources, SLOT_PAD - most - top_k, pair), BF16)
    metas = jnp.broadcast_to(metas[None], (experts, sources, top_k, pair))

    held = saved_hidden.reshape(experts, sources, most, 4, pair)
    held = lax.optimization_barrier(jnp.transpose(held, (3, 0, 1, 2, 4)))
    hidden = []
    for m in range(4):
        piece = lax.dynamic_index_in_dim(held, chips[m], axis=0, keepdims=False)
        piece = jnp.concatenate([piece, blank, metas], axis=2)
        hidden.append(across(piece, 2 * m) if m else piece)

    own_weight = jnp.transpose(down_proj, (1, 0, 2)).reshape(experts * block, width)
    own_weight = lax.optimization_barrier(own_weight)
    partner_weight = across(own_weight, 1)

    half = tokens // 2
    shards = [grad_out]
    for step in range(1, sources):
        carried = around(carried, 1)
        shards.append(carried)
    scatters, rows, returned, indices, placed, combines = [], [], [], [], [None], []
    for step in range(sources):
        own = shards[step]
        sent = own if step < 2 else after(own, scatters[step - 2])
        from_x, from_y = across(sent, 2), across(sent, 4)
        top, bottom = across(from_x[:half], 4), across(from_y[half:], 2)
        source = lax.rem(me - step + sources, sources)
        index = jnp.stack([source, me * experts, core]).astype(jnp.int32)
        if step >= 2:
            own = after(own, combines[step - 2])
        if step == sources - 1:
            before = early_grad(scatters, rows, 512)
            own = after(own, before)
        *grads, scatter, row = project(
            index, [own, from_x, from_y, top, bottom], own_weight, partner_weight, hidden, top_k
        )
        scatters.append(scatter)
        rows.append(row)
        returned = [grads[0]] + [across(grads[m], 2 * m) for m in range(1, 4)]
        indices = jnp.stack([source] + chips).astype(jnp.int32)
        spot, combine = place(indices, returned, placed[-1], sources, top_k)
        placed.append(spot)
        combines.append(around(combine, -step) if step else combine)
    partner = late_grad((1 - core).reshape(1), scatters[-1], rows[-1], before, None, experts, 896)
    partner = across(partner, 1)
    route_grad = 0.0
    expert_ids = jnp.arange(experts, dtype=routes.dtype)
    for step in range(sources):
        ids = lax.rem(me + step, sources) * experts + expert_ids
        named = routes.T[:, None, :] == ids[None, :, None]
        route_grad += jnp.sum(jnp.where(named, combines[step][None], 0.0), axis=1)
    hidden_grad = jnp.transpose(placed[-1][:, :, :most], (1, 0, 2, 3)).reshape(saved_hidden.shape)
    route_grad = ROUTE_SCALE * route_grad.T
    affinity_grad = (route_grad - jnp.sum(route_grad * shares, axis=-1, keepdims=True)) / totals
    down_grad = late_grad(core.reshape(1), scatters[-1], rows[-1], before, partner, experts, 896)
    return (affinity_grad, hidden_grad, down_grad)


def on_device(grad_out, routes, affinity, saved_hidden, down_proj):
    reps, sources = lax.axis_size("rep"), lax.axis_size("exp")
    block, experts, width = down_proj.shape
    tokens, top_k = routes.shape
    most = saved_hidden.shape[3]
    fits = block == 128 and tokens == 128 and width % 3584 == 0 and reps == 8 and 8 % experts == 0
    fits = fits and sources > 1 and most + top_k <= SLOT_PAD and top_k <= 8
    if fits and sources * tokens <= 2 * block * experts:
        return on_device_tokens(grad_out, routes, affinity, saved_hidden, down_proj)
    return on_device_weights(grad_out, routes, affinity, saved_hidden, down_proj)


def solution(mesh):
    return jax.shard_map(
        on_device,
        mesh=mesh,
        in_specs=(
            P(("rep", "exp"), None),
            P(("rep", "exp"), None),
            P(("rep", "exp"), None),
            P("rep", "exp", None, None, None),
            P("rep", "exp", None),
        ),
        out_specs=(
            P(("rep", "exp"), None),
            P("rep", "exp", None, None, None),
            P("rep", "exp", None),
        ),
        check_vma=False,
    )
```

```python
import functools
import jax
import jax.numpy as jnp
from jax import lax
from jax.experimental import pallas as pl
from jax.experimental.pallas import tpu as pltpu
from jax.sharding import PartitionSpec as P

ROUTE_SCALE = 2.5


def pack_routes(grad_rows, route_ids, route_weight, expert_count, most):
    expert_ids = jnp.arange(expert_count, dtype=jnp.int32)
    naming = jnp.sum((route_ids[:, :, None] == expert_ids[None, None, :]).astype(jnp.int32), axis=1)
    before = jnp.cumsum(naming, axis=0) - naming
    slot_ids = jnp.take_along_axis(before, route_ids, axis=1)
    placed = (route_ids * most + slot_ids).reshape(-1)
    token_ids = jnp.repeat(jnp.arange(grad_rows.shape[0], dtype=jnp.int32), route_ids.shape[1])
    source = jnp.zeros((expert_count * most,), jnp.int32).at[placed].set(token_ids)
    filled = jnp.zeros((expert_count * most,), jnp.int32).at[placed].set(1)
    weights = (
        jnp.zeros((expert_count * most,), route_weight.dtype)
        .at[placed]
        .set(route_weight.reshape(-1))
    )
    fetched = jnp.take(grad_rows, source, axis=0)
    packed = jnp.where(filled[:, None] > 0, fetched, jnp.zeros_like(fetched))
    return (packed, weights, placed)


def on_device_weights(grad_out, routes, affinity, saved_hidden, down_proj):
    exp_devices = lax.axis_size("exp")
    local_experts = down_proj.shape[1]
    expert_count = exp_devices * local_experts
    most = saved_hidden.shape[3]
    width = grad_out.shape[1]
    hidden_units = saved_hidden.shape[4]
    row_count = exp_devices * most
    totals = jnp.sum(affinity, axis=-1, keepdims=True)
    shares = affinity / totals
    route_weight = (ROUTE_SCALE * shares).astype(jnp.bfloat16)
    packed, weights, placed = pack_routes(grad_out, routes, route_weight, expert_count, most)
    outgoing = packed.reshape(exp_devices, local_experts, 1, most, width)
    outgoing_weight = weights.reshape(exp_devices, local_experts, 1, most)
    received, received_weight = (
        lax.all_to_all(outgoing, "exp", split_axis=0, concat_axis=2, tiled=True),
        lax.all_to_all(outgoing_weight, "exp", split_axis=0, concat_axis=2, tiled=True),
    )
    received = received.reshape(local_experts, row_count, width)
    row_scale = received_weight.reshape(local_experts, row_count).astype(jnp.float32)
    hidden = saved_hidden.reshape(local_experts, row_count, hidden_units)
    gathered = lax.all_gather(down_proj, "rep", axis=0, tiled=True)
    projected = jnp.einsum("erd,hed->erh", received, gathered, preferred_element_type=jnp.float32)
    hidden_grad = (row_scale[:, :, None] * projected).astype(jnp.bfloat16)
    combine_grad = ROUTE_SCALE * jnp.sum(hidden.astype(jnp.float32) * projected, axis=-1)
    scaled = (row_scale[:, :, None] * received.astype(jnp.float32)).astype(jnp.bfloat16)
    grad_term = jnp.einsum("erh,erd->hed", hidden, scaled, preferred_element_type=jnp.float32)
    down_grad = lax.psum_scatter(
        grad_term.astype(jnp.bfloat16), "rep", scatter_dimension=0, tiled=True
    ).astype(jnp.float32)
    returned = lax.all_to_all(
        combine_grad.reshape(local_experts, exp_devices, most),
        "exp",
        split_axis=1,
        concat_axis=0,
        tiled=True,
    )
    route_grad = jnp.take(returned.reshape(-1), placed).reshape(routes.shape)
    affinity_grad = (route_grad - jnp.sum(route_grad * shares, axis=-1, keepdims=True)) / totals
    return (affinity_grad, hidden_grad.reshape(saved_hidden.shape), down_grad)


SLOT_PAD = 64
F32 = jnp.float32
BF16 = jnp.bfloat16
VMEM_BYTES = 24 * 2**20


def nt_dot(a, b):
    return lax.dot_general(a, b, (((1,), (1,)), ((), ())), preferred_element_type=F32)


def tn_dot(a, b):
    return lax.dot_general(a, b, (((0,), (0,)), ((), ())), preferred_element_type=F32)


def project_kernel(top_k, idx_ref, *refs):
    parts = 1
    pieces, (own_weight, partner_weight) = refs[:parts], refs[parts : parts + 2]
    hidden_refs = refs[parts + 2 : parts + 6]
    grad_refs = refs[parts + 6 : parts + 10]
    scatter_ref, rows_out, rows, weight, terms, sems, out_sem = refs[parts + 10 :]
    e = pl.program_id(0)
    slots, pair = grad_refs[0].shape[1:]
    tokens = rows.shape[0] // 4
    spare = slots - 8
    store = pltpu.make_async_copy(rows, rows_out, out_sem)

    @pl.when(e == 0)
    def _():
        copies = []
        for m in range(4):
            at = pl.ds(pl.multiple_of(idx_ref[3 + m] * tokens, tokens), tokens)
            to = rows.at[m * tokens : (m + 1) * tokens]
            copies.append(pltpu.make_async_copy(pieces[0].at[at], to, sems.at[m]))
        for copy in copies:
            copy.start()
        for copy in copies:
            copy.wait()
        store.start()

    block = pair // 2
    core = idx_ref[2]
    weight[pl.ds(pl.multiple_of(core * block, block), block), :] = own_weight[...]
    weight[pl.ds(pl.multiple_of((1 - core) * block, block), block), :] = partner_weight[...]
    projected = nt_dot(weight[...], rows[...])
    earlier = (
        lax.broadcasted_iota(jnp.int32, (tokens, tokens), 0)
        < lax.broadcasted_iota(jnp.int32, (tokens, tokens), 1)
    ).astype(BF16)
    slot_ids = lax.broadcasted_iota(jnp.int32, (slots, tokens), 0).astype(F32)
    slot_rows = lax.broadcasted_iota(jnp.int32, (slots, pair), 0)
    expert = (idx_ref[1] + e).astype(F32)
    for m in range(4):
        held = hidden_refs[m][0, 0]
        meta = held[spare:].astype(F32)[8 - top_k :]
        named = jnp.zeros((1, tokens), F32)
        scale = jnp.zeros((1, tokens), F32)
        for k in range(top_k):
            hit = meta[k : k + 1, :tokens] == expert
            named = jnp.where(hit, 1.0, named)
            scale = jnp.where(hit, meta[k : k + 1, tokens:], scale)
        before = jnp.dot(
            jnp.broadcast_to(named, (8, tokens)).astype(BF16), earlier, preferred_element_type=F32
        )[0:1]
        slot = jnp.where(named > 0, before, -1.0)
        pick = (slot == slot_ids).astype(BF16)
        own = projected[:, m * tokens : (m + 1) * tokens]
        hidden = tn_dot(held, pick)
        grad = nt_dot(pick, (scale * own).astype(BF16))
        combine = jnp.sum(hidden * own, axis=0, keepdims=True)
        high = combine.astype(BF16).astype(F32)
        partial = jnp.concatenate([high, combine - high], axis=1)
        grad_refs[m][0] = jnp.where(slot_rows == slots - top_k, partial, grad).astype(BF16)
        scatter = (scale * hidden).astype(BF16)
        for half in range(2):
            terms[half, pl.ds(pl.multiple_of(e * block, block), block), m * tokens : (m + 1) * tokens] = (
                scatter[half * block : (half + 1) * block]
            )

    @pl.when(e == pl.num_programs(0) - 1)
    def _():
        height = terms.shape[1]
        experts = height // block
        row = lax.broadcasted_iota(jnp.int32, (height, height), 0)
        col = lax.broadcasted_iota(jnp.int32, (height, height), 1)
        order = (col == lax.rem(row, experts) * block + lax.div(row, experts)).astype(BF16)
        for half in range(2):
            scatter_ref[half] = jnp.dot(order, terms[half], preferred_element_type=F32).astype(BF16)
        store.wait()


def project(index, gathered, own_weight, partner_weight, hidden, top_k):
    experts, sources, slots, pair = hidden[0].shape
    width = own_weight.shape[1]
    count = gathered.shape[0]
    block = pair // 2
    return pl.pallas_call(
        functools.partial(project_kernel, top_k),
        grid_spec=pltpu.PrefetchScalarGridSpec(
            num_scalar_prefetch=1,
            grid=(experts,),
            in_specs=[pl.BlockSpec(memory_space=pl.ANY)]
            + [pl.BlockSpec((block, width), lambda e, idx: (e, 0))] * 2
            + [pl.BlockSpec((1, 1, slots, pair), lambda e, idx: (e, idx[0], 0, 0))] * 4,
            out_specs=[pl.BlockSpec((1, slots, pair), lambda e, idx: (e, 0, 0))] * 4
            + [
                pl.BlockSpec((2, experts * block, count), lambda e, idx: (0, 0, 0)),
                pl.BlockSpec(memory_space=pl.ANY),
            ],
            scratch_shapes=[
                pltpu.VMEM((count, width), BF16),
                pltpu.VMEM((pair, width), BF16),
                pltpu.VMEM((2, experts * block, count), BF16),
                pltpu.SemaphoreType.DMA((4,)),
                pltpu.SemaphoreType.DMA,
            ],
        ),
        out_shape=[jax.ShapeDtypeStruct((experts, slots, pair), BF16)] * 4
        + [
            jax.ShapeDtypeStruct((2, experts * block, count), BF16),
            jax.ShapeDtypeStruct((count, width), BF16),
        ],
        compiler_params=pltpu.CompilerParams(vmem_limit_bytes=VMEM_BYTES),
        cost_estimate=pl.CostEstimate(
            flops=4 * count * width * experts * pair,
            bytes_accessed=2 * (2 * count * width + 2 * own_weight.size),
            transcendentals=0,
        ),
    )(index, gathered, own_weight, partner_weight, *hidden)


def early_grad_kernel(terms, *refs):
    out_ref = refs[-1]
    for half in range(2):
        total = jnp.dot(refs[0][half], refs[terms][...], preferred_element_type=F32)
        for i in range(1, terms):
            total += jnp.dot(refs[i][half], refs[terms + i][...], preferred_element_type=F32)
        out_ref[half] = total


def early_grad(scatters, rows, tile):
    _, height, count = scatters[0].shape
    width = rows[0].shape[1]
    terms = len(rows)
    return pl.pallas_call(
        functools.partial(early_grad_kernel, terms),
        grid=(width // tile,),
        in_specs=[pl.BlockSpec((2, height, count), lambda i: (0, 0, 0))] * terms
        + [pl.BlockSpec((count, tile), lambda i: (0, i))] * terms,
        out_specs=pl.BlockSpec((2, height, tile), lambda i: (0, 0, i)),
        out_shape=jax.ShapeDtypeStruct((2, height, width), F32),
        compiler_params=pltpu.CompilerParams(vmem_limit_bytes=VMEM_BYTES),
        cost_estimate=pl.CostEstimate(
            flops=4 * height * count * width * terms,
            bytes_accessed=2 * terms * (rows[0].size + scatters[0].size) + 8 * height * width,
            transcendentals=0,
        ),
    )(*scatters, *rows)


def partner_grad_kernel(idx_ref, scatter_ref, rows_ref, before_ref, out_ref):
    total = before_ref[0] + jnp.dot(scatter_ref[0], rows_ref[...], preferred_element_type=F32)
    out_ref[...] = total.astype(BF16)


def own_grad_kernel(idx_ref, scatter_ref, rows_ref, before_ref, arrived_ref, out_ref, held):
    total = before_ref[0] + jnp.dot(scatter_ref[0], rows_ref[...], preferred_element_type=F32)
    total += arrived_ref[...].astype(F32)
    block, experts, _ = out_ref.shape
    held[...] = total
    group = 8 // experts

    def move(i, carry):
        both = held[pl.ds(pl.multiple_of(i * 8, 8), 8), :]
        for j in range(group):
            out_ref[i * group + j] = both[j * experts : (j + 1) * experts]
        return carry

    lax.fori_loop(0, block // group, move, 0, unroll=4)


def late_grad(index, scatter, rows, before, arrived, experts, tile):
    _, height, count = scatter.shape
    width = rows.shape[1]
    in_specs = [
        pl.BlockSpec((1, height, count), lambda i, idx: (idx[0], 0, 0)),
        pl.BlockSpec((count, tile), lambda i, idx: (0, i)),
        pl.BlockSpec((1, height, tile), lambda i, idx: (idx[0], 0, i)),
    ]
    args = [scatter, rows, before]
    if arrived is None:
        kernel, scratch = partner_grad_kernel, []
        out_spec = pl.BlockSpec((height, tile), lambda i, idx: (0, i))
        out_shape = jax.ShapeDtypeStruct((height, width), BF16)
    else:
        kernel, scratch = own_grad_kernel, [pltpu.VMEM((height, tile), F32)]
        in_specs.append(pl.BlockSpec((height, tile), lambda i, idx: (0, i)))
        args.append(arrived)
        out_spec = pl.BlockSpec((height // experts, experts, tile), lambda i, idx: (0, 0, i))
        out_shape = jax.ShapeDtypeStruct((height // experts, experts, width), F32)
    return pl.pallas_call(
        kernel,
        grid_spec=pltpu.PrefetchScalarGridSpec(
            num_scalar_prefetch=1,
            grid=(width // tile,),
            in_specs=in_specs,
            out_specs=out_spec,
            scratch_shapes=scratch,
        ),
        out_shape=out_shape,
        compiler_params=pltpu.CompilerParams(vmem_limit_bytes=VMEM_BYTES),
        cost_estimate=pl.CostEstimate(
            flops=2 * height * count * width,
            bytes_accessed=2 * (rows.size + scatter.size) + 8 * height * width,
            transcendentals=0,
        ),
    )(index, *args)


def place_kernel(top_k, first, idx_ref, *refs):
    pieces = refs[:4]
    out_ref, sum_ref = refs[-2:]
    experts, slots, pair = pieces[0].shape
    m = pl.program_id(0)

    @pl.when(m == 0)
    def _():
        sum_ref[...] = jnp.zeros_like(sum_ref)

    for i in range(4):

        @pl.when(m == i)
        def _():
            out_ref[0] = pieces[i][...]
            for e in range(experts):
                row = pieces[i][e, slots - 8 :].astype(F32)[8 - top_k : 9 - top_k]
                sum_ref[e : e + 1] += row[:, : pair // 2] + row[:, pair // 2 :]


def place(index, pieces, before, sources, top_k):
    experts, slots, pair = pieces[0].shape
    first = before is None
    shape = (sources, experts, slots, 4 * pair)
    return pl.pallas_call(
        functools.partial(place_kernel, top_k, first),
        grid_spec=pltpu.PrefetchScalarGridSpec(
            num_scalar_prefetch=1,
            grid=(4,),
            in_specs=[pl.BlockSpec((experts, slots, pair), lambda m, idx: (0, 0, 0))] * 4
            + ([] if first else [pl.BlockSpec(memory_space=pl.ANY)]),
            out_specs=[
                pl.BlockSpec((1, experts, slots, pair), lambda m, idx: (idx[0], 0, 0, idx[1 + m])),
                pl.BlockSpec((experts, pair // 2), lambda m, idx: (0, 0)),
            ],
        ),
        out_shape=[
            jax.ShapeDtypeStruct(shape, BF16),
            jax.ShapeDtypeStruct((experts, pair // 2), F32),
        ],
        input_output_aliases={} if first else {5: 0},
        compiler_params=pltpu.CompilerParams(vmem_limit_bytes=VMEM_BYTES),
        cost_estimate=pl.CostEstimate(
            flops=0, bytes_accessed=16 * experts * slots * pair, transcendentals=0
        ),
    )(index, *pieces, *([] if first else [before]))


def on_device_tokens(grad_out, routes, affinity, saved_hidden, down_proj):
    reps, sources = lax.axis_size("rep"), lax.axis_size("exp")
    block, experts, width = down_proj.shape
    tokens, top_k = routes.shape
    most, hidden_units = saved_hidden.shape[3:]
    pair = 2 * block
    me = lax.axis_index("exp")
    rep = lax.axis_index("rep")
    chip, core = lax.div(rep, 2), lax.rem(rep, 2)
    chips = [jnp.bitwise_xor(chip, m) for m in range(4)]

    def across(array, bits):
        return lax.ppermute(array, "rep", [(i, i ^ bits) for i in range(reps)])

    def around(array, shift):
        return lax.ppermute(array, "exp", [(i, (i + shift) % sources) for i in range(sources)])

    def after(array, other):
        return lax.optimization_barrier((array, other))[0]

    totals = jnp.sum(affinity, axis=-1, keepdims=True)
    shares = affinity / totals
    route_weight = (ROUTE_SCALE * shares).astype(BF16)
    meta = jnp.concatenate([routes.astype(BF16).T, route_weight.T], axis=1)
    metas = jnp.stack([meta] + [around(meta, shift) for shift in range(1, sources)])
    carried = after(grad_out, metas)
    metas = jnp.take(metas, lax.rem(me - jnp.arange(sources) + sources, sources), axis=0)
    blank = jnp.zeros((experts, sources, SLOT_PAD - most - top_k, pair), BF16)
    metas = jnp.broadcast_to(metas[None], (experts, sources, top_k, pair))

    held = saved_hidden.reshape(experts, sources, most, 4, pair)
    held = lax.optimization_barrier(jnp.transpose(held, (3, 0, 1, 2, 4)))
    hidden = []
    for m in range(4):
        piece = lax.dynamic_index_in_dim(held, chips[m], axis=0, keepdims=False)
        piece = jnp.concatenate([piece, blank, metas], axis=2)
        hidden.append(across(piece, 2 * m) if m else piece)

    own_weight = jnp.transpose(down_proj, (1, 0, 2)).reshape(experts * block, width)
    own_weight = lax.optimization_barrier(own_weight)
    partner_weight = across(own_weight, 1)

    shards = [grad_out]
    for step in range(1, sources):
        if step == 2:
            carried = after(carried, hidden)
        carried = around(carried, 1)
        shards.append(carried)
    same_core = [[i for i in range(reps) if i % 2 == c] for c in range(2)]
    scatters, rows, returned, indices, placed, combines = [], [], [], [], [None], []
    for step in range(sources):
        gathered = lax.all_gather(shards[step], "rep", axis=0, tiled=True, axis_index_groups=same_core)
        source = lax.rem(me - step + sources, sources)
        index = jnp.stack([source, me * experts, core] + chips).astype(jnp.int32)
        if step >= 2:
            gathered = after(gathered, combines[step - 2])
        if step == sources - 1:
            before = early_grad(scatters, rows, 512)
            gathered = after(gathered, before)
        *grads, scatter, row = project(index, gathered, own_weight, partner_weight, hidden, top_k)
        scatters.append(scatter)
        rows.append(row)
        returned = [grads[0]] + [across(grads[m], 2 * m) for m in range(1, 4)]
        indices = jnp.stack([source] + chips).astype(jnp.int32)
        spot, combine = place(indices, returned, placed[-1], sources, top_k)
        placed.append(spot)
        combines.append(around(combine, -step) if step else combine)
    partner = late_grad((1 - core).reshape(1), scatters[-1], rows[-1], before, None, experts, 896)
    partner = across(partner, 1)
    route_grad = 0.0
    expert_ids = jnp.arange(experts, dtype=routes.dtype)
    for step in range(sources):
        ids = lax.rem(me + step, sources) * experts + expert_ids
        named = routes.T[:, None, :] == ids[None, :, None]
        route_grad += jnp.sum(jnp.where(named, combines[step][None], 0.0), axis=1)
    hidden_grad = jnp.transpose(placed[-1][:, :, :most], (1, 0, 2, 3)).reshape(saved_hidden.shape)
    route_grad = ROUTE_SCALE * route_grad.T
    affinity_grad = (route_grad - jnp.sum(route_grad * shares, axis=-1, keepdims=True)) / totals
    down_grad = late_grad(core.reshape(1), scatters[-1], rows[-1], before, partner, experts, 896)
    return (affinity_grad, hidden_grad, down_grad)


def on_device(grad_out, routes, affinity, saved_hidden, down_proj):
    reps, sources = lax.axis_size("rep"), lax.axis_size("exp")
    block, experts, width = down_proj.shape
    tokens, top_k = routes.shape
    most = saved_hidden.shape[3]
    fits = block == 128 and tokens == 128 and width % 3584 == 0 and reps == 8 and 8 % experts == 0
    fits = fits and sources > 1 and most + top_k <= SLOT_PAD and top_k <= 8
    if fits and sources * tokens <= 2 * block * experts:
        return on_device_tokens(grad_out, routes, affinity, saved_hidden, down_proj)
    return on_device_weights(grad_out, routes, affinity, saved_hidden, down_proj)


def solution(mesh):
    return jax.shard_map(
        on_device,
        mesh=mesh,
        in_specs=(
            P(("rep", "exp"), None),
            P(("rep", "exp"), None),
            P(("rep", "exp"), None),
            P("rep", "exp", None, None, None),
            P("rep", "exp", None),
        ),
        out_specs=(
            P(("rep", "exp"), None),
            P("rep", "exp", None, None, None),
            P("rep", "exp", None),
        ),
        check_vma=False,
    )
```

```python
import functools
import jax
import jax.numpy as jnp
from jax import lax
from jax.experimental import pallas as pl
from jax.experimental.pallas import tpu as pltpu
from jax.sharding import PartitionSpec as P

ROUTE_SCALE = 2.5


def pack_routes(grad_rows, route_ids, route_weight, expert_count, most):
    expert_ids = jnp.arange(expert_count, dtype=jnp.int32)
    naming = jnp.sum((route_ids[:, :, None] == expert_ids[None, None, :]).astype(jnp.int32), axis=1)
    before = jnp.cumsum(naming, axis=0) - naming
    slot_ids = jnp.take_along_axis(before, route_ids, axis=1)
    placed = (route_ids * most + slot_ids).reshape(-1)
    token_ids = jnp.repeat(jnp.arange(grad_rows.shape[0], dtype=jnp.int32), route_ids.shape[1])
    source = jnp.zeros((expert_count * most,), jnp.int32).at[placed].set(token_ids)
    filled = jnp.zeros((expert_count * most,), jnp.int32).at[placed].set(1)
    weights = (
        jnp.zeros((expert_count * most,), route_weight.dtype)
        .at[placed]
        .set(route_weight.reshape(-1))
    )
    fetched = jnp.take(grad_rows, source, axis=0)
    packed = jnp.where(filled[:, None] > 0, fetched, jnp.zeros_like(fetched))
    return (packed, weights, placed)


def on_device_weights(grad_out, routes, affinity, saved_hidden, down_proj):
    exp_devices = lax.axis_size("exp")
    local_experts = down_proj.shape[1]
    expert_count = exp_devices * local_experts
    most = saved_hidden.shape[3]
    width = grad_out.shape[1]
    hidden_units = saved_hidden.shape[4]
    row_count = exp_devices * most
    totals = jnp.sum(affinity, axis=-1, keepdims=True)
    shares = affinity / totals
    route_weight = (ROUTE_SCALE * shares).astype(jnp.bfloat16)
    packed, weights, placed = pack_routes(grad_out, routes, route_weight, expert_count, most)
    outgoing = packed.reshape(exp_devices, local_experts, 1, most, width)
    outgoing_weight = weights.reshape(exp_devices, local_experts, 1, most)
    received, received_weight = (
        lax.all_to_all(outgoing, "exp", split_axis=0, concat_axis=2, tiled=True),
        lax.all_to_all(outgoing_weight, "exp", split_axis=0, concat_axis=2, tiled=True),
    )
    received = received.reshape(local_experts, row_count, width)
    row_scale = received_weight.reshape(local_experts, row_count).astype(jnp.float32)
    hidden = saved_hidden.reshape(local_experts, row_count, hidden_units)
    gathered = lax.all_gather(down_proj, "rep", axis=0, tiled=True)
    projected = jnp.einsum("erd,hed->erh", received, gathered, preferred_element_type=jnp.float32)
    hidden_grad = (row_scale[:, :, None] * projected).astype(jnp.bfloat16)
    combine_grad = ROUTE_SCALE * jnp.sum(hidden.astype(jnp.float32) * projected, axis=-1)
    scaled = (row_scale[:, :, None] * received.astype(jnp.float32)).astype(jnp.bfloat16)
    grad_term = jnp.einsum("erh,erd->hed", hidden, scaled, preferred_element_type=jnp.float32)
    down_grad = lax.psum_scatter(
        grad_term.astype(jnp.bfloat16), "rep", scatter_dimension=0, tiled=True
    ).astype(jnp.float32)
    returned = lax.all_to_all(
        combine_grad.reshape(local_experts, exp_devices, most),
        "exp",
        split_axis=1,
        concat_axis=0,
        tiled=True,
    )
    route_grad = jnp.take(returned.reshape(-1), placed).reshape(routes.shape)
    affinity_grad = (route_grad - jnp.sum(route_grad * shares, axis=-1, keepdims=True)) / totals
    return (affinity_grad, hidden_grad.reshape(saved_hidden.shape), down_grad)


SLOT_PAD = 64
F32 = jnp.float32
BF16 = jnp.bfloat16
VMEM_BYTES = 24 * 2**20


def nt_dot(a, b):
    return lax.dot_general(a, b, (((1,), (1,)), ((), ())), preferred_element_type=F32)


def tn_dot(a, b):
    return lax.dot_general(a, b, (((0,), (0,)), ((), ())), preferred_element_type=F32)


def project_kernel(top_k, sizes, idx_ref, *refs):
    parts = len(sizes)
    pieces, (own_weight, partner_weight) = refs[:parts], refs[parts : parts + 2]
    hidden_refs = refs[parts + 2 : parts + 6]
    grad_refs = refs[parts + 6 : parts + 10]
    scatter_ref, rows_out, rows, weight, terms, sems, out_sem = refs[parts + 10 :]
    e = pl.program_id(0)
    slots, pair = grad_refs[0].shape[1:]
    tokens = rows.shape[0] // 4
    spare = slots - 8
    store = pltpu.make_async_copy(rows, rows_out, out_sem)

    @pl.when(e == 0)
    def _():
        copies, at = [], 0
        for i, size in enumerate(sizes):
            copies.append(pltpu.make_async_copy(pieces[i], rows.at[at : at + size], sems.at[i]))
            at += size
        for copy in copies:
            copy.start()
        for copy in copies:
            copy.wait()
        store.start()

    block = pair // 2
    core = idx_ref[2]
    weight[pl.ds(pl.multiple_of(core * block, block), block), :] = own_weight[...]
    weight[pl.ds(pl.multiple_of((1 - core) * block, block), block), :] = partner_weight[...]
    projected = nt_dot(weight[...], rows[...])
    earlier = (
        lax.broadcasted_iota(jnp.int32, (tokens, tokens), 0)
        < lax.broadcasted_iota(jnp.int32, (tokens, tokens), 1)
    ).astype(BF16)
    slot_ids = lax.broadcasted_iota(jnp.int32, (slots, tokens), 0).astype(F32)
    slot_rows = lax.broadcasted_iota(jnp.int32, (slots, pair), 0)
    expert = (idx_ref[1] + e).astype(F32)
    for m in range(4):
        held = hidden_refs[m][0, 0]
        meta = held[spare:].astype(F32)[8 - top_k :]
        named = jnp.zeros((1, tokens), F32)
        scale = jnp.zeros((1, tokens), F32)
        for k in range(top_k):
            hit = meta[k : k + 1, :tokens] == expert
            named = jnp.where(hit, 1.0, named)
            scale = jnp.where(hit, meta[k : k + 1, tokens:], scale)
        before = jnp.dot(
            jnp.broadcast_to(named, (8, tokens)).astype(BF16), earlier, preferred_element_type=F32
        )[0:1]
        slot = jnp.where(named > 0, before, -1.0)
        pick = (slot == slot_ids).astype(BF16)
        own = projected[:, m * tokens : (m + 1) * tokens]
        hidden = tn_dot(held, pick)
        grad = nt_dot(pick, (scale * own).astype(BF16))
        combine = jnp.sum(hidden * own, axis=0, keepdims=True)
        high = combine.astype(BF16).astype(F32)
        partial = jnp.concatenate([high, combine - high], axis=1)
        grad_refs[m][0] = jnp.where(slot_rows == slots - top_k, partial, grad).astype(BF16)
        scatter = (scale * hidden).astype(BF16)
        for half in range(2):
            terms[half, pl.ds(pl.multiple_of(e * block, block), block), m * tokens : (m + 1) * tokens] = (
                scatter[half * block : (half + 1) * block]
            )

    @pl.when(e == pl.num_programs(0) - 1)
    def _():
        height = terms.shape[1]
        experts = height // block
        row = lax.broadcasted_iota(jnp.int32, (height, height), 0)
        col = lax.broadcasted_iota(jnp.int32, (height, height), 1)
        order = (col == lax.rem(row, experts) * block + lax.div(row, experts)).astype(BF16)
        for half in range(2):
            scatter_ref[half] = jnp.dot(order, terms[half], preferred_element_type=F32).astype(BF16)
        store.wait()


def project(index, pieces, own_weight, partner_weight, hidden, top_k):
    experts, sources, slots, pair = hidden[0].shape
    width = own_weight.shape[1]
    sizes = [p.shape[0] for p in pieces]
    count = sum(sizes)
    block = pair // 2
    return pl.pallas_call(
        functools.partial(project_kernel, top_k, sizes),
        grid_spec=pltpu.PrefetchScalarGridSpec(
            num_scalar_prefetch=1,
            grid=(experts,),
            in_specs=[pl.BlockSpec(memory_space=pl.ANY)] * len(sizes)
            + [pl.BlockSpec((block, width), lambda e, idx: (e, 0))] * 2
            + [pl.BlockSpec((1, 1, slots, pair), lambda e, idx: (e, idx[0], 0, 0))] * 4,
            out_specs=[pl.BlockSpec((1, slots, pair), lambda e, idx: (e, 0, 0))] * 4
            + [
                pl.BlockSpec((2, experts * block, count), lambda e, idx: (0, 0, 0)),
                pl.BlockSpec(memory_space=pl.ANY),
            ],
            scratch_shapes=[
                pltpu.VMEM((count, width), BF16),
                pltpu.VMEM((pair, width), BF16),
                pltpu.VMEM((2, experts * block, count), BF16),
                pltpu.SemaphoreType.DMA((len(sizes),)),
                pltpu.SemaphoreType.DMA,
            ],
        ),
        out_shape=[jax.ShapeDtypeStruct((experts, slots, pair), BF16)] * 4
        + [
            jax.ShapeDtypeStruct((2, experts * block, count), BF16),
            jax.ShapeDtypeStruct((count, width), BF16),
        ],
        compiler_params=pltpu.CompilerParams(vmem_limit_bytes=VMEM_BYTES),
        cost_estimate=pl.CostEstimate(
            flops=4 * count * width * experts * pair,
            bytes_accessed=2 * (2 * count * width + 2 * own_weight.size),
            transcendentals=0,
        ),
    )(index, *pieces, own_weight, partner_weight, *hidden)


def early_grad_kernel(terms, *refs):
    out_ref = refs[-1]
    for half in range(2):
        total = jnp.dot(refs[0][half], refs[terms][...], preferred_element_type=F32)
        for i in range(1, terms):
            total += jnp.dot(refs[i][half], refs[terms + i][...], preferred_element_type=F32)
        out_ref[half] = total


def early_grad(scatters, rows, tile):
    _, height, count = scatters[0].shape
    width = rows[0].shape[1]
    terms = len(rows)
    return pl.pallas_call(
        functools.partial(early_grad_kernel, terms),
        grid=(width // tile,),
        in_specs=[pl.BlockSpec((2, height, count), lambda i: (0, 0, 0))] * terms
        + [pl.BlockSpec((count, tile), lambda i: (0, i))] * terms,
        out_specs=pl.BlockSpec((2, height, tile), lambda i: (0, 0, i)),
        out_shape=jax.ShapeDtypeStruct((2, height, width), F32),
        compiler_params=pltpu.CompilerParams(vmem_limit_bytes=VMEM_BYTES),
        cost_estimate=pl.CostEstimate(
            flops=4 * height * count * width * terms,
            bytes_accessed=2 * terms * (rows[0].size + scatters[0].size) + 8 * height * width,
            transcendentals=0,
        ),
    )(*scatters, *rows)


def partner_grad_kernel(idx_ref, scatter_ref, rows_ref, before_ref, out_ref):
    total = before_ref[0] + jnp.dot(scatter_ref[0], rows_ref[...], preferred_element_type=F32)
    out_ref[...] = total.astype(BF16)


def own_grad_kernel(idx_ref, scatter_ref, rows_ref, before_ref, arrived_ref, out_ref, held):
    total = before_ref[0] + jnp.dot(scatter_ref[0], rows_ref[...], preferred_element_type=F32)
    total += arrived_ref[...].astype(F32)
    block, experts, _ = out_ref.shape
    held[...] = total
    group = 8 // experts

    def move(i, carry):
        both = held[pl.ds(pl.multiple_of(i * 8, 8), 8), :]
        for j in range(group):
            out_ref[i * group + j] = both[j * experts : (j + 1) * experts]
        return carry

    lax.fori_loop(0, block // group, move, 0, unroll=4)


def late_grad(index, scatter, rows, before, arrived, experts, tile):
    _, height, count = scatter.shape
    width = rows.shape[1]
    in_specs = [
        pl.BlockSpec((1, height, count), lambda i, idx: (idx[0], 0, 0)),
        pl.BlockSpec((count, tile), lambda i, idx: (0, i)),
        pl.BlockSpec((1, height, tile), lambda i, idx: (idx[0], 0, i)),
    ]
    args = [scatter, rows, before]
    if arrived is None:
        kernel, scratch = partner_grad_kernel, []
        out_spec = pl.BlockSpec((height, tile), lambda i, idx: (0, i))
        out_shape = jax.ShapeDtypeStruct((height, width), BF16)
    else:
        kernel, scratch = own_grad_kernel, [pltpu.VMEM((height, tile), F32)]
        in_specs.append(pl.BlockSpec((height, tile), lambda i, idx: (0, i)))
        args.append(arrived)
        out_spec = pl.BlockSpec((height // experts, experts, tile), lambda i, idx: (0, 0, i))
        out_shape = jax.ShapeDtypeStruct((height // experts, experts, width), F32)
    return pl.pallas_call(
        kernel,
        grid_spec=pltpu.PrefetchScalarGridSpec(
            num_scalar_prefetch=1,
            grid=(width // tile,),
            in_specs=in_specs,
            out_specs=out_spec,
            scratch_shapes=scratch,
        ),
        out_shape=out_shape,
        compiler_params=pltpu.CompilerParams(vmem_limit_bytes=VMEM_BYTES),
        cost_estimate=pl.CostEstimate(
            flops=2 * height * count * width,
            bytes_accessed=2 * (rows.size + scatter.size) + 8 * height * width,
            transcendentals=0,
        ),
    )(index, *args)


def place_kernel(top_k, first, idx_ref, *refs):
    pieces = refs[:4]
    out_ref, sum_ref = refs[-2:]
    experts, slots, pair = pieces[0].shape
    m = pl.program_id(0)

    @pl.when(m == 0)
    def _():
        sum_ref[...] = jnp.zeros_like(sum_ref)

    for i in range(4):

        @pl.when(m == i)
        def _():
            out_ref[0] = pieces[i][...]
            for e in range(experts):
                row = pieces[i][e, slots - 8 :].astype(F32)[8 - top_k : 9 - top_k]
                sum_ref[e : e + 1] += row[:, : pair // 2] + row[:, pair // 2 :]


def place(index, pieces, before, sources, top_k):
    experts, slots, pair = pieces[0].shape
    first = before is None
    shape = (sources, experts, slots, 4 * pair)
    return pl.pallas_call(
        functools.partial(place_kernel, top_k, first),
        grid_spec=pltpu.PrefetchScalarGridSpec(
            num_scalar_prefetch=1,
            grid=(4,),
            in_specs=[pl.BlockSpec((experts, slots, pair), lambda m, idx: (0, 0, 0))] * 4
            + ([] if first else [pl.BlockSpec(memory_space=pl.ANY)]),
            out_specs=[
                pl.BlockSpec((1, experts, slots, pair), lambda m, idx: (idx[0], 0, 0, idx[1 + m])),
                pl.BlockSpec((experts, pair // 2), lambda m, idx: (0, 0)),
            ],
        ),
        out_shape=[
            jax.ShapeDtypeStruct(shape, BF16),
            jax.ShapeDtypeStruct((experts, pair // 2), F32),
        ],
        input_output_aliases={} if first else {5: 0},
        compiler_params=pltpu.CompilerParams(vmem_limit_bytes=VMEM_BYTES),
        cost_estimate=pl.CostEstimate(
            flops=0, bytes_accessed=16 * experts * slots * pair, transcendentals=0
        ),
    )(index, *pieces, *([] if first else [before]))


def on_device_tokens(grad_out, routes, affinity, saved_hidden, down_proj):
    reps, sources = lax.axis_size("rep"), lax.axis_size("exp")
    block, experts, width = down_proj.shape
    tokens, top_k = routes.shape
    most, hidden_units = saved_hidden.shape[3:]
    pair = 2 * block
    me = lax.axis_index("exp")
    rep = lax.axis_index("rep")
    chip, core = lax.div(rep, 2), lax.rem(rep, 2)
    chips = [jnp.bitwise_xor(chip, m) for m in range(4)]

    def across(array, bits):
        return lax.ppermute(array, "rep", [(i, i ^ bits) for i in range(reps)])

    def around(array, shift):
        return lax.ppermute(array, "exp", [(i, (i + shift) % sources) for i in range(sources)])

    totals = jnp.sum(affinity, axis=-1, keepdims=True)
    shares = affinity / totals
    route_weight = (ROUTE_SCALE * shares).astype(BF16)
    meta = jnp.concatenate([routes.astype(BF16).T, route_weight.T], axis=1)
    fence = lax.optimization_barrier
    half = tokens // 2

    def kernel(step, pieces):
        source = lax.rem(me - step + sources, sources)
        index = jnp.stack([source, me * experts, core]).astype(jnp.int32)
        *grads, scatter, row = project(index, pieces, own_weight, partner_weight, hidden, top_k)
        return grads, scatter, row

    def send_back(grads):
        return [grads[0]] + [across(grads[m], 2 * m) for m in range(1, 4)]

    def put(step, returned, placed):
        source = lax.rem(me - step + sources, sources)
        return place(jnp.stack([source] + chips).astype(jnp.int32), returned, placed, sources, top_k)

    metas = [meta] + [around(meta, shift) for shift in range(1, sources)]
    x0, y0, next1 = across(grad_out, 2), across(grad_out, 4), around(grad_out, 1)
    held = jnp.transpose(saved_hidden.reshape(experts, sources, most, 4, pair), (3, 0, 1, 2, 4))
    held = fence(held)
    own_weight = jnp.transpose(down_proj, (1, 0, 2)).reshape(experts * block, width)
    metas, x0, y0, next1, held, own_weight = fence((metas, x0, y0, next1, held, own_weight))

    metas = jnp.take(jnp.stack(metas), lax.rem(me - jnp.arange(sources) + sources, sources), axis=0)
    blank = jnp.zeros((experts, sources, SLOT_PAD - most - top_k, pair), BF16)
    metas = jnp.broadcast_to(metas[None], (experts, sources, top_k, pair))
    hidden = []
    for m in range(4):
        piece = lax.dynamic_index_in_dim(held, chips[m], axis=0, keepdims=False)
        piece = jnp.concatenate([piece, blank, metas], axis=2)
        hidden.append(across(piece, 2 * m) if m else piece)
    top0, bottom0 = across(x0[:half], 4), across(y0[half:], 2)
    next2 = around(next1, 1)
    partner_weight = across(own_weight, 1)
    hidden, top0, bottom0, next2, partner_weight, x0, y0, next1 = fence(
        (hidden, top0, bottom0, next2, partner_weight, x0, y0, next1)
    )

    x1, y1, x3 = across(next1, 2), across(next1, 4), around(x0, -1)
    grads0, scatter0, row0 = kernel(0, [grad_out, x0, y0, top0, bottom0])
    x1, y1, x3, grads0, scatter0, row0, y0, top0, bottom0, next2 = fence(
        (x1, y1, x3, grads0, scatter0, row0, y0, top0, bottom0, next2)
    )

    top1, bottom1 = across(x1[:half], 4), across(y1[half:], 2)
    x2, y2, y3, own3 = across(next2, 2), across(next2, 4), around(y0, -1), around(grad_out, -1)
    returned0 = send_back(grads0)
    top1, bottom1, x2, y2, y3, own3, returned0, top0, bottom0 = fence(
        (top1, bottom1, x2, y2, y3, own3, returned0, top0, bottom0)
    )

    top2, bottom2 = across(x2[:half], 4), across(y2[half:], 2)
    top3, bottom3 = around(top0, -1), around(bottom0, -1)
    grads1, scatter1, row1 = kernel(1, [next1, x1, y1, top1, bottom1])
    placed, combine0 = put(0, returned0, None)
    top2, bottom2, top3, bottom3, grads1, scatter1, row1, placed, combine0, x3 = fence(
        (top2, bottom2, top3, bottom3, grads1, scatter1, row1, placed, combine0, x3)
    )

    returned1 = send_back(grads1)
    grads2, scatter2, row2 = kernel(2, [next2, x2, y2, top2, bottom2])
    returned1, grads2, scatter2, row2, x3 = fence((returned1, grads2, scatter2, row2, x3))

    returned2 = send_back(grads2)
    placed, combine1 = put(1, returned1, placed)
    grads3, scatter3, row3 = kernel(3, [own3, x3, y3, top3, bottom3])
    before = early_grad([scatter0, scatter1, scatter2], [row0, row1, row2], 512)
    returned2, placed, combine1, grads3, scatter3, row3, before = fence(
        (returned2, placed, combine1, grads3, scatter3, row3, before)
    )

    returned3 = send_back(grads3)
    partner = late_grad((1 - core).reshape(1), scatter3, row3, before, None, experts, 896)
    partner = across(partner, 1)
    placed, combine2 = put(2, returned2, placed)
    placed, combine3 = put(3, returned3, placed)
    combines = [combine0, around(combine1, -1), around(combine2, -2), around(combine3, 1)]
    route_grad = 0.0
    expert_ids = jnp.arange(experts, dtype=routes.dtype)
    for step in range(sources):
        ids = lax.rem(me + step, sources) * experts + expert_ids
        named = routes.T[:, None, :] == ids[None, :, None]
        route_grad += jnp.sum(jnp.where(named, combines[step][None], 0.0), axis=1)
    hidden_grad = jnp.transpose(placed[:, :, :most], (1, 0, 2, 3)).reshape(saved_hidden.shape)
    route_grad = ROUTE_SCALE * route_grad.T
    affinity_grad = (route_grad - jnp.sum(route_grad * shares, axis=-1, keepdims=True)) / totals
    down_grad = late_grad(core.reshape(1), scatter3, row3, before, partner, experts, 896)
    return (affinity_grad, hidden_grad, down_grad)


def on_device(grad_out, routes, affinity, saved_hidden, down_proj):
    reps, sources = lax.axis_size("rep"), lax.axis_size("exp")
    block, experts, width = down_proj.shape
    tokens, top_k = routes.shape
    most = saved_hidden.shape[3]
    fits = block == 128 and tokens == 128 and width % 3584 == 0 and reps == 8 and 8 % experts == 0
    fits = fits and sources == 4 and most + top_k <= SLOT_PAD and top_k <= 8
    if fits and sources * tokens <= 2 * block * experts:
        return on_device_tokens(grad_out, routes, affinity, saved_hidden, down_proj)
    return on_device_weights(grad_out, routes, affinity, saved_hidden, down_proj)


def solution(mesh):
    return jax.shard_map(
        on_device,
        mesh=mesh,
        in_specs=(
            P(("rep", "exp"), None),
            P(("rep", "exp"), None),
            P(("rep", "exp"), None),
            P("rep", "exp", None, None, None),
            P("rep", "exp", None),
        ),
        out_specs=(
            P(("rep", "exp"), None),
            P("rep", "exp", None, None, None),
            P("rep", "exp", None),
        ),
        check_vma=False,
    )
```

```python
import functools
import jax
import jax.numpy as jnp
from jax import lax
from jax.experimental import pallas as pl
from jax.experimental.pallas import tpu as pltpu
from jax.sharding import PartitionSpec as P

ROUTE_SCALE = 2.5


def pack_routes(grad_rows, route_ids, route_weight, expert_count, most):
    expert_ids = jnp.arange(expert_count, dtype=jnp.int32)
    naming = jnp.sum((route_ids[:, :, None] == expert_ids[None, None, :]).astype(jnp.int32), axis=1)
    before = jnp.cumsum(naming, axis=0) - naming
    slot_ids = jnp.take_along_axis(before, route_ids, axis=1)
    placed = (route_ids * most + slot_ids).reshape(-1)
    token_ids = jnp.repeat(jnp.arange(grad_rows.shape[0], dtype=jnp.int32), route_ids.shape[1])
    source = jnp.zeros((expert_count * most,), jnp.int32).at[placed].set(token_ids)
    filled = jnp.zeros((expert_count * most,), jnp.int32).at[placed].set(1)
    weights = (
        jnp.zeros((expert_count * most,), route_weight.dtype)
        .at[placed]
        .set(route_weight.reshape(-1))
    )
    fetched = jnp.take(grad_rows, source, axis=0)
    packed = jnp.where(filled[:, None] > 0, fetched, jnp.zeros_like(fetched))
    return (packed, weights, placed)


def on_device_weights(grad_out, routes, affinity, saved_hidden, down_proj):
    exp_devices = lax.axis_size("exp")
    local_experts = down_proj.shape[1]
    expert_count = exp_devices * local_experts
    most = saved_hidden.shape[3]
    width = grad_out.shape[1]
    hidden_units = saved_hidden.shape[4]
    row_count = exp_devices * most
    totals = jnp.sum(affinity, axis=-1, keepdims=True)
    shares = affinity / totals
    route_weight = (ROUTE_SCALE * shares).astype(jnp.bfloat16)
    packed, weights, placed = pack_routes(grad_out, routes, route_weight, expert_count, most)
    outgoing = packed.reshape(exp_devices, local_experts, 1, most, width)
    outgoing_weight = weights.reshape(exp_devices, local_experts, 1, most)
    received, received_weight = (
        lax.all_to_all(outgoing, "exp", split_axis=0, concat_axis=2, tiled=True),
        lax.all_to_all(outgoing_weight, "exp", split_axis=0, concat_axis=2, tiled=True),
    )
    received = received.reshape(local_experts, row_count, width)
    row_scale = received_weight.reshape(local_experts, row_count).astype(jnp.float32)
    hidden = saved_hidden.reshape(local_experts, row_count, hidden_units)
    gathered = lax.all_gather(down_proj, "rep", axis=0, tiled=True)
    projected = jnp.einsum("erd,hed->erh", received, gathered, preferred_element_type=jnp.float32)
    hidden_grad = (row_scale[:, :, None] * projected).astype(jnp.bfloat16)
    combine_grad = ROUTE_SCALE * jnp.sum(hidden.astype(jnp.float32) * projected, axis=-1)
    scaled = (row_scale[:, :, None] * received.astype(jnp.float32)).astype(jnp.bfloat16)
    grad_term = jnp.einsum("erh,erd->hed", hidden, scaled, preferred_element_type=jnp.float32)
    down_grad = lax.psum_scatter(
        grad_term.astype(jnp.bfloat16), "rep", scatter_dimension=0, tiled=True
    ).astype(jnp.float32)
    returned = lax.all_to_all(
        combine_grad.reshape(local_experts, exp_devices, most),
        "exp",
        split_axis=1,
        concat_axis=0,
        tiled=True,
    )
    route_grad = jnp.take(returned.reshape(-1), placed).reshape(routes.shape)
    affinity_grad = (route_grad - jnp.sum(route_grad * shares, axis=-1, keepdims=True)) / totals
    return (affinity_grad, hidden_grad.reshape(saved_hidden.shape), down_grad)


SLOT_PAD = 64
F32 = jnp.float32
BF16 = jnp.bfloat16
VMEM_BYTES = 32 * 2**20


def nt_dot(a, b):
    return lax.dot_general(a, b, (((1,), (1,)), ((), ())), preferred_element_type=F32)


def tn_dot(a, b):
    return lax.dot_general(a, b, (((0,), (0,)), ((), ())), preferred_element_type=F32)


def project_kernel(top_k, sizes, items, idx_ref, *refs):
    parts = len(sizes)
    pieces, (own_weight, partner_weight) = refs[:parts], refs[parts : parts + 2]
    hidden_refs = refs[parts + 2 : parts + 2 + items]
    grad_refs = refs[parts + 2 + items : parts + 2 + 2 * items]
    scatter_ref, rows, weight, terms, slot_ref, scale_ref, sems = refs[parts + 2 + 2 * items :]
    step = pl.program_id(0)
    group, slots, pair = grad_refs[0].shape
    block = pair // 2
    tokens = rows.shape[0] // items
    experts = slot_ref.shape[0]
    core = idx_ref[5]

    @pl.when(step == 0)
    def _():
        copies, at = [], 0
        for i, size in enumerate(sizes):
            copies.append(pltpu.make_async_copy(pieces[i], rows.at[at : at + size], sems.at[i]))
            at += size
        for copy in copies:
            copy.start()
        metas = [hidden_refs[i][0, 0][slots - 8 :].astype(F32)[8 - top_k :] for i in range(items)]
        fill = jnp.full((8 - items, tokens), -1.0, F32)
        routes = [jnp.concatenate([m[k : k + 1, :tokens] for m in metas] + [fill], axis=0) for k in range(top_k)]
        weights = [jnp.concatenate([m[k : k + 1, tokens:] for m in metas] + [fill], axis=0) for k in range(top_k)]
        earlier = (
            lax.broadcasted_iota(jnp.int32, (tokens, tokens), 0)
            < lax.broadcasted_iota(jnp.int32, (tokens, tokens), 1)
        ).astype(BF16)
        every = []
        for e in range(experts):
            expert = (idx_ref[4] + e).astype(F32)
            named = jnp.zeros((8, tokens), F32)
            scale = jnp.zeros((8, tokens), F32)
            for k in range(top_k):
                hit = routes[k] == expert
                named = jnp.where(hit, 1.0, named)
                scale = jnp.where(hit, weights[k], scale)
            scale_ref[e] = scale
            every.append(named)
        named = jnp.concatenate(every, axis=0)
        before = jnp.dot(named.astype(BF16), earlier, preferred_element_type=F32)
        slot = jnp.where(named > 0, before, -1.0)
        for e in range(experts):
            slot_ref[e] = slot[e * 8 : (e + 1) * 8]
        for copy in copies:
            copy.wait()

    for q in range(group):
        to = pl.multiple_of(q * pair + core * block, block)
        weight[pl.ds(to, block), :] = own_weight[q * block : (q + 1) * block]
        to = pl.multiple_of(q * pair + (1 - core) * block, block)
        weight[pl.ds(to, block), :] = partner_weight[q * block : (q + 1) * block]
    projected = nt_dot(weight[...], rows[...])
    slot_ids = lax.broadcasted_iota(jnp.int32, (slots, tokens), 0).astype(F32)
    slot_rows = lax.broadcasted_iota(jnp.int32, (slots, pair), 0)
    for q in range(group):
        e = step * group + q
        slot_all, scale_all = slot_ref[e], scale_ref[e]
        for i in range(items):
            scale = scale_all[i : i + 1]
            pick = (slot_all[i : i + 1] == slot_ids).astype(BF16)
            own = projected[q * pair : (q + 1) * pair, i * tokens : (i + 1) * tokens]
            hidden = tn_dot(hidden_refs[i][q, 0], pick)
            grad = nt_dot(pick, (scale * own).astype(BF16))
            combine = jnp.sum(hidden * own, axis=0, keepdims=True)
            high = combine.astype(BF16).astype(F32)
            partial = jnp.concatenate([high, combine - high], axis=1)
            grad_refs[i][q] = jnp.where(slot_rows == slots - top_k, partial, grad).astype(BF16)
            scatter = (scale * hidden).astype(BF16)
            for half in range(2):
                at = pl.ds(pl.multiple_of(e * block, block), block)
                terms[half, at, i * tokens : (i + 1) * tokens] = scatter[half * block : (half + 1) * block]

    @pl.when(step == pl.num_programs(0) - 1)
    def _():
        height = terms.shape[1]
        row = lax.broadcasted_iota(jnp.int32, (height, height), 0)
        col = lax.broadcasted_iota(jnp.int32, (height, height), 1)
        order = (col == lax.rem(row, experts) * block + lax.div(row, experts)).astype(BF16)
        for half in range(2):
            scatter_ref[half] = jnp.dot(order, terms[half], preferred_element_type=F32).astype(BF16)


def project(index, items, own_weight, partner_weight, hidden, top_k, group=2):
    experts, sources, slots, pair = hidden[0].shape
    width = own_weight.shape[1]
    pieces = [piece for rows, _, _ in items for piece in rows]
    sizes = [p.shape[0] for p in pieces]
    count = sum(sizes)
    block = pair // 2
    return pl.pallas_call(
        functools.partial(project_kernel, top_k, sizes, len(items)),
        grid_spec=pltpu.PrefetchScalarGridSpec(
            num_scalar_prefetch=1,
            grid=(experts // group,),
            in_specs=[pl.BlockSpec(memory_space=pl.ANY)] * len(sizes)
            + [pl.BlockSpec((group * block, width), lambda e, idx: (e, 0))] * 2
            + [
                pl.BlockSpec((group, 1, slots, pair), lambda e, idx, k=k: (e, idx[k], 0, 0))
                for _, _, k in items
            ],
            out_specs=[pl.BlockSpec((group, slots, pair), lambda e, idx: (e, 0, 0))] * len(items)
            + [pl.BlockSpec((2, experts * block, count), lambda e, idx: (0, 0, 0))],
            scratch_shapes=[
                pltpu.VMEM((count, width), BF16),
                pltpu.VMEM((group * pair, width), BF16),
                pltpu.VMEM((2, experts * block, count), BF16),
                pltpu.VMEM((experts, 8, block), F32),
                pltpu.VMEM((experts, 8, block), F32),
                pltpu.SemaphoreType.DMA((len(sizes),)),
            ],
        ),
        out_shape=[jax.ShapeDtypeStruct((experts, slots, pair), BF16)] * len(items)
        + [jax.ShapeDtypeStruct((2, experts * block, count), BF16)],
        compiler_params=pltpu.CompilerParams(vmem_limit_bytes=VMEM_BYTES),
        cost_estimate=pl.CostEstimate(
            flops=4 * count * width * experts * pair,
            bytes_accessed=2 * (count * width + 2 * own_weight.size),
            transcendentals=0,
        ),
    )(index, *pieces, own_weight, partner_weight, *[hidden[m] for _, m, _ in items])


def fill_rows(pieces, rows):
    at = 0
    for piece in pieces:
        size = piece.shape[0]
        rows[at : at + size, :] = piece[...]
        at += size


def sum_terms(scatters, rows, half):
    total, at = None, 0
    for scatter in scatters:
        count = scatter.shape[2]
        term = jnp.dot(scatter[half], rows[at : at + count, :], preferred_element_type=F32)
        total = term if total is None else total + term
        at += count
    return total


def early_grad_kernel(terms, *refs):
    scatters, pieces, out_ref, rows = refs[:terms], refs[terms:-2], refs[-2], refs[-1]
    fill_rows(pieces, rows)
    for half in range(2):
        out_ref[half] = sum_terms(scatters, rows, half)


def early_grad(scatters, pieces, tile):
    height = scatters[0].shape[1]
    width = pieces[0].shape[1]
    count = sum(p.shape[0] for p in pieces)
    return pl.pallas_call(
        functools.partial(early_grad_kernel, len(scatters)),
        grid=(width // tile,),
        in_specs=[pl.BlockSpec(a.shape, lambda i: (0, 0, 0)) for a in scatters]
        + [pl.BlockSpec((p.shape[0], tile), lambda i: (0, i)) for p in pieces],
        out_specs=pl.BlockSpec((2, height, tile), lambda i: (0, 0, i)),
        out_shape=jax.ShapeDtypeStruct((2, height, width), F32),
        scratch_shapes=[pltpu.VMEM((count, tile), BF16)],
        compiler_params=pltpu.CompilerParams(vmem_limit_bytes=VMEM_BYTES),
        cost_estimate=pl.CostEstimate(
            flops=4 * height * count * width,
            bytes_accessed=2 * count * (width + 2 * height) + 8 * height * width,
            transcendentals=0,
        ),
    )(*scatters, *pieces)


def late_grad_kernel(terms, last, idx_ref, *refs):
    scatters, before_ref = refs[:terms], refs[terms]
    if not last:
        pieces, out_ref, rows = refs[terms + 1 : -2], refs[-2], refs[-1]
    else:
        arrived_ref, pieces, out_ref, rows, held = refs[terms + 1], refs[terms + 2 : -3], *refs[-3:]
    fill_rows(pieces, rows)
    total = before_ref[0] + sum_terms(scatters, rows, 0)
    if not last:
        out_ref[...] = total.astype(BF16)
        return
    held[...] = total + arrived_ref[...].astype(F32)
    block, experts, _ = out_ref.shape
    group = 8 // experts

    def move(i, carry):
        both = held[pl.ds(pl.multiple_of(i * 8, 8), 8), :]
        for j in range(group):
            out_ref[i * group + j] = both[j * experts : (j + 1) * experts]
        return carry

    lax.fori_loop(0, block // group, move, 0, unroll=4)


def late_grad(index, scatters, pieces, before, arrived, experts, tile):
    height = scatters[0].shape[1]
    width = pieces[0].shape[1]
    count = sum(p.shape[0] for p in pieces)
    in_specs = [pl.BlockSpec((1,) + a.shape[1:], lambda i, idx: (idx[0], 0, 0)) for a in scatters]
    in_specs.append(pl.BlockSpec((1, height, tile), lambda i, idx: (idx[0], 0, i)))
    args = [*scatters, before]
    scratch = [pltpu.VMEM((count, tile), BF16)]
    last = arrived is not None
    if last:
        in_specs.append(pl.BlockSpec((height, tile), lambda i, idx: (0, i)))
        args.append(arrived)
        scratch.append(pltpu.VMEM((height, tile), F32))
        out_spec = pl.BlockSpec((height // experts, experts, tile), lambda i, idx: (0, 0, i))
        out_shape = jax.ShapeDtypeStruct((height // experts, experts, width), F32)
    else:
        out_spec = pl.BlockSpec((height, tile), lambda i, idx: (0, i))
        out_shape = jax.ShapeDtypeStruct((height, width), BF16)
    in_specs += [pl.BlockSpec((p.shape[0], tile), lambda i, idx: (0, i)) for p in pieces]
    return pl.pallas_call(
        functools.partial(late_grad_kernel, len(scatters), last),
        grid_spec=pltpu.PrefetchScalarGridSpec(
            num_scalar_prefetch=1,
            grid=(width // tile,),
            in_specs=in_specs,
            out_specs=out_spec,
            scratch_shapes=scratch,
        ),
        out_shape=out_shape,
        compiler_params=pltpu.CompilerParams(vmem_limit_bytes=VMEM_BYTES),
        cost_estimate=pl.CostEstimate(
            flops=2 * height * count * width,
            bytes_accessed=2 * count * (width + height) + 8 * height * width,
            transcendentals=0,
        ),
    )(index, *args, *pieces)


def place_kernel(top_k, first, idx_ref, *refs):
    pieces = refs[:4]
    out_ref, sum_ref = refs[-2:]
    experts, slots, pair = pieces[0].shape
    m = pl.program_id(0)

    @pl.when(m == 0)
    def _():
        sum_ref[...] = jnp.zeros_like(sum_ref)

    for i in range(4):

        @pl.when(m == i)
        def _():
            out_ref[0] = pieces[i][...]
            for e in range(experts):
                row = pieces[i][e, slots - 8 :].astype(F32)[8 - top_k : 9 - top_k]
                sum_ref[e : e + 1] += row[:, : pair // 2] + row[:, pair // 2 :]


def place(index, pieces, before, sources, top_k):
    experts, slots, pair = pieces[0].shape
    first = before is None
    shape = (sources, experts, slots, 4 * pair)
    return pl.pallas_call(
        functools.partial(place_kernel, top_k, first),
        grid_spec=pltpu.PrefetchScalarGridSpec(
            num_scalar_prefetch=1,
            grid=(4,),
            in_specs=[pl.BlockSpec((experts, slots, pair), lambda m, idx: (0, 0, 0))] * 4
            + ([] if first else [pl.BlockSpec(memory_space=pl.ANY)]),
            out_specs=[
                pl.BlockSpec((1, experts, slots, pair), lambda m, idx: (idx[0], 0, 0, idx[1 + m])),
                pl.BlockSpec((experts, pair // 2), lambda m, idx: (0, 0)),
            ],
        ),
        out_shape=[
            jax.ShapeDtypeStruct(shape, BF16),
            jax.ShapeDtypeStruct((experts, pair // 2), F32),
        ],
        input_output_aliases={} if first else {5: 0},
        compiler_params=pltpu.CompilerParams(vmem_limit_bytes=VMEM_BYTES),
        cost_estimate=pl.CostEstimate(
            flops=0, bytes_accessed=16 * experts * slots * pair, transcendentals=0
        ),
    )(index, *pieces, *([] if first else [before]))


def on_device_tokens(grad_out, routes, affinity, saved_hidden, down_proj):
    reps, sources = lax.axis_size("rep"), lax.axis_size("exp")
    block, experts, width = down_proj.shape
    tokens, top_k = routes.shape
    most, hidden_units = saved_hidden.shape[3:]
    pair = 2 * block
    me = lax.axis_index("exp")
    rep = lax.axis_index("rep")
    chip, core = lax.div(rep, 2), lax.rem(rep, 2)
    chips = [jnp.bitwise_xor(chip, m) for m in range(4)]

    def across(array, bits):
        return lax.ppermute(array, "rep", [(i, i ^ bits) for i in range(reps)])

    def around(array, shift):
        return lax.ppermute(array, "exp", [(i, (i + shift) % sources) for i in range(sources)])

    totals = jnp.sum(affinity, axis=-1, keepdims=True)
    shares = affinity / totals
    route_weight = (ROUTE_SCALE * shares).astype(BF16)
    meta = jnp.concatenate([routes.astype(BF16).T, route_weight.T], axis=1)
    fence = lax.optimization_barrier
    half = tokens // 2

    slabs = [lax.rem(me - step + sources, sources) for step in range(sources)]
    index = jnp.stack(slabs + [me * experts, core]).astype(jnp.int32)

    def kernel(items):
        *grads, scatter = project(index, items, own_weight, partner_weight, hidden, top_k)
        return grads, scatter

    def send_back(grads, chip_of):
        return [across(g, 2 * m) if m else g for g, m in zip(grads, chip_of)]

    def put(step, returned, placed):
        spots = jnp.stack([slabs[step]] + chips).astype(jnp.int32)
        return place(spots, returned, placed, sources, top_k)

    x0, y0, next1 = across(grad_out, 2), across(grad_out, 4), around(grad_out, 1)
    metas = [meta, around(meta, 1), around(meta, 2), around(fence((meta, x0))[0], 3)]
    held = jnp.transpose(saved_hidden.reshape(experts, sources, most, 4, pair), (3, 0, 1, 2, 4))
    held = fence(held)
    held = [lax.dynamic_index_in_dim(held, chips[m], axis=0, keepdims=False) for m in range(4)]
    own_weight = jnp.transpose(down_proj, (1, 0, 2)).reshape(experts * block, width)
    metas, x0, y0, next1, held, own_weight = fence((metas, x0, y0, next1, held, own_weight))

    metas = jnp.take(jnp.stack(metas), lax.rem(me - jnp.arange(sources) + sources, sources), axis=0)
    blank = jnp.zeros((experts, sources, SLOT_PAD - most - top_k, pair), BF16)
    metas = jnp.broadcast_to(metas[None], (experts, sources, top_k, pair))
    hidden = []
    for m in range(4):
        piece = jnp.concatenate([held[m], blank, metas], axis=2)
        hidden.append(across(piece, 2 * m) if m else piece)
    top0, bottom0 = across(x0[:half], 4), across(y0[half:], 2)
    next2 = around(next1, 1)
    partner_weight = across(own_weight, 1)
    hidden, top0, bottom0, next2, partner_weight, x0, y0, next1 = fence(
        (hidden, top0, bottom0, next2, partner_weight, x0, y0, next1)
    )

    x1, y1, x3 = across(next1, 2), across(next1, 4), around(x0, -1)
    grads0, scatter0 = kernel([([grad_out], 0, 0), ([x0], 1, 0), ([y0], 2, 0), ([top0, bottom0], 3, 0)])
    x1, y1, x3, grads0, scatter0, y0, top0, bottom0, next2 = fence(
        (x1, y1, x3, grads0, scatter0, y0, top0, bottom0, next2)
    )

    top1, bottom1 = across(x1[:half], 4), across(y1[half:], 2)
    x2, y2, y3, own3 = across(next2, 2), across(next2, 4), around(y0, -1), around(grad_out, -1)
    returned0 = send_back(grads0, (0, 1, 2, 3))
    grads1, scatter1 = kernel([([next1], 0, 1), ([x1], 1, 1), ([y1], 2, 1), ([next2], 0, 2), ([x3], 1, 3)])
    top1, bottom1, x2, y2, y3, own3, returned0, top0, bottom0, grads1, scatter1 = fence(
        (top1, bottom1, x2, y2, y3, own3, returned0, top0, bottom0, grads1, scatter1)
    )

    top2, bottom2 = across(x2[:half], 4), across(y2[half:], 2)
    top3, bottom3 = around(top0, -1), around(bottom0, -1)
    returned1 = send_back(grads1, (0, 1, 2, 0, 1))
    grads2, scatter2 = kernel(
        [([x2], 1, 2), ([y2], 2, 2), ([y3], 2, 3), ([own3], 0, 3), ([top1, bottom1], 3, 1)]
    )
    before = early_grad(
        [scatter0, scatter1], [grad_out, x0, y0, top0, bottom0, next1, x1, y1, next2, x3], 512
    )
    placed, combine0 = put(0, returned0, None)
    top2, bottom2, top3, bottom3, returned1, grads2, scatter2, before, placed, combine0 = fence(
        (top2, bottom2, top3, bottom3, returned1, grads2, scatter2, before, placed, combine0)
    )

    returned2 = send_back(grads2, (1, 2, 2, 0, 3))
    grads3, scatter3 = kernel([([top2, bottom2], 3, 2), ([top3, bottom3], 3, 3)])
    returned3 = send_back(grads3, (3, 3))
    late = [x2, y2, y3, own3, top1, bottom1, top2, bottom2, top3, bottom3]
    late_scatters = [scatter2, scatter3]
    partner = late_grad((1 - core).reshape(1), late_scatters, late, before, None, experts, 896)
    partner = across(partner, 1)
    placed, combine1 = put(1, [*returned1[:3], returned2[4]], placed)
    placed, combine2 = put(2, [returned1[3], returned2[0], returned2[1], returned3[0]], placed)
    placed, combine3 = put(3, [returned2[3], returned1[4], returned2[2], returned3[1]], placed)
    combines = [combine0, around(combine1, -1), around(combine2, -2), around(combine3, 1)]
    route_grad = 0.0
    expert_ids = jnp.arange(experts, dtype=routes.dtype)
    for step in range(sources):
        ids = lax.rem(me + step, sources) * experts + expert_ids
        named = routes.T[:, None, :] == ids[None, :, None]
        route_grad += jnp.sum(jnp.where(named, combines[step][None], 0.0), axis=1)
    hidden_grad = jnp.transpose(placed[:, :, :most], (1, 0, 2, 3)).reshape(saved_hidden.shape)
    route_grad = ROUTE_SCALE * route_grad.T
    affinity_grad = (route_grad - jnp.sum(route_grad * shares, axis=-1, keepdims=True)) / totals
    down_grad = late_grad(core.reshape(1), late_scatters, late, before, partner, experts, 896)
    return (affinity_grad, hidden_grad, down_grad)


def on_device(grad_out, routes, affinity, saved_hidden, down_proj):
    reps, sources = lax.axis_size("rep"), lax.axis_size("exp")
    block, experts, width = down_proj.shape
    tokens, top_k = routes.shape
    most = saved_hidden.shape[3]
    fits = block == 128 and tokens == 128 and width % 3584 == 0 and reps == 8 and 8 % experts == 0
    fits = fits and sources == 4 and most + top_k <= SLOT_PAD and top_k <= 8
    if fits and sources * tokens <= 2 * block * experts:
        return on_device_tokens(grad_out, routes, affinity, saved_hidden, down_proj)
    return on_device_weights(grad_out, routes, affinity, saved_hidden, down_proj)


def solution(mesh):
    return jax.shard_map(
        on_device,
        mesh=mesh,
        in_specs=(
            P(("rep", "exp"), None),
            P(("rep", "exp"), None),
            P(("rep", "exp"), None),
            P("rep", "exp", None, None, None),
            P("rep", "exp", None),
        ),
        out_specs=(
            P(("rep", "exp"), None),
            P("rep", "exp", None, None, None),
            P("rep", "exp", None),
        ),
        check_vma=False,
    )
```

```python
import functools
import jax
import jax.numpy as jnp
from jax import lax
from jax.experimental import pallas as pl
from jax.experimental.pallas import tpu as pltpu
from jax.sharding import PartitionSpec as P

ROUTE_SCALE = 2.5


def pack_routes(grad_rows, route_ids, route_weight, expert_count, most):
    expert_ids = jnp.arange(expert_count, dtype=jnp.int32)
    naming = jnp.sum((route_ids[:, :, None] == expert_ids[None, None, :]).astype(jnp.int32), axis=1)
    before = jnp.cumsum(naming, axis=0) - naming
    slot_ids = jnp.take_along_axis(before, route_ids, axis=1)
    placed = (route_ids * most + slot_ids).reshape(-1)
    token_ids = jnp.repeat(jnp.arange(grad_rows.shape[0], dtype=jnp.int32), route_ids.shape[1])
    source = jnp.zeros((expert_count * most,), jnp.int32).at[placed].set(token_ids)
    filled = jnp.zeros((expert_count * most,), jnp.int32).at[placed].set(1)
    weights = (
        jnp.zeros((expert_count * most,), route_weight.dtype)
        .at[placed]
        .set(route_weight.reshape(-1))
    )
    fetched = jnp.take(grad_rows, source, axis=0)
    packed = jnp.where(filled[:, None] > 0, fetched, jnp.zeros_like(fetched))
    return (packed, weights, placed)


def on_device_weights(grad_out, routes, affinity, saved_hidden, down_proj):
    exp_devices = lax.axis_size("exp")
    local_experts = down_proj.shape[1]
    expert_count = exp_devices * local_experts
    most = saved_hidden.shape[3]
    width = grad_out.shape[1]
    hidden_units = saved_hidden.shape[4]
    row_count = exp_devices * most
    totals = jnp.sum(affinity, axis=-1, keepdims=True)
    shares = affinity / totals
    route_weight = (ROUTE_SCALE * shares).astype(jnp.bfloat16)
    packed, weights, placed = pack_routes(grad_out, routes, route_weight, expert_count, most)
    outgoing = packed.reshape(exp_devices, local_experts, 1, most, width)
    outgoing_weight = weights.reshape(exp_devices, local_experts, 1, most)
    received, received_weight = (
        lax.all_to_all(outgoing, "exp", split_axis=0, concat_axis=2, tiled=True),
        lax.all_to_all(outgoing_weight, "exp", split_axis=0, concat_axis=2, tiled=True),
    )
    received = received.reshape(local_experts, row_count, width)
    row_scale = received_weight.reshape(local_experts, row_count).astype(jnp.float32)
    hidden = saved_hidden.reshape(local_experts, row_count, hidden_units)
    gathered = lax.all_gather(down_proj, "rep", axis=0, tiled=True)
    projected = jnp.einsum("erd,hed->erh", received, gathered, preferred_element_type=jnp.float32)
    hidden_grad = (row_scale[:, :, None] * projected).astype(jnp.bfloat16)
    combine_grad = ROUTE_SCALE * jnp.sum(hidden.astype(jnp.float32) * projected, axis=-1)
    scaled = (row_scale[:, :, None] * received.astype(jnp.float32)).astype(jnp.bfloat16)
    grad_term = jnp.einsum("erh,erd->hed", hidden, scaled, preferred_element_type=jnp.float32)
    down_grad = lax.psum_scatter(
        grad_term.astype(jnp.bfloat16), "rep", scatter_dimension=0, tiled=True
    ).astype(jnp.float32)
    returned = lax.all_to_all(
        combine_grad.reshape(local_experts, exp_devices, most),
        "exp",
        split_axis=1,
        concat_axis=0,
        tiled=True,
    )
    route_grad = jnp.take(returned.reshape(-1), placed).reshape(routes.shape)
    affinity_grad = (route_grad - jnp.sum(route_grad * shares, axis=-1, keepdims=True)) / totals
    return (affinity_grad, hidden_grad.reshape(saved_hidden.shape), down_grad)


SLOT_PAD = 64
F32 = jnp.float32
BF16 = jnp.bfloat16
VMEM_BYTES = 36 * 2**20


def nt_dot(a, b):
    return lax.dot_general(a, b, (((1,), (1,)), ((), ())), preferred_element_type=F32)


def tn_dot(a, b):
    return lax.dot_general(a, b, (((0,), (0,)), ((), ())), preferred_element_type=F32)


def project_kernel(top_k, sizes, items, idx_ref, *refs):
    parts = len(sizes)
    pieces, (own_weight, partner_weight) = refs[:parts], refs[parts : parts + 2]
    hidden_refs = refs[parts + 2 : parts + 2 + items]
    grad_refs = refs[parts + 2 + items : parts + 2 + 2 * items]
    scatter_ref, rows, weight, terms, slot_ref, scale_ref, sems = refs[parts + 2 + 2 * items :]
    step = pl.program_id(0)
    group, slots, pair = grad_refs[0].shape
    block = pair // 2
    tokens = rows.shape[0] // items
    experts = slot_ref.shape[0]
    core = idx_ref[5]

    @pl.when(step == 0)
    def _():
        copies, at = [], 0
        for i, size in enumerate(sizes):
            copies.append(pltpu.make_async_copy(pieces[i], rows.at[at : at + size], sems.at[i]))
            at += size
        for copy in copies:
            copy.start()
        metas = [hidden_refs[i][0, 0][slots - 8 :].astype(F32)[8 - top_k :] for i in range(items)]
        fill = jnp.full((8 - items, tokens), -1.0, F32)
        routes = [jnp.concatenate([m[k : k + 1, :tokens] for m in metas] + [fill], axis=0) for k in range(top_k)]
        weights = [jnp.concatenate([m[k : k + 1, tokens:] for m in metas] + [fill], axis=0) for k in range(top_k)]
        earlier = (
            lax.broadcasted_iota(jnp.int32, (tokens, tokens), 0)
            < lax.broadcasted_iota(jnp.int32, (tokens, tokens), 1)
        ).astype(BF16)
        every = []
        for e in range(experts):
            expert = (idx_ref[4] + e).astype(F32)
            named = jnp.zeros((8, tokens), F32)
            scale = jnp.zeros((8, tokens), F32)
            for k in range(top_k):
                hit = routes[k] == expert
                named = jnp.where(hit, 1.0, named)
                scale = jnp.where(hit, weights[k], scale)
            scale_ref[e] = scale
            every.append(named)
        named = jnp.concatenate(every, axis=0)
        before = jnp.dot(named.astype(BF16), earlier, preferred_element_type=F32)
        slot = jnp.where(named > 0, before, -1.0)
        for e in range(experts):
            slot_ref[e] = slot[e * 8 : (e + 1) * 8]
        for copy in copies:
            copy.wait()

    for q in range(group):
        to = pl.multiple_of(q * pair + core * block, block)
        weight[pl.ds(to, block), :] = own_weight[q * block : (q + 1) * block]
        to = pl.multiple_of(q * pair + (1 - core) * block, block)
        weight[pl.ds(to, block), :] = partner_weight[q * block : (q + 1) * block]
    projected = nt_dot(weight[...], rows[...])
    slot_ids = lax.broadcasted_iota(jnp.int32, (slots, tokens), 0).astype(F32)
    slot_rows = lax.broadcasted_iota(jnp.int32, (slots, pair), 0)
    for q in range(group):
        e = step * group + q
        slot_all, scale_all = slot_ref[e], scale_ref[e]
        for i in range(items):
            scale = scale_all[i : i + 1]
            pick = (slot_all[i : i + 1] == slot_ids).astype(BF16)
            own = projected[q * pair : (q + 1) * pair, i * tokens : (i + 1) * tokens]
            hidden = tn_dot(hidden_refs[i][q, 0], pick)
            grad = nt_dot(pick, (scale * own).astype(BF16))
            combine = jnp.sum(hidden * own, axis=0, keepdims=True)
            high = combine.astype(BF16).astype(F32)
            partial = jnp.concatenate([high, combine - high], axis=1)
            grad_refs[i][q] = jnp.where(slot_rows == slots - top_k, partial, grad).astype(BF16)
            scatter = (scale * hidden).astype(BF16)
            for half in range(2):
                at = pl.ds(pl.multiple_of(e * block, block), block)
                terms[half, at, i * tokens : (i + 1) * tokens] = scatter[half * block : (half + 1) * block]

    @pl.when(step == pl.num_programs(0) - 1)
    def _():
        height = terms.shape[1]
        row = lax.broadcasted_iota(jnp.int32, (height, height), 0)
        col = lax.broadcasted_iota(jnp.int32, (8, height), 1)
        shift = block.bit_length() - 1
        to = (jnp.bitwise_and(col, block - 1) * experts + jnp.right_shift(col, shift))[0:1]
        order = (row == to).astype(BF16)
        for half in range(2):
            scatter_ref[half] = jnp.dot(order, terms[half], preferred_element_type=F32).astype(BF16)


def project(index, items, own_weight, partner_weight, hidden, top_k, group=2):
    experts, sources, slots, pair = hidden[0].shape
    width = own_weight.shape[1]
    pieces = [piece for rows, _, _ in items for piece in rows]
    sizes = [p.shape[0] for p in pieces]
    count = sum(sizes)
    block = pair // 2
    return pl.pallas_call(
        functools.partial(project_kernel, top_k, sizes, len(items)),
        grid_spec=pltpu.PrefetchScalarGridSpec(
            num_scalar_prefetch=1,
            grid=(experts // group,),
            in_specs=[pl.BlockSpec(memory_space=pl.ANY)] * len(sizes)
            + [pl.BlockSpec((group * block, width), lambda e, idx: (e, 0))] * 2
            + [
                pl.BlockSpec((group, 1, slots, pair), lambda e, idx, k=k: (e, idx[k], 0, 0))
                for _, _, k in items
            ],
            out_specs=[pl.BlockSpec((group, slots, pair), lambda e, idx: (e, 0, 0))] * len(items)
            + [pl.BlockSpec((2, experts * block, count), lambda e, idx: (0, 0, 0))],
            scratch_shapes=[
                pltpu.VMEM((count, width), BF16),
                pltpu.VMEM((group * pair, width), BF16),
                pltpu.VMEM((2, experts * block, count), BF16),
                pltpu.VMEM((experts, 8, block), F32),
                pltpu.VMEM((experts, 8, block), F32),
                pltpu.SemaphoreType.DMA((len(sizes),)),
            ],
        ),
        out_shape=[jax.ShapeDtypeStruct((experts, slots, pair), BF16)] * len(items)
        + [jax.ShapeDtypeStruct((2, experts * block, count), BF16)],
        compiler_params=pltpu.CompilerParams(vmem_limit_bytes=VMEM_BYTES),
        cost_estimate=pl.CostEstimate(
            flops=4 * count * width * experts * pair,
            bytes_accessed=2 * (count * width + 2 * own_weight.size),
            transcendentals=0,
        ),
    )(index, *pieces, own_weight, partner_weight, *[hidden[m] for _, m, _ in items])


def fill_rows(pieces, rows):
    at = 0
    for piece in pieces:
        size = piece.shape[0]
        rows[at : at + size, :] = piece[...]
        at += size


def sum_terms(scatters, rows, half):
    total, at = None, 0
    for scatter in scatters:
        count = scatter.shape[2]
        term = jnp.dot(scatter[half], rows[at : at + count, :], preferred_element_type=F32)
        total = term if total is None else total + term
        at += count
    return total


def half_grad_kernel(terms, arrivals, last, idx_ref, *refs):
    scatters, arrived = refs[:terms], refs[terms : terms + arrivals]
    if last:
        pieces, (out_ref, rows, held) = refs[terms + arrivals : -3], refs[-3:]
    else:
        pieces, (out_ref, rows) = refs[terms + arrivals : -2], refs[-2:]
    fill_rows(pieces, rows)
    total = sum_terms(scatters, rows, 0)
    for array in arrived:
        total += array[...].astype(F32)
    if not last:
        out_ref[...] = total.astype(BF16)
        return
    held[...] = total
    block, experts, _ = out_ref.shape
    group = 8 // experts

    def move(i, carry):
        both = held[pl.ds(pl.multiple_of(i * 8, 8), 8), :]
        for j in range(group):
            out_ref[i * group + j] = both[j * experts : (j + 1) * experts]
        return carry

    lax.fori_loop(0, block // group, move, 0, unroll=4)


def half_grad(index, scatters, pieces, arrived, experts, tile, last):
    height = scatters[0].shape[1]
    width = pieces[0].shape[1]
    count = sum(p.shape[0] for p in pieces)
    in_specs = [pl.BlockSpec((1,) + a.shape[1:], lambda i, idx: (idx[0], 0, 0)) for a in scatters]
    in_specs += [pl.BlockSpec((height, tile), lambda i, idx: (0, i)) for _ in arrived]
    in_specs += [pl.BlockSpec((p.shape[0], tile), lambda i, idx: (0, i)) for p in pieces]
    scratch = [pltpu.VMEM((count, tile), BF16)]
    if last:
        scratch.append(pltpu.VMEM((height, tile), F32))
        out_spec = pl.BlockSpec((height // experts, experts, tile), lambda i, idx: (0, 0, i))
        out_shape = jax.ShapeDtypeStruct((height // experts, experts, width), F32)
    else:
        out_spec = pl.BlockSpec((height, tile), lambda i, idx: (0, i))
        out_shape = jax.ShapeDtypeStruct((height, width), BF16)
    return pl.pallas_call(
        functools.partial(half_grad_kernel, len(scatters), len(arrived), last),
        grid_spec=pltpu.PrefetchScalarGridSpec(
            num_scalar_prefetch=1,
            grid=(width // tile,),
            in_specs=in_specs,
            out_specs=out_spec,
            scratch_shapes=scratch,
        ),
        out_shape=out_shape,
        compiler_params=pltpu.CompilerParams(vmem_limit_bytes=VMEM_BYTES),
        cost_estimate=pl.CostEstimate(
            flops=2 * height * count * width,
            bytes_accessed=2 * count * (width + height) + 4 * height * width,
            transcendentals=0,
        ),
    )(index, *scatters, *arrived, *pieces)


def place_kernel(top_k, first, idx_ref, *refs):
    pieces = refs[:4]
    out_ref, sum_ref = refs[-2:]
    experts, slots, pair = pieces[0].shape
    m = pl.program_id(0)

    @pl.when(m == 0)
    def _():
        sum_ref[...] = jnp.zeros_like(sum_ref)

    for i in range(4):

        @pl.when(m == i)
        def _():
            out_ref[0] = pieces[i][...]
            for e in range(experts):
                row = pieces[i][e, slots - 8 :].astype(F32)[8 - top_k : 9 - top_k]
                sum_ref[e : e + 1] += row[:, : pair // 2] + row[:, pair // 2 :]


def place(index, pieces, before, sources, top_k):
    experts, slots, pair = pieces[0].shape
    first = before is None
    shape = (sources, experts, slots, 4 * pair)
    return pl.pallas_call(
        functools.partial(place_kernel, top_k, first),
        grid_spec=pltpu.PrefetchScalarGridSpec(
            num_scalar_prefetch=1,
            grid=(4,),
            in_specs=[pl.BlockSpec((experts, slots, pair), lambda m, idx: (0, 0, 0))] * 4
            + ([] if first else [pl.BlockSpec(memory_space=pl.ANY)]),
            out_specs=[
                pl.BlockSpec((1, experts, slots, pair), lambda m, idx: (idx[0], 0, 0, idx[1 + m])),
                pl.BlockSpec((experts, pair // 2), lambda m, idx: (0, 0)),
            ],
        ),
        out_shape=[
            jax.ShapeDtypeStruct(shape, BF16),
            jax.ShapeDtypeStruct((experts, pair // 2), F32),
        ],
        input_output_aliases={} if first else {5: 0},
        compiler_params=pltpu.CompilerParams(vmem_limit_bytes=VMEM_BYTES),
        cost_estimate=pl.CostEstimate(
            flops=0, bytes_accessed=16 * experts * slots * pair, transcendentals=0
        ),
    )(index, *pieces, *([] if first else [before]))


def on_device_tokens(grad_out, routes, affinity, saved_hidden, down_proj):
    reps, sources = lax.axis_size("rep"), lax.axis_size("exp")
    block, experts, width = down_proj.shape
    tokens, top_k = routes.shape
    most, hidden_units = saved_hidden.shape[3:]
    pair = 2 * block
    me = lax.axis_index("exp")
    rep = lax.axis_index("rep")
    chip, core = lax.div(rep, 2), lax.rem(rep, 2)
    chips = [jnp.bitwise_xor(chip, m) for m in range(4)]

    def across(array, bits):
        return lax.ppermute(array, "rep", [(i, i ^ bits) for i in range(reps)])

    def around(array, shift):
        return lax.ppermute(array, "exp", [(i, (i + shift) % sources) for i in range(sources)])

    totals = jnp.sum(affinity, axis=-1, keepdims=True)
    shares = affinity / totals
    route_weight = (ROUTE_SCALE * shares).astype(BF16)
    meta = jnp.concatenate([routes.astype(BF16).T, route_weight.T], axis=1)
    fence = lax.optimization_barrier

    slabs = [lax.rem(me - step + sources, sources) for step in range(sources)]
    index = jnp.stack(slabs + [me * experts, core]).astype(jnp.int32)

    def kernel(items):
        *grads, scatter = project(index, items, own_weight, partner_weight, hidden, top_k)
        return grads, scatter

    def send_back(grads, chip_of):
        return [across(g, 2 * m) if m else g for g, m in zip(grads, chip_of)]

    def put(step, returned, placed):
        spots = jnp.stack([slabs[step]] + chips).astype(jnp.int32)
        return place(spots, returned, placed, sources, top_k)

    x0, y0, next1 = across(grad_out, 2), across(grad_out, 4), around(grad_out, 1)
    held = jnp.transpose(saved_hidden.reshape(experts, sources, most, 4, pair), (3, 0, 1, 2, 4))
    held = fence(held)
    held = [lax.dynamic_index_in_dim(held, chips[m], axis=0, keepdims=False) for m in range(4)]
    own_weight = jnp.transpose(down_proj, (1, 0, 2)).reshape(experts * block, width)
    last_meta, held, own_weight = fence((meta, held, own_weight))
    metas = [meta, around(meta, 1), around(meta, 2), around(last_meta, 3)]
    metas, x0, y0, next1, held, own_weight = fence((metas, x0, y0, next1, held, own_weight))

    xy0, x1 = across(x0, 4), across(next1, 2)
    next2, own3 = around(next1, 1), around(fence((grad_out, y0))[0], -1)
    metas = jnp.take(jnp.stack(metas), lax.rem(me - jnp.arange(sources) + sources, sources), axis=0)
    blank = jnp.zeros((experts, sources, SLOT_PAD - most - top_k, pair), BF16)
    metas = jnp.broadcast_to(metas[None], (experts, sources, top_k, pair))
    hidden = []
    for m in range(4):
        piece = jnp.concatenate([held[m], blank, metas], axis=2)
        hidden.append(across(piece, 2 * m) if m else piece)
    partner_weight = across(own_weight, 1)
    hidden, xy0, x1, next2, own3, partner_weight, x0, y0, next1 = fence(
        (hidden, xy0, x1, next2, own3, partner_weight, x0, y0, next1)
    )

    y1, x2, x3 = across(next1, 4), across(next2, 2), around(x0, -1)
    grads0, scatter0 = kernel([([grad_out], 0, 0), ([x0], 1, 0), ([y0], 2, 0), ([xy0], 3, 0)])
    y1, x2, x3, grads0, scatter0, y0, xy0, next2, x1 = fence(
        (y1, x2, x3, grads0, scatter0, y0, xy0, next2, x1)
    )

    xy1, y2, y3 = across(y1, 2), across(next2, 4), around(y0, -1)
    grads1, scatter1 = kernel(
        [([next1], 0, 1), ([x1], 1, 1), ([y1], 2, 1), ([next2], 0, 2), ([x2], 1, 2), ([x3], 1, 3)]
    )
    xy1, y2, y3, grads1, scatter1, xy0, x2, grads0 = fence((xy1, y2, y3, grads1, scatter1, xy0, x2, grads0))

    xy2, xy3 = across(x2, 4), around(xy0, -1)
    returned0 = send_back(grads0, (0, 1, 2, 3))
    grads2, scatter2 = kernel([([xy1], 3, 1), ([y2], 2, 2), ([own3], 0, 3), ([y3], 2, 3)])
    first = [grad_out, x0, y0, xy0, next1, x1, y1, next2, x2, x3]
    other, mine = (1 - core).reshape(1), core.reshape(1)
    partner = half_grad(other, [scatter0, scatter1], first, [], experts, 896, False)
    xy2, xy3, returned0, grads2, scatter2, partner, grads1 = fence(
        (xy2, xy3, returned0, grads2, scatter2, partner, grads1)
    )

    partner = across(partner, 1)
    returned1 = send_back(grads1, (0, 1, 2, 0, 1, 1))
    grads3, scatter3 = kernel([([xy2], 3, 2), ([xy3], 3, 3)])
    late = [xy1, y2, own3, y3, xy2, xy3]
    later = half_grad(other, [scatter2, scatter3], late, [], experts, 896, False)
    partner, returned1, later, grads3, scatter3 = fence((partner, returned1, later, grads3, scatter3))
    later = across(later, 1)
    returned2 = send_back(grads2, (3, 2, 0, 2))
    returned3 = send_back(grads3, (3, 3))
    placed, combine0 = put(0, returned0, None)
    placed, combine1 = put(1, [*returned1[:3], returned2[0]], placed)
    placed, combine2 = put(2, [returned1[3], returned1[4], returned2[1], returned3[0]], placed)
    placed, combine3 = put(3, [returned2[2], returned1[5], returned2[3], returned3[1]], placed)
    combines = [combine0, around(combine1, -1), around(combine2, -2), around(combine3, 1)]
    route_grad = 0.0
    expert_ids = jnp.arange(experts, dtype=routes.dtype)
    for step in range(sources):
        ids = lax.rem(me + step, sources) * experts + expert_ids
        named = routes.T[:, None, :] == ids[None, :, None]
        route_grad += jnp.sum(jnp.where(named, combines[step][None], 0.0), axis=1)
    hidden_grad = jnp.transpose(placed[:, :, :most], (1, 0, 2, 3)).reshape(saved_hidden.shape)
    route_grad = ROUTE_SCALE * route_grad.T
    affinity_grad = (route_grad - jnp.sum(route_grad * shares, axis=-1, keepdims=True)) / totals
    scatters = [scatter0, scatter1, scatter2, scatter3]
    down_grad = half_grad(mine, scatters, first + late, [partner, later], experts, 896, True)
    return (affinity_grad, hidden_grad, down_grad)


def on_device(grad_out, routes, affinity, saved_hidden, down_proj):
    reps, sources = lax.axis_size("rep"), lax.axis_size("exp")
    block, experts, width = down_proj.shape
    tokens, top_k = routes.shape
    most = saved_hidden.shape[3]
    fits = block == 128 and tokens == 128 and width % 3584 == 0 and reps == 8 and 8 % experts == 0
    fits = fits and sources == 4 and most + top_k <= SLOT_PAD and top_k <= 8
    if fits and sources * tokens <= 2 * block * experts:
        return on_device_tokens(grad_out, routes, affinity, saved_hidden, down_proj)
    return on_device_weights(grad_out, routes, affinity, saved_hidden, down_proj)


def solution(mesh):
    return jax.shard_map(
        on_device,
        mesh=mesh,
        in_specs=(
            P(("rep", "exp"), None),
            P(("rep", "exp"), None),
            P(("rep", "exp"), None),
            P("rep", "exp", None, None, None),
            P("rep", "exp", None),
        ),
        out_specs=(
            P(("rep", "exp"), None),
            P("rep", "exp", None, None, None),
            P("rep", "exp", None),
        ),
        check_vma=False,
    )
```

```python
import functools
import jax
import jax.numpy as jnp
from jax import lax
from jax.experimental import pallas as pl
from jax.experimental.pallas import tpu as pltpu
from jax.sharding import PartitionSpec as P

ROUTE_SCALE = 2.5


def pack_routes(grad_rows, route_ids, route_weight, expert_count, most):
    expert_ids = jnp.arange(expert_count, dtype=jnp.int32)
    naming = jnp.sum((route_ids[:, :, None] == expert_ids[None, None, :]).astype(jnp.int32), axis=1)
    before = jnp.cumsum(naming, axis=0) - naming
    slot_ids = jnp.take_along_axis(before, route_ids, axis=1)
    placed = (route_ids * most + slot_ids).reshape(-1)
    token_ids = jnp.repeat(jnp.arange(grad_rows.shape[0], dtype=jnp.int32), route_ids.shape[1])
    source = jnp.zeros((expert_count * most,), jnp.int32).at[placed].set(token_ids)
    filled = jnp.zeros((expert_count * most,), jnp.int32).at[placed].set(1)
    weights = (
        jnp.zeros((expert_count * most,), route_weight.dtype)
        .at[placed]
        .set(route_weight.reshape(-1))
    )
    fetched = jnp.take(grad_rows, source, axis=0)
    packed = jnp.where(filled[:, None] > 0, fetched, jnp.zeros_like(fetched))
    return (packed, weights, placed)


def on_device_weights(grad_out, routes, affinity, saved_hidden, down_proj):
    exp_devices = lax.axis_size("exp")
    local_experts = down_proj.shape[1]
    expert_count = exp_devices * local_experts
    most = saved_hidden.shape[3]
    width = grad_out.shape[1]
    hidden_units = saved_hidden.shape[4]
    row_count = exp_devices * most
    totals = jnp.sum(affinity, axis=-1, keepdims=True)
    shares = affinity / totals
    route_weight = (ROUTE_SCALE * shares).astype(jnp.bfloat16)
    packed, weights, placed = pack_routes(grad_out, routes, route_weight, expert_count, most)
    outgoing = packed.reshape(exp_devices, local_experts, 1, most, width)
    outgoing_weight = weights.reshape(exp_devices, local_experts, 1, most)
    received, received_weight = (
        lax.all_to_all(outgoing, "exp", split_axis=0, concat_axis=2, tiled=True),
        lax.all_to_all(outgoing_weight, "exp", split_axis=0, concat_axis=2, tiled=True),
    )
    received = received.reshape(local_experts, row_count, width)
    row_scale = received_weight.reshape(local_experts, row_count).astype(jnp.float32)
    hidden = saved_hidden.reshape(local_experts, row_count, hidden_units)
    gathered = lax.all_gather(down_proj, "rep", axis=0, tiled=True)
    projected = jnp.einsum("erd,hed->erh", received, gathered, preferred_element_type=jnp.float32)
    hidden_grad = (row_scale[:, :, None] * projected).astype(jnp.bfloat16)
    combine_grad = ROUTE_SCALE * jnp.sum(hidden.astype(jnp.float32) * projected, axis=-1)
    scaled = (row_scale[:, :, None] * received.astype(jnp.float32)).astype(jnp.bfloat16)
    grad_term = jnp.einsum("erh,erd->hed", hidden, scaled, preferred_element_type=jnp.float32)
    down_grad = lax.psum_scatter(
        grad_term.astype(jnp.bfloat16), "rep", scatter_dimension=0, tiled=True
    ).astype(jnp.float32)
    returned = lax.all_to_all(
        combine_grad.reshape(local_experts, exp_devices, most),
        "exp",
        split_axis=1,
        concat_axis=0,
        tiled=True,
    )
    route_grad = jnp.take(returned.reshape(-1), placed).reshape(routes.shape)
    affinity_grad = (route_grad - jnp.sum(route_grad * shares, axis=-1, keepdims=True)) / totals
    return (affinity_grad, hidden_grad.reshape(saved_hidden.shape), down_grad)


SLOT_PAD = 64
F32 = jnp.float32
BF16 = jnp.bfloat16
VMEM_BYTES = 36 * 2**20


def nt_dot(a, b):
    return lax.dot_general(a, b, (((1,), (1,)), ((), ())), preferred_element_type=F32)


def tn_dot(a, b):
    return lax.dot_general(a, b, (((0,), (0,)), ((), ())), preferred_element_type=F32)


def project_kernel(top_k, sizes, items, idx_ref, *refs):
    parts = len(sizes)
    pieces, weight_refs = refs[:parts], refs[parts : parts + 2]
    hidden_refs = refs[parts + 2 : parts + 2 + items]
    grad_refs = refs[parts + 2 + items : parts + 2 + 2 * items]
    scatter_ref, rows, weight, terms, slot_ref, scale_ref, sems = refs[parts + 2 + 2 * items :]
    step = pl.program_id(0)
    group, slots, pair = grad_refs[0].shape
    block = pair // 2
    tokens = rows.shape[0] // items
    experts = slot_ref.shape[0]

    @pl.when(step == 0)
    def _():
        copies, at = [], 0
        for i, size in enumerate(sizes):
            copies.append(pltpu.make_async_copy(pieces[i], rows.at[at : at + size], sems.at[i]))
            at += size
        for copy in copies:
            copy.start()
        metas = [hidden_refs[i][0, 0][slots - 8 :].astype(F32)[8 - top_k :] for i in range(items)]
        fill = jnp.full((8 - items, tokens), -1.0, F32)
        routes = [jnp.concatenate([m[k : k + 1, :tokens] for m in metas] + [fill], axis=0) for k in range(top_k)]
        weights = [jnp.concatenate([m[k : k + 1, tokens:] for m in metas] + [fill], axis=0) for k in range(top_k)]
        earlier = (
            lax.broadcasted_iota(jnp.int32, (tokens, tokens), 0)
            < lax.broadcasted_iota(jnp.int32, (tokens, tokens), 1)
        ).astype(BF16)
        every = []
        for e in range(experts):
            expert = (idx_ref[4] + e).astype(F32)
            named = jnp.zeros((8, tokens), F32)
            scale = jnp.zeros((8, tokens), F32)
            for k in range(top_k):
                hit = routes[k] == expert
                named = jnp.where(hit, 1.0, named)
                scale = jnp.where(hit, weights[k], scale)
            scale_ref[e] = scale
            every.append(named)
        named = jnp.concatenate(every, axis=0)
        before = jnp.dot(named.astype(BF16), earlier, preferred_element_type=F32)
        slot = jnp.where(named > 0, before, -1.0)
        for e in range(experts):
            slot_ref[e] = slot[e * 8 : (e + 1) * 8]
        for copy in copies:
            copy.wait()

    for q in range(group):
        for c in range(2):
            at = q * pair + c * block
            weight[at : at + block, :] = weight_refs[c][0, q * block : (q + 1) * block]
    projected = nt_dot(weight[...], rows[...])
    slot_ids = lax.broadcasted_iota(jnp.int32, (slots, tokens), 0).astype(F32)
    slot_rows = lax.broadcasted_iota(jnp.int32, (slots, pair), 0)
    for q in range(group):
        e = step * group + q
        slot_all, scale_all = slot_ref[e], scale_ref[e]
        for i in range(items):
            scale = scale_all[i : i + 1]
            pick = (slot_all[i : i + 1] == slot_ids).astype(BF16)
            own = projected[q * pair : (q + 1) * pair, i * tokens : (i + 1) * tokens]
            hidden = tn_dot(hidden_refs[i][q, 0], pick)
            grad = nt_dot(pick, (scale * own).astype(BF16))
            combine = jnp.sum(hidden * own, axis=0, keepdims=True)
            high = combine.astype(BF16).astype(F32)
            partial = jnp.concatenate([high, combine - high], axis=1)
            grad_refs[i][q] = jnp.where(slot_rows == slots - top_k, partial, grad).astype(BF16)
            scatter = (scale * hidden).astype(BF16)
            for half in range(2):
                at = pl.ds(pl.multiple_of(e * block, block), block)
                terms[half, at, i * tokens : (i + 1) * tokens] = scatter[half * block : (half + 1) * block]

    @pl.when(step == pl.num_programs(0) - 1)
    def _():
        height = terms.shape[1]
        row = lax.broadcasted_iota(jnp.int32, (height, height), 0)
        col = lax.broadcasted_iota(jnp.int32, (8, height), 1)
        shift = block.bit_length() - 1
        to = (jnp.bitwise_and(col, block - 1) * experts + jnp.right_shift(col, shift))[0:1]
        order = (row == to).astype(BF16)
        for half in range(2):
            scatter_ref[half] = jnp.dot(order, terms[half], preferred_element_type=F32).astype(BF16)


def project(index, items, weights, hidden, top_k, group=2):
    experts, sources, slots, pair = hidden[0].shape
    width = weights.shape[2]
    pieces = [piece for rows, _, _ in items for piece in rows]
    sizes = [p.shape[0] for p in pieces]
    count = sum(sizes)
    block = pair // 2
    return pl.pallas_call(
        functools.partial(project_kernel, top_k, sizes, len(items)),
        grid_spec=pltpu.PrefetchScalarGridSpec(
            num_scalar_prefetch=1,
            grid=(experts // group,),
            in_specs=[pl.BlockSpec(memory_space=pl.ANY)] * len(sizes)
            + [pl.BlockSpec((1, group * block, width), lambda e, idx, c=c: (c, e, 0)) for c in range(2)]
            + [
                pl.BlockSpec((group, 1, slots, pair), lambda e, idx, k=k: (e, idx[k], 0, 0))
                for _, _, k in items
            ],
            out_specs=[pl.BlockSpec((group, slots, pair), lambda e, idx: (e, 0, 0))] * len(items)
            + [pl.BlockSpec((2, experts * block, count), lambda e, idx: (0, 0, 0))],
            scratch_shapes=[
                pltpu.VMEM((count, width), BF16),
                pltpu.VMEM((group * pair, width), BF16),
                pltpu.VMEM((2, experts * block, count), BF16),
                pltpu.VMEM((experts, 8, block), F32),
                pltpu.VMEM((experts, 8, block), F32),
                pltpu.SemaphoreType.DMA((len(sizes),)),
            ],
        ),
        out_shape=[jax.ShapeDtypeStruct((experts, slots, pair), BF16)] * len(items)
        + [jax.ShapeDtypeStruct((2, experts * block, count), BF16)],
        compiler_params=pltpu.CompilerParams(vmem_limit_bytes=VMEM_BYTES),
        cost_estimate=pl.CostEstimate(
            flops=4 * count * width * experts * pair,
            bytes_accessed=2 * (count * width + weights.size),
            transcendentals=0,
        ),
    )(index, *pieces, weights, weights, *[hidden[m] for _, m, _ in items])


def fill_rows(pieces, rows):
    at = 0
    for piece in pieces:
        size = piece.shape[0]
        rows[at : at + size, :] = piece[...]
        at += size


def sum_terms(scatters, rows, half):
    total, at = None, 0
    for scatter in scatters:
        count = scatter.shape[2]
        term = jnp.dot(scatter[half], rows[at : at + count, :], preferred_element_type=F32)
        total = term if total is None else total + term
        at += count
    return total


def half_grad_kernel(terms, arrivals, last, idx_ref, *refs):
    scatters, arrived = refs[:terms], refs[terms : terms + arrivals]
    if last:
        pieces, (out_ref, rows, held) = refs[terms + arrivals : -3], refs[-3:]
    else:
        pieces, (out_ref, rows) = refs[terms + arrivals : -2], refs[-2:]
    fill_rows(pieces, rows)
    total = sum_terms(scatters, rows, 0)
    for array in arrived:
        total += array[...].astype(F32)
    if not last:
        out_ref[...] = total.astype(BF16)
        return
    held[...] = total
    block, experts, _ = out_ref.shape
    group = 8 // experts

    def move(i, carry):
        both = held[pl.ds(pl.multiple_of(i * 8, 8), 8), :]
        for j in range(group):
            out_ref[i * group + j] = both[j * experts : (j + 1) * experts]
        return carry

    lax.fori_loop(0, block // group, move, 0, unroll=4)


def half_grad(index, scatters, pieces, arrived, experts, tile, last):
    height = scatters[0].shape[1]
    width = pieces[0].shape[1]
    count = sum(p.shape[0] for p in pieces)
    in_specs = [pl.BlockSpec((1,) + a.shape[1:], lambda i, idx: (idx[0], 0, 0)) for a in scatters]
    in_specs += [pl.BlockSpec((height, tile), lambda i, idx: (0, i)) for _ in arrived]
    in_specs += [pl.BlockSpec((p.shape[0], tile), lambda i, idx: (0, i)) for p in pieces]
    scratch = [pltpu.VMEM((count, tile), BF16)]
    if last:
        scratch.append(pltpu.VMEM((height, tile), F32))
        out_spec = pl.BlockSpec((height // experts, experts, tile), lambda i, idx: (0, 0, i))
        out_shape = jax.ShapeDtypeStruct((height // experts, experts, width), F32)
    else:
        out_spec = pl.BlockSpec((height, tile), lambda i, idx: (0, i))
        out_shape = jax.ShapeDtypeStruct((height, width), BF16)
    return pl.pallas_call(
        functools.partial(half_grad_kernel, len(scatters), len(arrived), last),
        grid_spec=pltpu.PrefetchScalarGridSpec(
            num_scalar_prefetch=1,
            grid=(width // tile,),
            in_specs=in_specs,
            out_specs=out_spec,
            scratch_shapes=scratch,
        ),
        out_shape=out_shape,
        compiler_params=pltpu.CompilerParams(vmem_limit_bytes=VMEM_BYTES),
        cost_estimate=pl.CostEstimate(
            flops=2 * height * count * width,
            bytes_accessed=2 * count * (width + height) + 4 * height * width,
            transcendentals=0,
        ),
    )(index, *scatters, *arrived, *pieces)


def place_kernel(top_k, idx_ref, *refs):
    count = len(refs) - 5
    pieces, (out_ref, sum_ref, tails, out_sems, tail_sems) = refs[:count], refs[count:]
    experts, slots, pair = pieces[0].shape
    rows = tails.shape[2]
    slabs = count // 4
    stores, loads = [], []
    for i in range(count):
        column = pl.multiple_of(idx_ref[slabs + i % 4] * pair, pair)
        to = out_ref.at[idx_ref[i // 4], :, :, pl.ds(column, pair)]
        stores.append(pltpu.make_async_copy(pieces[i], to, out_sems.at[i]))
        loads.append(pltpu.make_async_copy(pieces[i].at[:, slots - rows :, :], tails.at[i], tail_sems.at[i]))
    for copy in loads + stores:
        copy.start()
    for copy in loads:
        copy.wait()
    for k in range(slabs):
        for e in range(experts):
            total = sum(tails[4 * k + m, e].astype(F32) for m in range(4))
            row = total[rows - top_k : rows - top_k + 1]
            sum_ref[k * experts + e : k * experts + e + 1] = row[:, : pair // 2] + row[:, pair // 2 :]
    for copy in stores:
        copy.wait()


def place(index, pieces, top_k):
    experts, slots, pair = pieces[0].shape
    slabs = len(pieces) // 4
    return pl.pallas_call(
        functools.partial(place_kernel, top_k),
        grid_spec=pltpu.PrefetchScalarGridSpec(
            num_scalar_prefetch=1,
            grid=(1,),
            in_specs=[pl.BlockSpec(memory_space=pl.ANY)] * len(pieces),
            out_specs=[
                pl.BlockSpec(memory_space=pl.ANY),
                pl.BlockSpec((slabs * experts, pair // 2), lambda i, idx: (0, 0)),
            ],
            scratch_shapes=[
                pltpu.VMEM((len(pieces), experts, 16, pair), BF16),
                pltpu.SemaphoreType.DMA((len(pieces),)),
                pltpu.SemaphoreType.DMA((len(pieces),)),
            ],
        ),
        out_shape=[
            jax.ShapeDtypeStruct((slabs, experts, slots, 4 * pair), BF16),
            jax.ShapeDtypeStruct((slabs * experts, pair // 2), F32),
        ],
        compiler_params=pltpu.CompilerParams(vmem_limit_bytes=8 * 2**20),
        cost_estimate=pl.CostEstimate(
            flops=0, bytes_accessed=4 * len(pieces) * experts * slots * pair, transcendentals=0
        ),
    )(index, *pieces)


def on_device_tokens(grad_out, routes, affinity, saved_hidden, down_proj):
    reps, sources = lax.axis_size("rep"), lax.axis_size("exp")
    block, experts, width = down_proj.shape
    tokens, top_k = routes.shape
    most, hidden_units = saved_hidden.shape[3:]
    pair = 2 * block
    me = lax.axis_index("exp")
    rep = lax.axis_index("rep")
    chip, core = lax.div(rep, 2), lax.rem(rep, 2)
    chips = [jnp.bitwise_xor(chip, m) for m in range(4)]

    def across(array, bits):
        return lax.ppermute(array, "rep", [(i, i ^ bits) for i in range(reps)])

    def around(array, shift):
        return lax.ppermute(array, "exp", [(i, (i + shift) % sources) for i in range(sources)])

    totals = jnp.sum(affinity, axis=-1, keepdims=True)
    shares = affinity / totals
    route_weight = (ROUTE_SCALE * shares).astype(BF16)
    meta = jnp.concatenate([routes.astype(BF16).T, route_weight.T], axis=1)
    fence = lax.optimization_barrier

    slabs = [lax.rem(me - step + sources, sources) for step in range(sources)]
    index = jnp.stack(slabs + [me * experts]).astype(jnp.int32)

    def kernel(items):
        *grads, scatter = project(index, items, weights, hidden, top_k)
        return grads, scatter

    def send_back(grads, chip_of):
        return [across(g, 2 * m) if m else g for g, m in zip(grads, chip_of)]

    x0, y0, next1 = across(grad_out, 2), across(grad_out, 4), around(grad_out, 1)
    held = jnp.transpose(saved_hidden.reshape(experts, sources, most, 4, pair), (3, 0, 1, 2, 4))
    held = fence(held)
    held = [lax.dynamic_index_in_dim(held, chips[m], axis=0, keepdims=False) for m in range(4)]
    last_meta, down_proj, held = fence((meta, down_proj, held))
    own_weight = jnp.transpose(down_proj, (1, 0, 2)).reshape(experts * block, width)
    cores = [[i, i + 1] for i in range(0, reps, 2)]
    weights = lax.all_gather(own_weight, "rep", axis=0, axis_index_groups=cores)
    metas = [meta, around(meta, 1), around(meta, 2), around(last_meta, 3)]
    metas, x0, y0, next1, held = fence((metas, x0, y0, next1, held))

    xy0, x1, next2 = across(x0, 4), across(next1, 2), around(next1, 1)
    own3 = around(fence((grad_out, next2))[0], -1)
    metas = jnp.take(jnp.stack(metas), lax.rem(me - jnp.arange(sources) + sources, sources), axis=0)
    blank = jnp.zeros((experts, sources, SLOT_PAD - most - top_k, pair), BF16)
    metas = jnp.broadcast_to(metas[None], (experts, sources, top_k, pair))
    hidden = []
    for m in range(4):
        piece = jnp.concatenate([held[m], blank, metas], axis=2)
        hidden.append(across(piece, 2 * m) if m else piece)
    hidden, xy0, x1, next2, own3, x0, y0, next1 = fence((hidden, xy0, x1, next2, own3, x0, y0, next1))

    y1, x2, x3 = across(next1, 4), across(next2, 2), around(x0, -1)
    grads0, scatter0 = kernel([([grad_out], 0, 0), ([x0], 1, 0), ([y0], 2, 0), ([xy0], 3, 0)])
    y1, x2, x3, grads0, scatter0, y0, xy0, next2, x1 = fence(
        (y1, x2, x3, grads0, scatter0, y0, xy0, next2, x1)
    )

    xy1, y2, y3 = across(y1, 2), across(next2, 4), around(y0, -1)
    grads1, scatter1 = kernel(
        [([next1], 0, 1), ([x1], 1, 1), ([y1], 2, 1), ([next2], 0, 2), ([x2], 1, 2), ([x3], 1, 3)]
    )
    xy1, y2, y3, grads1, scatter1, xy0, x2, grads0 = fence((xy1, y2, y3, grads1, scatter1, xy0, x2, grads0))

    xy2, xy3 = across(x2, 4), around(xy0, -1)
    returned0 = send_back(grads0, (0, 1, 2, 3))
    grads2, scatter2 = kernel([([xy1], 3, 1), ([y2], 2, 2), ([own3], 0, 3), ([y3], 2, 3)])
    first = [grad_out, x0, y0, xy0, next1, x1, y1, next2, x2, x3]
    other, mine = (1 - core).reshape(1), core.reshape(1)
    partner = half_grad(other, [scatter0, scatter1], first, [], experts, 896, False)
    xy2, xy3, returned0, grads2, scatter2, partner, grads1 = fence(
        (xy2, xy3, returned0, grads2, scatter2, partner, grads1)
    )

    partner = across(partner, 1)
    returned1 = send_back(grads1, (0, 1, 2, 0, 1, 1))
    grads3, scatter3 = kernel([([xy2], 3, 2), ([xy3], 3, 3)])
    late = [xy1, y2, own3, y3, xy2, xy3]
    later = half_grad(other, [scatter2, scatter3], late, [], experts, 896, False)
    partner, returned1, later, grads3, scatter3 = fence((partner, returned1, later, grads3, scatter3))
    later = across(later, 1)
    returned2 = send_back(grads2, (3, 2, 0, 2))
    returned3 = send_back(grads3, (3, 3))
    returned = [
        *returned0,
        *returned1[:3],
        returned2[0],
        returned1[3],
        returned1[4],
        returned2[1],
        returned3[0],
        returned2[2],
        returned1[5],
        returned2[3],
        returned3[1],
    ]
    placed, combine = place(jnp.stack(slabs + chips).astype(jnp.int32), returned, top_k)
    combine = combine.reshape(sources, experts, tokens)
    combines = [combine[0], around(combine[1], -1), around(combine[2], -2), around(combine[3], 1)]
    route_grad = 0.0
    expert_ids = jnp.arange(experts, dtype=routes.dtype)
    for step in range(sources):
        ids = lax.rem(me + step, sources) * experts + expert_ids
        named = routes.T[:, None, :] == ids[None, :, None]
        route_grad += jnp.sum(jnp.where(named, combines[step][None], 0.0), axis=1)
    hidden_grad = jnp.transpose(placed[:, :, :most], (1, 0, 2, 3)).reshape(saved_hidden.shape)
    route_grad = ROUTE_SCALE * route_grad.T
    affinity_grad = (route_grad - jnp.sum(route_grad * shares, axis=-1, keepdims=True)) / totals
    scatters = [scatter0, scatter1, scatter2, scatter3]
    down_grad = half_grad(mine, scatters, first + late, [partner, later], experts, 896, True)
    return (affinity_grad, hidden_grad, down_grad)


def on_device(grad_out, routes, affinity, saved_hidden, down_proj):
    reps, sources = lax.axis_size("rep"), lax.axis_size("exp")
    block, experts, width = down_proj.shape
    tokens, top_k = routes.shape
    most = saved_hidden.shape[3]
    fits = block == 128 and tokens == 128 and width % 3584 == 0 and reps == 8 and 8 % experts == 0
    fits = fits and sources == 4 and most + top_k <= SLOT_PAD and top_k <= 8
    if fits and sources * tokens <= 2 * block * experts:
        return on_device_tokens(grad_out, routes, affinity, saved_hidden, down_proj)
    return on_device_weights(grad_out, routes, affinity, saved_hidden, down_proj)


def solution(mesh):
    return jax.shard_map(
        on_device,
        mesh=mesh,
        in_specs=(
            P(("rep", "exp"), None),
            P(("rep", "exp"), None),
            P(("rep", "exp"), None),
            P("rep", "exp", None, None, None),
            P("rep", "exp", None),
        ),
        out_specs=(
            P(("rep", "exp"), None),
            P("rep", "exp", None, None, None),
            P("rep", "exp", None),
        ),
        check_vma=False,
    )
```

```python
import functools
import jax
import jax.numpy as jnp
from jax import lax
from jax.experimental import pallas as pl
from jax.experimental.pallas import tpu as pltpu
from jax.sharding import PartitionSpec as P

ROUTE_SCALE = 2.5


def pack_routes(grad_rows, route_ids, route_weight, expert_count, most):
    expert_ids = jnp.arange(expert_count, dtype=jnp.int32)
    naming = jnp.sum((route_ids[:, :, None] == expert_ids[None, None, :]).astype(jnp.int32), axis=1)
    before = jnp.cumsum(naming, axis=0) - naming
    slot_ids = jnp.take_along_axis(before, route_ids, axis=1)
    placed = (route_ids * most + slot_ids).reshape(-1)
    token_ids = jnp.repeat(jnp.arange(grad_rows.shape[0], dtype=jnp.int32), route_ids.shape[1])
    source = jnp.zeros((expert_count * most,), jnp.int32).at[placed].set(token_ids)
    filled = jnp.zeros((expert_count * most,), jnp.int32).at[placed].set(1)
    weights = (
        jnp.zeros((expert_count * most,), route_weight.dtype)
        .at[placed]
        .set(route_weight.reshape(-1))
    )
    fetched = jnp.take(grad_rows, source, axis=0)
    packed = jnp.where(filled[:, None] > 0, fetched, jnp.zeros_like(fetched))
    return (packed, weights, placed)


def on_device_weights(grad_out, routes, affinity, saved_hidden, down_proj):
    exp_devices = lax.axis_size("exp")
    local_experts = down_proj.shape[1]
    expert_count = exp_devices * local_experts
    most = saved_hidden.shape[3]
    width = grad_out.shape[1]
    hidden_units = saved_hidden.shape[4]
    row_count = exp_devices * most
    totals = jnp.sum(affinity, axis=-1, keepdims=True)
    shares = affinity / totals
    route_weight = (ROUTE_SCALE * shares).astype(jnp.bfloat16)
    packed, weights, placed = pack_routes(grad_out, routes, route_weight, expert_count, most)
    outgoing = packed.reshape(exp_devices, local_experts, 1, most, width)
    outgoing_weight = weights.reshape(exp_devices, local_experts, 1, most)
    received, received_weight = (
        lax.all_to_all(outgoing, "exp", split_axis=0, concat_axis=2, tiled=True),
        lax.all_to_all(outgoing_weight, "exp", split_axis=0, concat_axis=2, tiled=True),
    )
    received = received.reshape(local_experts, row_count, width)
    row_scale = received_weight.reshape(local_experts, row_count).astype(jnp.float32)
    hidden = saved_hidden.reshape(local_experts, row_count, hidden_units)
    gathered = lax.all_gather(down_proj, "rep", axis=0, tiled=True)
    projected = jnp.einsum("erd,hed->erh", received, gathered, preferred_element_type=jnp.float32)
    hidden_grad = (row_scale[:, :, None] * projected).astype(jnp.bfloat16)
    combine_grad = ROUTE_SCALE * jnp.sum(hidden.astype(jnp.float32) * projected, axis=-1)
    scaled = (row_scale[:, :, None] * received.astype(jnp.float32)).astype(jnp.bfloat16)
    grad_term = jnp.einsum("erh,erd->hed", hidden, scaled, preferred_element_type=jnp.float32)
    down_grad = lax.psum_scatter(
        grad_term.astype(jnp.bfloat16), "rep", scatter_dimension=0, tiled=True
    ).astype(jnp.float32)
    returned = lax.all_to_all(
        combine_grad.reshape(local_experts, exp_devices, most),
        "exp",
        split_axis=1,
        concat_axis=0,
        tiled=True,
    )
    route_grad = jnp.take(returned.reshape(-1), placed).reshape(routes.shape)
    affinity_grad = (route_grad - jnp.sum(route_grad * shares, axis=-1, keepdims=True)) / totals
    return (affinity_grad, hidden_grad.reshape(saved_hidden.shape), down_grad)


SLOT_PAD = 64
F32 = jnp.float32
BF16 = jnp.bfloat16
VMEM_BYTES = 36 * 2**20


def nt_dot(a, b):
    return lax.dot_general(a, b, (((1,), (1,)), ((), ())), preferred_element_type=F32)


def tn_dot(a, b):
    return lax.dot_general(a, b, (((0,), (0,)), ((), ())), preferred_element_type=F32)


def project_kernel(top_k, sizes, items, idx_ref, *refs):
    parts = len(sizes)
    pieces, weight_refs = refs[:parts], refs[parts : parts + 2]
    hidden_refs = refs[parts + 2 : parts + 2 + items]
    grad_refs = refs[parts + 2 + items : parts + 2 + 2 * items]
    scatter_ref, rows, weight, terms, slot_ref, scale_ref, sems = refs[parts + 2 + 2 * items :]
    step = pl.program_id(0)
    group, slots, pair = grad_refs[0].shape
    block = pair // 2
    tokens = rows.shape[0] // items
    experts = slot_ref.shape[0]

    @pl.when(step == 0)
    def _():
        copies, at = [], 0
        for i, size in enumerate(sizes):
            copies.append(pltpu.make_async_copy(pieces[i], rows.at[at : at + size], sems.at[i]))
            at += size
        for copy in copies:
            copy.start()
        metas = [hidden_refs[i][0, 0][slots - 8 :].astype(F32)[8 - top_k :] for i in range(items)]
        fill = jnp.full((8 - items, tokens), -1.0, F32)
        routes = [jnp.concatenate([m[k : k + 1, :tokens] for m in metas] + [fill], axis=0) for k in range(top_k)]
        weights = [jnp.concatenate([m[k : k + 1, tokens:] for m in metas] + [fill], axis=0) for k in range(top_k)]
        earlier = (
            lax.broadcasted_iota(jnp.int32, (tokens, tokens), 0)
            < lax.broadcasted_iota(jnp.int32, (tokens, tokens), 1)
        ).astype(BF16)
        every = []
        for e in range(experts):
            expert = (idx_ref[4] + e).astype(F32)
            named = jnp.zeros((8, tokens), F32)
            scale = jnp.zeros((8, tokens), F32)
            for k in range(top_k):
                hit = routes[k] == expert
                named = jnp.where(hit, 1.0, named)
                scale = jnp.where(hit, weights[k], scale)
            scale_ref[e] = scale
            every.append(named)
        named = jnp.concatenate(every, axis=0)
        before = jnp.dot(named.astype(BF16), earlier, preferred_element_type=F32)
        slot = jnp.where(named > 0, before, -1.0)
        for e in range(experts):
            slot_ref[e] = slot[e * 8 : (e + 1) * 8]
        for copy in copies:
            copy.wait()

    for q in range(group):
        for c in range(2):
            at = q * pair + c * block
            weight[at : at + block, :] = weight_refs[c][q * block : (q + 1) * block]
    projected = nt_dot(weight[...], rows[...])
    slot_ids = lax.broadcasted_iota(jnp.int32, (slots, tokens), 0).astype(F32)
    slot_rows = lax.broadcasted_iota(jnp.int32, (slots, pair), 0)
    for q in range(group):
        e = step * group + q
        slot_all, scale_all = slot_ref[e], scale_ref[e]
        for i in range(items):
            scale = scale_all[i : i + 1]
            pick = (slot_all[i : i + 1] == slot_ids).astype(BF16)
            own = projected[q * pair : (q + 1) * pair, i * tokens : (i + 1) * tokens]
            hidden = tn_dot(hidden_refs[i][q, 0], pick)
            grad = nt_dot(pick, (scale * own).astype(BF16))
            combine = jnp.sum(hidden * own, axis=0, keepdims=True)
            high = combine.astype(BF16).astype(F32)
            partial = jnp.concatenate([high, combine - high], axis=1)
            grad_refs[i][q] = jnp.where(slot_rows == slots - top_k, partial, grad).astype(BF16)
            scatter = (scale * hidden).astype(BF16)
            for half in range(2):
                at = pl.ds(pl.multiple_of(e * block, block), block)
                terms[half, at, i * tokens : (i + 1) * tokens] = scatter[half * block : (half + 1) * block]

    @pl.when(step == pl.num_programs(0) - 1)
    def _():
        height = terms.shape[1]
        row = lax.broadcasted_iota(jnp.int32, (height, height), 0)
        col = lax.broadcasted_iota(jnp.int32, (8, height), 1)
        shift = block.bit_length() - 1
        to = (jnp.bitwise_and(col, block - 1) * experts + jnp.right_shift(col, shift))[0:1]
        order = (row == to).astype(BF16)
        for half in range(2):
            scatter_ref[half] = jnp.dot(order, terms[half], preferred_element_type=F32).astype(BF16)


def project(index, items, own_weight, partner_weight, hidden, top_k, group=2):
    experts, sources, slots, pair = hidden[0].shape
    width = own_weight.shape[1]
    pieces = [piece for rows, _, _ in items for piece in rows]
    sizes = [p.shape[0] for p in pieces]
    count = sum(sizes)
    block = pair // 2
    return pl.pallas_call(
        functools.partial(project_kernel, top_k, sizes, len(items)),
        grid_spec=pltpu.PrefetchScalarGridSpec(
            num_scalar_prefetch=1,
            grid=(experts // group,),
            in_specs=[pl.BlockSpec(memory_space=pltpu.HBM)] * len(sizes)
            + [pl.BlockSpec((group * block, width), lambda e, idx: (e, 0))] * 2
            + [
                pl.BlockSpec((group, 1, slots, pair), lambda e, idx, k=k: (e, idx[k], 0, 0))
                for _, _, k in items
            ],
            out_specs=[pl.BlockSpec((group, slots, pair), lambda e, idx: (e, 0, 0))] * len(items)
            + [pl.BlockSpec((2, experts * block, count), lambda e, idx: (0, 0, 0))],
            scratch_shapes=[
                pltpu.VMEM((count, width), BF16),
                pltpu.VMEM((group * pair, width), BF16),
                pltpu.VMEM((2, experts * block, count), BF16),
                pltpu.VMEM((experts, 8, block), F32),
                pltpu.VMEM((experts, 8, block), F32),
                pltpu.SemaphoreType.DMA((len(sizes),)),
            ],
        ),
        out_shape=[jax.ShapeDtypeStruct((experts, slots, pair), BF16)] * len(items)
        + [jax.ShapeDtypeStruct((2, experts * block, count), BF16)],
        compiler_params=pltpu.CompilerParams(vmem_limit_bytes=VMEM_BYTES),
        cost_estimate=pl.CostEstimate(
            flops=4 * count * width * experts * pair,
            bytes_accessed=2 * (count * width + 2 * own_weight.size),
            transcendentals=0,
        ),
    )(index, *pieces, own_weight, partner_weight, *[hidden[m] for _, m, _ in items])


def fill_rows(pieces, rows):
    at = 0
    for piece in pieces:
        size = piece.shape[0]
        rows[at : at + size, :] = piece[...]
        at += size


def sum_terms(scatters, rows, half):
    total, at = None, 0
    for scatter in scatters:
        count = scatter.shape[2]
        term = jnp.dot(scatter[half], rows[at : at + count, :], preferred_element_type=F32)
        total = term if total is None else total + term
        at += count
    return total


def half_grad_kernel(terms, arrivals, last, *refs):
    scatters, arrived = refs[:terms], refs[terms : terms + arrivals]
    if last:
        pieces, (out_ref, rows, held) = refs[terms + arrivals : -3], refs[-3:]
    else:
        pieces, (out_ref, rows) = refs[terms + arrivals : -2], refs[-2:]
    fill_rows(pieces, rows)
    total = sum_terms(scatters, rows, 0)
    for array in arrived:
        total += array[...].astype(F32)
    if not last:
        out_ref[...] = total.astype(BF16)
        return
    held[...] = total
    block, experts, _ = out_ref.shape
    group = 8 // experts

    def move(i, carry):
        both = held[pl.ds(pl.multiple_of(i * 8, 8), 8), :]
        for j in range(group):
            out_ref[i * group + j] = both[j * experts : (j + 1) * experts]
        return carry

    lax.fori_loop(0, block // group, move, 0, unroll=4)


def half_grad(half, scatters, pieces, arrived, experts, tile, last):
    height = scatters[0].shape[1]
    width = pieces[0].shape[1]
    count = sum(p.shape[0] for p in pieces)
    in_specs = [pl.BlockSpec((1,) + a.shape[1:], lambda i: (half, 0, 0)) for a in scatters]
    in_specs += [pl.BlockSpec((height, tile), lambda i: (0, i)) for _ in arrived]
    in_specs += [pl.BlockSpec((p.shape[0], tile), lambda i: (0, i)) for p in pieces]
    scratch = [pltpu.VMEM((count, tile), BF16)]
    if last:
        scratch.append(pltpu.VMEM((height, tile), F32))
        out_spec = pl.BlockSpec((height // experts, experts, tile), lambda i: (0, 0, i))
        out_shape = jax.ShapeDtypeStruct((height // experts, experts, width), F32)
    else:
        out_spec = pl.BlockSpec((height, tile), lambda i: (0, i))
        out_shape = jax.ShapeDtypeStruct((height, width), BF16)
    return pl.pallas_call(
        functools.partial(half_grad_kernel, len(scatters), len(arrived), last),
        grid=(width // tile,),
        in_specs=in_specs,
        out_specs=out_spec,
        out_shape=out_shape,
        scratch_shapes=scratch,
        compiler_params=pltpu.CompilerParams(vmem_limit_bytes=VMEM_BYTES),
        cost_estimate=pl.CostEstimate(
            flops=2 * height * count * width,
            bytes_accessed=2 * count * (width + height) + 4 * height * width,
            transcendentals=0,
        ),
    )(*scatters, *arrived, *pieces)


def place_kernel(top_k, idx_ref, *refs):
    count = len(refs) - 5
    block = refs[0].shape[2] // 2
    pieces, (out_ref, sum_ref, tails, out_sems, tail_sems) = refs[:count], refs[count:]
    experts, slots, pair = pieces[0].shape
    rows = tails.shape[2]
    slabs = count // 4
    stores, loads = [], []
    for i in range(count):
        for half in range(2):
            column = pl.multiple_of(idx_ref[slabs + 2 * (i % 4) + half] * block, block)
            to = out_ref.at[idx_ref[i // 4], :, :, pl.ds(column, block)]
            part = pieces[i].at[:, :, half * block : (half + 1) * block]
            stores.append(pltpu.make_async_copy(part, to, out_sems.at[2 * i + half]))
        loads.append(pltpu.make_async_copy(pieces[i].at[:, slots - rows :, :], tails.at[i], tail_sems.at[i]))
    for copy in loads + stores:
        copy.start()
    for copy in loads:
        copy.wait()
    for k in range(slabs):
        for e in range(experts):
            total = sum(tails[4 * k + m, e].astype(F32) for m in range(4))
            row = total[rows - top_k : rows - top_k + 1]
            sum_ref[k * experts + e : k * experts + e + 1] = row[:, : pair // 2] + row[:, pair // 2 :]
    for copy in stores:
        copy.wait()


def place(index, pieces, top_k):
    experts, slots, pair = pieces[0].shape
    slabs = len(pieces) // 4
    return pl.pallas_call(
        functools.partial(place_kernel, top_k),
        grid_spec=pltpu.PrefetchScalarGridSpec(
            num_scalar_prefetch=1,
            grid=(1,),
            in_specs=[pl.BlockSpec(memory_space=pltpu.HBM)] * len(pieces),
            out_specs=[
                pl.BlockSpec(memory_space=pl.ANY),
                pl.BlockSpec((slabs * experts, pair // 2), lambda i, idx: (0, 0)),
            ],
            scratch_shapes=[
                pltpu.VMEM((len(pieces), experts, 16, pair), BF16),
                pltpu.SemaphoreType.DMA((2 * len(pieces),)),
                pltpu.SemaphoreType.DMA((len(pieces),)),
            ],
        ),
        out_shape=[
            jax.ShapeDtypeStruct((slabs, experts, slots, 4 * pair), BF16),
            jax.ShapeDtypeStruct((slabs * experts, pair // 2), F32),
        ],
        compiler_params=pltpu.CompilerParams(vmem_limit_bytes=8 * 2**20),
        cost_estimate=pl.CostEstimate(
            flops=0, bytes_accessed=4 * len(pieces) * experts * slots * pair, transcendentals=0
        ),
    )(index, *pieces)


def on_device_tokens(grad_out, routes, affinity, saved_hidden, down_proj):
    reps, sources = lax.axis_size("rep"), lax.axis_size("exp")
    block, experts, width = down_proj.shape
    tokens, top_k = routes.shape
    most, hidden_units = saved_hidden.shape[3:]
    pair = 2 * block
    me = lax.axis_index("exp")
    rep = lax.axis_index("rep")
    chip, core = lax.div(rep, 2), lax.rem(rep, 2)
    blocks = [2 * jnp.bitwise_xor(chip, m) + jnp.bitwise_xor(core, c) for m in range(4) for c in range(2)]

    def across(array, bits):
        return lax.ppermute(array, "rep", [(i, i ^ bits) for i in range(reps)])

    def around(array, shift):
        return lax.ppermute(array, "exp", [(i, (i + shift) % sources) for i in range(sources)])

    totals = jnp.sum(affinity, axis=-1, keepdims=True)
    shares = affinity / totals
    route_weight = (ROUTE_SCALE * shares).astype(BF16)
    meta = jnp.concatenate([routes.astype(BF16).T, route_weight.T], axis=1)
    fence = lax.optimization_barrier

    slabs = [lax.rem(me - step + sources, sources) for step in range(sources)]
    index = jnp.stack(slabs + [me * experts]).astype(jnp.int32)

    def kernel(items):
        *grads, scatter = project(index, items, own_weight, partner_weight, hidden, top_k)
        return grads, scatter

    def send_back(grads, chip_of):
        return [across(g, 2 * m) if m else g for g, m in zip(grads, chip_of)]

    x0, y0, next1 = across(grad_out, 2), across(grad_out, 4), around(grad_out, 1)
    held = jnp.transpose(saved_hidden.reshape(experts, sources, most, 8, block), (3, 0, 1, 2, 4))
    held = fence(held)
    held = [lax.dynamic_index_in_dim(held, b, axis=0, keepdims=False) for b in blocks]
    own_weight = jnp.transpose(down_proj, (1, 0, 2)).reshape(experts * block, width)
    last_meta, held, own_weight = fence((meta, held, own_weight))
    metas = [meta, around(meta, 1), around(meta, 2), around(last_meta, 3)]
    metas, x0, y0, next1, held, own_weight = fence((metas, x0, y0, next1, held, own_weight))

    xy0, x1, next2 = across(x0, 4), across(next1, 2), around(next1, 1)
    own3 = around(fence((grad_out, next2))[0], -1)
    partner_weight = across(own_weight, 1)
    metas = jnp.take(jnp.stack(metas), lax.rem(me - jnp.arange(sources) + sources, sources), axis=0)
    blank = jnp.zeros((experts, sources, SLOT_PAD - most - top_k, pair), BF16)
    metas = jnp.broadcast_to(metas[None], (experts, sources, top_k, pair))
    hidden = []
    for m in range(4):
        piece = jnp.concatenate([held[2 * m], held[2 * m + 1]], axis=3)
        hidden.append(jnp.concatenate([piece, blank, metas], axis=2))
    hidden = [
        hidden[0],
        across(fence((hidden[1], x1))[0], 2),
        across(fence((hidden[2], xy0))[0], 4),
        across(hidden[3], 6),
    ]
    hidden, xy0, x1, next2, own3, partner_weight, x0, y0, next1 = fence(
        (hidden, xy0, x1, next2, own3, partner_weight, x0, y0, next1)
    )

    y1, x2, x3 = across(next1, 4), across(next2, 2), around(x0, -1)
    grads0, scatter0 = kernel([([grad_out], 0, 0), ([x0], 1, 0), ([y0], 2, 0), ([xy0], 3, 0)])
    y1, x2, x3, grads0, scatter0, y0, xy0, next2, x1 = fence(
        (y1, x2, x3, grads0, scatter0, y0, xy0, next2, x1)
    )

    xy1, y2, y3 = across(y1, 2), across(next2, 4), around(y0, -1)
    grads1, scatter1 = kernel(
        [([next1], 0, 1), ([x1], 1, 1), ([y1], 2, 1), ([next2], 0, 2), ([x2], 1, 2), ([x3], 1, 3)]
    )
    xy1, y2, y3, grads1, scatter1, xy0, x2, grads0 = fence((xy1, y2, y3, grads1, scatter1, xy0, x2, grads0))

    xy2, xy3 = across(x2, 4), around(xy0, -1)
    returned0 = send_back(grads0, (0, 1, 2, 3))
    grads2, scatter2 = kernel([([xy1], 3, 1), ([y2], 2, 2), ([own3], 0, 3), ([y3], 2, 3)])
    first = [grad_out, x0, y0, xy0, next1, x1, y1, next2, x2, x3]
    mine, other = 0, 1
    partner = half_grad(other, [scatter0, scatter1], first, [], experts, 896, False)
    xy2, xy3, returned0, grads2, scatter2, partner, grads1 = fence(
        (xy2, xy3, returned0, grads2, scatter2, partner, grads1)
    )

    partner = across(partner, 1)
    returned1 = send_back(grads1, (0, 1, 2, 0, 1, 1))
    grads3, scatter3 = kernel([([xy2], 3, 2), ([xy3], 3, 3)])
    late = [xy1, y2, own3, y3, xy2, xy3]
    later = half_grad(other, [scatter2, scatter3], late, [], experts, 896, False)
    partner, returned1, later, grads3, scatter3 = fence((partner, returned1, later, grads3, scatter3))
    later = across(later, 1)
    returned2 = send_back(grads2, (3, 2, 0, 2))
    returned3 = send_back(grads3, (3, 3))
    returned = [
        *returned0,
        *returned1[:3],
        returned2[0],
        returned1[3],
        returned1[4],
        returned2[1],
        returned3[0],
        returned2[2],
        returned1[5],
        returned2[3],
        returned3[1],
    ]
    placed, combine = place(jnp.stack(slabs + blocks).astype(jnp.int32), returned, top_k)
    combine = combine.reshape(sources, experts, tokens)
    combines = [combine[0], around(combine[1], -1), around(combine[2], -2), around(combine[3], 1)]
    route_grad = 0.0
    expert_ids = jnp.arange(experts, dtype=routes.dtype)
    for step in range(sources):
        ids = lax.rem(me + step, sources) * experts + expert_ids
        named = routes.T[:, None, :] == ids[None, :, None]
        route_grad += jnp.sum(jnp.where(named, combines[step][None], 0.0), axis=1)
    hidden_grad = jnp.transpose(placed[:, :, :most], (1, 0, 2, 3)).reshape(saved_hidden.shape)
    route_grad = ROUTE_SCALE * route_grad.T
    affinity_grad = (route_grad - jnp.sum(route_grad * shares, axis=-1, keepdims=True)) / totals
    scatters = [scatter0, scatter1, scatter2, scatter3]
    down_grad = half_grad(mine, scatters, first + late, [partner, later], experts, 896, True)
    return (affinity_grad, hidden_grad, down_grad)


def on_device(grad_out, routes, affinity, saved_hidden, down_proj):
    reps, sources = lax.axis_size("rep"), lax.axis_size("exp")
    block, experts, width = down_proj.shape
    tokens, top_k = routes.shape
    most = saved_hidden.shape[3]
    fits = block == 128 and tokens == 128 and width % 3584 == 0 and reps == 8 and 8 % experts == 0
    fits = fits and sources == 4 and most + top_k <= SLOT_PAD and top_k <= 8
    if fits and sources * tokens <= 2 * block * experts:
        return on_device_tokens(grad_out, routes, affinity, saved_hidden, down_proj)
    return on_device_weights(grad_out, routes, affinity, saved_hidden, down_proj)


def solution(mesh):
    return jax.shard_map(
        on_device,
        mesh=mesh,
        in_specs=(
            P(("rep", "exp"), None),
            P(("rep", "exp"), None),
            P(("rep", "exp"), None),
            P("rep", "exp", None, None, None),
            P("rep", "exp", None),
        ),
        out_specs=(
            P(("rep", "exp"), None),
            P("rep", "exp", None, None, None),
            P("rep", "exp", None),
        ),
        check_vma=False,
    )
```

```python
import functools
import jax
import jax.numpy as jnp
from jax import lax
from jax.experimental import pallas as pl
from jax.experimental.pallas import tpu as pltpu
from jax.sharding import PartitionSpec as P

ROUTE_SCALE = 2.5


def pack_routes(grad_rows, route_ids, route_weight, expert_count, most):
    expert_ids = jnp.arange(expert_count, dtype=jnp.int32)
    naming = jnp.sum((route_ids[:, :, None] == expert_ids[None, None, :]).astype(jnp.int32), axis=1)
    before = jnp.cumsum(naming, axis=0) - naming
    slot_ids = jnp.take_along_axis(before, route_ids, axis=1)
    placed = (route_ids * most + slot_ids).reshape(-1)
    token_ids = jnp.repeat(jnp.arange(grad_rows.shape[0], dtype=jnp.int32), route_ids.shape[1])
    source = jnp.zeros((expert_count * most,), jnp.int32).at[placed].set(token_ids)
    filled = jnp.zeros((expert_count * most,), jnp.int32).at[placed].set(1)
    weights = (
        jnp.zeros((expert_count * most,), route_weight.dtype)
        .at[placed]
        .set(route_weight.reshape(-1))
    )
    fetched = jnp.take(grad_rows, source, axis=0)
    packed = jnp.where(filled[:, None] > 0, fetched, jnp.zeros_like(fetched))
    return (packed, weights, placed)


def on_device_weights(grad_out, routes, affinity, saved_hidden, down_proj):
    exp_devices = lax.axis_size("exp")
    local_experts = down_proj.shape[1]
    expert_count = exp_devices * local_experts
    most = saved_hidden.shape[3]
    width = grad_out.shape[1]
    hidden_units = saved_hidden.shape[4]
    row_count = exp_devices * most
    totals = jnp.sum(affinity, axis=-1, keepdims=True)
    shares = affinity / totals
    route_weight = (ROUTE_SCALE * shares).astype(jnp.bfloat16)
    packed, weights, placed = pack_routes(grad_out, routes, route_weight, expert_count, most)
    outgoing = packed.reshape(exp_devices, local_experts, 1, most, width)
    outgoing_weight = weights.reshape(exp_devices, local_experts, 1, most)
    received, received_weight = (
        lax.all_to_all(outgoing, "exp", split_axis=0, concat_axis=2, tiled=True),
        lax.all_to_all(outgoing_weight, "exp", split_axis=0, concat_axis=2, tiled=True),
    )
    received = received.reshape(local_experts, row_count, width)
    row_scale = received_weight.reshape(local_experts, row_count).astype(jnp.float32)
    hidden = saved_hidden.reshape(local_experts, row_count, hidden_units)
    gathered = lax.all_gather(down_proj, "rep", axis=0, tiled=True)
    projected = jnp.einsum("erd,hed->erh", received, gathered, preferred_element_type=jnp.float32)
    hidden_grad = (row_scale[:, :, None] * projected).astype(jnp.bfloat16)
    combine_grad = ROUTE_SCALE * jnp.sum(hidden.astype(jnp.float32) * projected, axis=-1)
    scaled = (row_scale[:, :, None] * received.astype(jnp.float32)).astype(jnp.bfloat16)
    grad_term = jnp.einsum("erh,erd->hed", hidden, scaled, preferred_element_type=jnp.float32)
    down_grad = lax.psum_scatter(
        grad_term.astype(jnp.bfloat16), "rep", scatter_dimension=0, tiled=True
    ).astype(jnp.float32)
    returned = lax.all_to_all(
        combine_grad.reshape(local_experts, exp_devices, most),
        "exp",
        split_axis=1,
        concat_axis=0,
        tiled=True,
    )
    route_grad = jnp.take(returned.reshape(-1), placed).reshape(routes.shape)
    affinity_grad = (route_grad - jnp.sum(route_grad * shares, axis=-1, keepdims=True)) / totals
    return (affinity_grad, hidden_grad.reshape(saved_hidden.shape), down_grad)


SLOT_PAD = 64
F32 = jnp.float32
BF16 = jnp.bfloat16
VMEM_BYTES = 36 * 2**20


def nt_dot(a, b):
    return lax.dot_general(a, b, (((1,), (1,)), ((), ())), preferred_element_type=F32)


def tn_dot(a, b):
    return lax.dot_general(a, b, (((0,), (0,)), ((), ())), preferred_element_type=F32)


def project_kernel(top_k, sizes, items, idx_ref, *refs):
    parts = len(sizes)
    pieces, weight_refs = refs[:parts], refs[parts : parts + 2]
    hidden_refs = refs[parts + 2 : parts + 2 + items]
    grad_refs = refs[parts + 2 + items : parts + 2 + 2 * items]
    scatter_ref, rows, weight, terms, slot_ref, scale_ref, sems = refs[parts + 2 + 2 * items :]
    step = pl.program_id(0)
    group, slots, pair = grad_refs[0].shape
    block = pair // 2
    tokens = rows.shape[0] // items
    experts = slot_ref.shape[0]

    @pl.when(step == 0)
    def _():
        copies, at = [], 0
        for i, size in enumerate(sizes):
            copies.append(pltpu.make_async_copy(pieces[i], rows.at[at : at + size], sems.at[i]))
            at += size
        for copy in copies:
            copy.start()
        metas = [hidden_refs[i][0, 0][slots - 8 :].astype(F32)[8 - top_k :] for i in range(items)]
        fill = jnp.full((8 - items, tokens), -1.0, F32)
        routes = [jnp.concatenate([m[k : k + 1, :tokens] for m in metas] + [fill], axis=0) for k in range(top_k)]
        weights = [jnp.concatenate([m[k : k + 1, tokens:] for m in metas] + [fill], axis=0) for k in range(top_k)]
        earlier = (
            lax.broadcasted_iota(jnp.int32, (tokens, tokens), 0)
            < lax.broadcasted_iota(jnp.int32, (tokens, tokens), 1)
        ).astype(BF16)
        every = []
        for e in range(experts):
            expert = (idx_ref[4] + e).astype(F32)
            named = jnp.zeros((8, tokens), F32)
            scale = jnp.zeros((8, tokens), F32)
            for k in range(top_k):
                hit = routes[k] == expert
                named = jnp.where(hit, 1.0, named)
                scale = jnp.where(hit, weights[k], scale)
            scale_ref[e] = scale
            every.append(named)
        named = jnp.concatenate(every, axis=0)
        before = jnp.dot(named.astype(BF16), earlier, preferred_element_type=F32)
        slot = jnp.where(named > 0, before, -1.0)
        for e in range(experts):
            slot_ref[e] = slot[e * 8 : (e + 1) * 8]
        for copy in copies:
            copy.wait()

    for q in range(group):
        for c in range(2):
            at = q * pair + c * block
            weight[at : at + block, :] = weight_refs[c][0, q * block : (q + 1) * block]
    projected = nt_dot(weight[...], rows[...])
    slot_ids = lax.broadcasted_iota(jnp.int32, (slots, tokens), 0).astype(F32)
    slot_rows = lax.broadcasted_iota(jnp.int32, (slots, pair), 0)
    for q in range(group):
        e = step * group + q
        slot_all, scale_all = slot_ref[e], scale_ref[e]
        for i in range(items):
            scale = scale_all[i : i + 1]
            pick = (slot_all[i : i + 1] == slot_ids).astype(BF16)
            own = projected[q * pair : (q + 1) * pair, i * tokens : (i + 1) * tokens]
            hidden = tn_dot(hidden_refs[i][q, 0], pick)
            grad = nt_dot(pick, (scale * own).astype(BF16))
            combine = jnp.sum(hidden * own, axis=0, keepdims=True)
            high = combine.astype(BF16).astype(F32)
            partial = jnp.concatenate([high, combine - high], axis=1)
            grad_refs[i][q] = jnp.where(slot_rows == slots - top_k, partial, grad).astype(BF16)
            scatter = (scale * hidden).astype(BF16)
            for half in range(2):
                at = pl.ds(pl.multiple_of(e * block, block), block)
                terms[half, at, i * tokens : (i + 1) * tokens] = scatter[half * block : (half + 1) * block]

    @pl.when(step == pl.num_programs(0) - 1)
    def _():
        height = terms.shape[1]
        row = lax.broadcasted_iota(jnp.int32, (height, height), 0)
        col = lax.broadcasted_iota(jnp.int32, (8, height), 1)
        shift = block.bit_length() - 1
        to = (jnp.bitwise_and(col, block - 1) * experts + jnp.right_shift(col, shift))[0:1]
        order = (row == to).astype(BF16)
        for half in range(2):
            scatter_ref[half] = jnp.dot(order, terms[half], preferred_element_type=F32).astype(BF16)


def project(index, items, weights, hidden, top_k, group=2):
    experts, sources, slots, pair = hidden[0].shape
    width = weights.shape[2]
    pieces = [piece for rows, _, _ in items for piece in rows]
    sizes = [p.shape[0] for p in pieces]
    count = sum(sizes)
    block = pair // 2
    return pl.pallas_call(
        functools.partial(project_kernel, top_k, sizes, len(items)),
        grid_spec=pltpu.PrefetchScalarGridSpec(
            num_scalar_prefetch=1,
            grid=(experts // group,),
            in_specs=[pl.BlockSpec(memory_space=pl.ANY)] * len(sizes)
            + [pl.BlockSpec((1, group * block, width), lambda e, idx, c=c: (c, e, 0)) for c in range(2)]
            + [
                pl.BlockSpec((group, 1, slots, pair), lambda e, idx, k=k: (e, idx[k], 0, 0))
                for _, _, k in items
            ],
            out_specs=[pl.BlockSpec((group, slots, pair), lambda e, idx: (e, 0, 0))] * len(items)
            + [pl.BlockSpec((2, experts * block, count), lambda e, idx: (0, 0, 0))],
            scratch_shapes=[
                pltpu.VMEM((count, width), BF16),
                pltpu.VMEM((group * pair, width), BF16),
                pltpu.VMEM((2, experts * block, count), BF16),
                pltpu.VMEM((experts, 8, block), F32),
                pltpu.VMEM((experts, 8, block), F32),
                pltpu.SemaphoreType.DMA((len(sizes),)),
            ],
        ),
        out_shape=[jax.ShapeDtypeStruct((experts, slots, pair), BF16)] * len(items)
        + [jax.ShapeDtypeStruct((2, experts * block, count), BF16)],
        compiler_params=pltpu.CompilerParams(vmem_limit_bytes=VMEM_BYTES),
        cost_estimate=pl.CostEstimate(
            flops=4 * count * width * experts * pair,
            bytes_accessed=2 * (count * width + weights.size),
            transcendentals=0,
        ),
    )(index, *pieces, weights, weights, *[hidden[m] for _, m, _ in items])


def fill_rows(pieces, rows):
    at = 0
    for piece in pieces:
        size = piece.shape[0]
        rows[at : at + size, :] = piece[...]
        at += size


def sum_terms(scatters, rows, half):
    total, at = None, 0
    for scatter in scatters:
        count = scatter.shape[2]
        term = jnp.dot(scatter[half], rows[at : at + count, :], preferred_element_type=F32)
        total = term if total is None else total + term
        at += count
    return total


def half_grad_kernel(terms, arrivals, last, *refs):
    scatters, arrived = refs[:terms], refs[terms : terms + arrivals]
    pieces, (out_ref, rows) = refs[terms + arrivals : -2], refs[-2:]
    fill_rows(pieces, rows)
    total = sum_terms(scatters, rows, 0)
    for array in arrived:
        total += array[...].astype(F32)
    if not last:
        out_ref[...] = total.astype(BF16)
        return
    out_ref[...] = total.reshape(out_ref.shape)


def half_grad(half, scatters, pieces, arrived, experts, tile, last):
    height = scatters[0].shape[1]
    width = pieces[0].shape[1]
    count = sum(p.shape[0] for p in pieces)
    in_specs = [pl.BlockSpec((1,) + a.shape[1:], lambda i: (half, 0, 0)) for a in scatters]
    in_specs += [pl.BlockSpec((height, tile), lambda i: (0, i)) for _ in arrived]
    in_specs += [pl.BlockSpec((p.shape[0], tile), lambda i: (0, i)) for p in pieces]
    scratch = [pltpu.VMEM((count, tile), BF16)]
    if last:
        out_spec = pl.BlockSpec((height // experts, experts, tile), lambda i: (0, 0, i))
        out_shape = jax.ShapeDtypeStruct((height // experts, experts, width), F32)
    else:
        out_spec = pl.BlockSpec((height, tile), lambda i: (0, i))
        out_shape = jax.ShapeDtypeStruct((height, width), BF16)
    return pl.pallas_call(
        functools.partial(half_grad_kernel, len(scatters), len(arrived), last),
        grid=(width // tile,),
        in_specs=in_specs,
        out_specs=out_spec,
        out_shape=out_shape,
        scratch_shapes=scratch,
        compiler_params=pltpu.CompilerParams(vmem_limit_bytes=VMEM_BYTES),
        cost_estimate=pl.CostEstimate(
            flops=2 * height * count * width,
            bytes_accessed=2 * count * (width + height) + 4 * height * width,
            transcendentals=0,
        ),
    )(*scatters, *arrived, *pieces)


def place_kernel(top_k, idx_ref, *refs):
    count = len(refs) - 5
    block = refs[0].shape[2] // 2
    pieces, (out_ref, sum_ref, tails, out_sems, tail_sems) = refs[:count], refs[count:]
    experts, slots, pair = pieces[0].shape
    rows = tails.shape[2]
    slabs = count // 4
    stores, loads = [], []
    for i in range(count):
        for half in range(2):
            column = pl.multiple_of(idx_ref[slabs + 2 * (i % 4) + half] * block, block)
            to = out_ref.at[idx_ref[i // 4], :, :, pl.ds(column, block)]
            part = pieces[i].at[:, :, half * block : (half + 1) * block]
            stores.append(pltpu.make_async_copy(part, to, out_sems.at[2 * i + half]))
        loads.append(pltpu.make_async_copy(pieces[i].at[:, slots - rows :, :], tails.at[i], tail_sems.at[i]))
    for copy in loads + stores:
        copy.start()
    for copy in loads:
        copy.wait()
    for k in range(slabs):
        for e in range(experts):
            total = sum(tails[4 * k + m, e].astype(F32) for m in range(4))
            row = total[rows - top_k : rows - top_k + 1]
            sum_ref[k * experts + e : k * experts + e + 1] = row[:, : pair // 2] + row[:, pair // 2 :]
    for copy in stores:
        copy.wait()


def place(index, pieces, top_k):
    experts, slots, pair = pieces[0].shape
    slabs = len(pieces) // 4
    return pl.pallas_call(
        functools.partial(place_kernel, top_k),
        grid_spec=pltpu.PrefetchScalarGridSpec(
            num_scalar_prefetch=1,
            grid=(1,),
            in_specs=[pl.BlockSpec(memory_space=pl.ANY)] * len(pieces),
            out_specs=[
                pl.BlockSpec(memory_space=pl.ANY),
                pl.BlockSpec((slabs * experts, pair // 2), lambda i, idx: (0, 0)),
            ],
            scratch_shapes=[
                pltpu.VMEM((len(pieces), experts, 16, pair), BF16),
                pltpu.SemaphoreType.DMA((2 * len(pieces),)),
                pltpu.SemaphoreType.DMA((len(pieces),)),
            ],
        ),
        out_shape=[
            jax.ShapeDtypeStruct((slabs, experts, slots, 4 * pair), BF16),
            jax.ShapeDtypeStruct((slabs * experts, pair // 2), F32),
        ],
        compiler_params=pltpu.CompilerParams(vmem_limit_bytes=60 * 2**20),
        cost_estimate=pl.CostEstimate(
            flops=0, bytes_accessed=4 * len(pieces) * experts * slots * pair, transcendentals=0
        ),
    )(index, *pieces)


def on_device_tokens(grad_out, routes, affinity, saved_hidden, down_proj):
    reps, sources = lax.axis_size("rep"), lax.axis_size("exp")
    block, experts, width = down_proj.shape
    tokens, top_k = routes.shape
    most, hidden_units = saved_hidden.shape[3:]
    pair = 2 * block
    me = lax.axis_index("exp")
    rep = lax.axis_index("rep")
    chip, core = lax.div(rep, 2), lax.rem(rep, 2)
    blocks = [2 * jnp.bitwise_xor(chip, m) + jnp.bitwise_xor(core, c) for m in range(4) for c in range(2)]

    def across(array, bits):
        return lax.ppermute(array, "rep", [(i, i ^ bits) for i in range(reps)])

    def around(array, shift):
        return lax.ppermute(array, "exp", [(i, (i + shift) % sources) for i in range(sources)])

    totals = jnp.sum(affinity, axis=-1, keepdims=True)
    shares = affinity / totals
    route_weight = (ROUTE_SCALE * shares).astype(BF16)
    meta = jnp.concatenate([routes.astype(BF16).T, route_weight.T], axis=1)
    fence = lax.optimization_barrier

    slabs = [lax.rem(me - step + sources, sources) for step in range(sources)]
    index = jnp.stack(slabs + [me * experts]).astype(jnp.int32)

    def kernel(items):
        *grads, scatter = project(index, items, weights, hidden, top_k)
        return grads, scatter

    def send_back(grads, chip_of):
        return [across(g, 2 * m) if m else g for g, m in zip(grads, chip_of)]

    x0, y0, next1 = across(grad_out, 2), across(grad_out, 4), around(grad_out, 1)
    held = jnp.transpose(saved_hidden.reshape(experts, sources, most, 8, block), (3, 0, 1, 2, 4))
    held = fence(held)
    held = [lax.dynamic_index_in_dim(held, b, axis=0, keepdims=False) for b in blocks]
    own_weight = jnp.transpose(down_proj, (1, 0, 2)).reshape(experts * block, width)
    last_meta, held, own_weight = fence((meta, held, own_weight))
    metas = [meta, around(meta, 1), around(meta, 2), around(last_meta, 3)]
    metas, x0, y0, next1, held, own_weight = fence((metas, x0, y0, next1, held, own_weight))

    xy0, x1, next2 = across(x0, 4), across(next1, 2), around(next1, 1)
    own3 = around(fence((grad_out, next2))[0], -1)
    partner_weight = across(own_weight, 1)
    metas = jnp.take(jnp.stack(metas), lax.rem(me - jnp.arange(sources) + sources, sources), axis=0)
    blank = jnp.zeros((experts, sources, SLOT_PAD - most - top_k, pair), BF16)
    metas = jnp.broadcast_to(metas[None], (experts, sources, top_k, pair))
    hidden = []
    for m in range(4):
        piece = jnp.concatenate([held[2 * m], held[2 * m + 1]], axis=3)
        hidden.append(jnp.concatenate([piece, blank, metas], axis=2))
    diagonal = across(hidden[3], 6)
    hidden = [
        hidden[0],
        across(fence((hidden[1], x1, diagonal))[0], 2),
        across(fence((hidden[2], xy0, diagonal))[0], 4),
        diagonal,
    ]
    weights = jnp.stack([own_weight, partner_weight])
    hidden, xy0, x1, next2, own3, weights, x0, y0, next1 = fence(
        (hidden, xy0, x1, next2, own3, weights, x0, y0, next1)
    )

    y1, x2, x3 = across(next1, 4), across(next2, 2), around(x0, -1)
    grads0, scatter0 = kernel([([grad_out], 0, 0), ([x0], 1, 0), ([y0], 2, 0), ([xy0], 3, 0)])
    y1, x2, x3, grads0, scatter0, y0, xy0, next2, x1 = fence(
        (y1, x2, x3, grads0, scatter0, y0, xy0, next2, x1)
    )

    xy1, y2, y3 = across(y1, 2), across(next2, 4), around(y0, -1)
    grads1, scatter1 = kernel(
        [([next1], 0, 1), ([x1], 1, 1), ([y1], 2, 1), ([next2], 0, 2), ([x2], 1, 2), ([x3], 1, 3)]
    )
    xy1, y2, y3, grads1, scatter1, xy0, x2, grads0 = fence((xy1, y2, y3, grads1, scatter1, xy0, x2, grads0))

    xy2, xy3 = across(x2, 4), around(xy0, -1)
    returned0 = send_back(grads0, (0, 1, 2, 3))
    grads2, scatter2 = kernel([([xy1], 3, 1), ([y2], 2, 2), ([own3], 0, 3), ([y3], 2, 3)])
    first = [grad_out, x0, y0, xy0, next1, x1, y1, next2, x2, x3]
    mine, other = 0, 1
    partner = half_grad(other, [scatter0, scatter1], first, [], experts, 896, False)
    xy2, xy3, returned0, grads2, scatter2, partner, grads1 = fence(
        (xy2, xy3, returned0, grads2, scatter2, partner, grads1)
    )

    partner = across(partner, 1)
    returned1 = send_back(grads1, (0, 1, 2, 0, 1, 1))
    grads3, scatter3 = kernel([([xy2], 3, 2), ([xy3], 3, 3)])
    late = [xy1, y2, own3, y3, xy2, xy3]
    later = half_grad(other, [scatter2, scatter3], late, [], experts, 896, False)
    partner, later = fence((partner, later))
    returned1, grads3 = fence((returned1, grads3))
    later = across(later, 1)
    returned2 = send_back(grads2, (3, 2, 0, 2))
    returned3 = send_back(grads3, (3, 3))
    returned = [
        *returned0,
        *returned1[:3],
        returned2[0],
        returned1[3],
        returned1[4],
        returned2[1],
        returned3[0],
        returned2[2],
        returned1[5],
        returned2[3],
        returned3[1],
    ]
    placed, combine = place(jnp.stack(slabs + blocks).astype(jnp.int32), returned, top_k)
    combine = combine.reshape(sources, experts, tokens)
    combines = [combine[0], around(combine[1], -1), around(combine[2], -2), around(combine[3], 1)]
    route_grad = 0.0
    expert_ids = jnp.arange(experts, dtype=routes.dtype)
    for step in range(sources):
        ids = lax.rem(me + step, sources) * experts + expert_ids
        named = routes.T[:, None, :] == ids[None, :, None]
        route_grad += jnp.sum(jnp.where(named, combines[step][None], 0.0), axis=1)
    hidden_grad = jnp.transpose(placed[:, :, :most], (1, 0, 2, 3)).reshape(saved_hidden.shape)
    route_grad = ROUTE_SCALE * route_grad.T
    affinity_grad = (route_grad - jnp.sum(route_grad * shares, axis=-1, keepdims=True)) / totals
    scatters = [scatter0, scatter1, scatter2, scatter3]
    down_grad = half_grad(mine, scatters, first + late, [partner, later], experts, 896, True)
    return (affinity_grad, hidden_grad, down_grad)


def on_device(grad_out, routes, affinity, saved_hidden, down_proj):
    reps, sources = lax.axis_size("rep"), lax.axis_size("exp")
    block, experts, width = down_proj.shape
    tokens, top_k = routes.shape
    most = saved_hidden.shape[3]
    fits = block == 128 and tokens == 128 and width % 3584 == 0 and reps == 8 and 8 % experts == 0
    fits = fits and sources == 4 and most + top_k <= SLOT_PAD and top_k <= 8
    if fits and sources * tokens <= 2 * block * experts:
        return on_device_tokens(grad_out, routes, affinity, saved_hidden, down_proj)
    return on_device_weights(grad_out, routes, affinity, saved_hidden, down_proj)


def solution(mesh):
    return jax.shard_map(
        on_device,
        mesh=mesh,
        in_specs=(
            P(("rep", "exp"), None),
            P(("rep", "exp"), None),
            P(("rep", "exp"), None),
            P("rep", "exp", None, None, None),
            P("rep", "exp", None),
        ),
        out_specs=(
            P(("rep", "exp"), None),
            P("rep", "exp", None, None, None),
            P("rep", "exp", None),
        ),
        check_vma=False,
    )
```

```python
import functools
import jax
import jax.numpy as jnp
from jax import lax
from jax.experimental import pallas as pl
from jax.experimental.pallas import tpu as pltpu
from jax.sharding import PartitionSpec as P

ROUTE_SCALE = 2.5


def pack_routes(grad_rows, route_ids, route_weight, expert_count, most):
    expert_ids = jnp.arange(expert_count, dtype=jnp.int32)
    naming = jnp.sum((route_ids[:, :, None] == expert_ids[None, None, :]).astype(jnp.int32), axis=1)
    before = jnp.cumsum(naming, axis=0) - naming
    slot_ids = jnp.take_along_axis(before, route_ids, axis=1)
    placed = (route_ids * most + slot_ids).reshape(-1)
    token_ids = jnp.repeat(jnp.arange(grad_rows.shape[0], dtype=jnp.int32), route_ids.shape[1])
    source = jnp.zeros((expert_count * most,), jnp.int32).at[placed].set(token_ids)
    filled = jnp.zeros((expert_count * most,), jnp.int32).at[placed].set(1)
    weights = (
        jnp.zeros((expert_count * most,), route_weight.dtype)
        .at[placed]
        .set(route_weight.reshape(-1))
    )
    fetched = jnp.take(grad_rows, source, axis=0)
    packed = jnp.where(filled[:, None] > 0, fetched, jnp.zeros_like(fetched))
    return (packed, weights, placed)


def on_device_weights(grad_out, routes, affinity, saved_hidden, down_proj):
    exp_devices = lax.axis_size("exp")
    local_experts = down_proj.shape[1]
    expert_count = exp_devices * local_experts
    most = saved_hidden.shape[3]
    width = grad_out.shape[1]
    hidden_units = saved_hidden.shape[4]
    row_count = exp_devices * most
    totals = jnp.sum(affinity, axis=-1, keepdims=True)
    shares = affinity / totals
    route_weight = (ROUTE_SCALE * shares).astype(jnp.bfloat16)
    packed, weights, placed = pack_routes(grad_out, routes, route_weight, expert_count, most)
    outgoing = packed.reshape(exp_devices, local_experts, 1, most, width)
    outgoing_weight = weights.reshape(exp_devices, local_experts, 1, most)
    received, received_weight = (
        lax.all_to_all(outgoing, "exp", split_axis=0, concat_axis=2, tiled=True),
        lax.all_to_all(outgoing_weight, "exp", split_axis=0, concat_axis=2, tiled=True),
    )
    received = received.reshape(local_experts, row_count, width)
    row_scale = received_weight.reshape(local_experts, row_count).astype(jnp.float32)
    hidden = saved_hidden.reshape(local_experts, row_count, hidden_units)
    gathered = lax.all_gather(down_proj, "rep", axis=0, tiled=True)
    projected = jnp.einsum("erd,hed->erh", received, gathered, preferred_element_type=jnp.float32)
    hidden_grad = (row_scale[:, :, None] * projected).astype(jnp.bfloat16)
    combine_grad = ROUTE_SCALE * jnp.sum(hidden.astype(jnp.float32) * projected, axis=-1)
    scaled = (row_scale[:, :, None] * received.astype(jnp.float32)).astype(jnp.bfloat16)
    grad_term = jnp.einsum("erh,erd->hed", hidden, scaled, preferred_element_type=jnp.float32)
    down_grad = lax.psum_scatter(
        grad_term.astype(jnp.bfloat16), "rep", scatter_dimension=0, tiled=True
    ).astype(jnp.float32)
    returned = lax.all_to_all(
        combine_grad.reshape(local_experts, exp_devices, most),
        "exp",
        split_axis=1,
        concat_axis=0,
        tiled=True,
    )
    route_grad = jnp.take(returned.reshape(-1), placed).reshape(routes.shape)
    affinity_grad = (route_grad - jnp.sum(route_grad * shares, axis=-1, keepdims=True)) / totals
    return (affinity_grad, hidden_grad.reshape(saved_hidden.shape), down_grad)


SLOT_PAD = 64
F32 = jnp.float32
BF16 = jnp.bfloat16
VMEM_BYTES = 30 * 2**20


def nt_dot(a, b):
    return lax.dot_general(a, b, (((1,), (1,)), ((), ())), preferred_element_type=F32)


def tn_dot(a, b):
    return lax.dot_general(a, b, (((0,), (0,)), ((), ())), preferred_element_type=F32)


def project_kernel(top_k, sizes, items, idx_ref, *refs):
    parts = len(sizes)
    pieces, weight_refs = refs[:parts], refs[parts : parts + 2]
    hidden_refs = refs[parts + 2 : parts + 2 + items]
    grad_refs = refs[parts + 2 + items : parts + 2 + 2 * items]
    scatter_ref, rows, weight, terms, slot_ref, scale_ref, sems = refs[parts + 2 + 2 * items :]
    step = pl.program_id(0)
    group, slots, pair = grad_refs[0].shape
    block = pair // 2
    tokens = rows.shape[0] // items
    experts = slot_ref.shape[0]

    @pl.when(step == 0)
    def _():
        copies, at = [], 0
        for i, size in enumerate(sizes):
            copies.append(pltpu.make_async_copy(pieces[i], rows.at[at : at + size], sems.at[i]))
            at += size
        for copy in copies:
            copy.start()
        metas = [hidden_refs[i][0, 0][slots - 8 :].astype(F32)[8 - top_k :] for i in range(items)]
        fill = jnp.full((8 - items, tokens), -1.0, F32)
        routes = [jnp.concatenate([m[k : k + 1, :tokens] for m in metas] + [fill], axis=0) for k in range(top_k)]
        weights = [jnp.concatenate([m[k : k + 1, tokens:] for m in metas] + [fill], axis=0) for k in range(top_k)]
        earlier = (
            lax.broadcasted_iota(jnp.int32, (tokens, tokens), 0)
            < lax.broadcasted_iota(jnp.int32, (tokens, tokens), 1)
        ).astype(BF16)
        every = []
        for e in range(experts):
            expert = (idx_ref[4] + e).astype(F32)
            named = jnp.zeros((8, tokens), F32)
            scale = jnp.zeros((8, tokens), F32)
            for k in range(top_k):
                hit = routes[k] == expert
                named = jnp.where(hit, 1.0, named)
                scale = jnp.where(hit, weights[k], scale)
            scale_ref[e] = scale
            every.append(named)
        named = jnp.concatenate(every, axis=0)
        before = jnp.dot(named.astype(BF16), earlier, preferred_element_type=F32)
        slot = jnp.where(named > 0, before, -1.0)
        for e in range(experts):
            slot_ref[e] = slot[e * 8 : (e + 1) * 8]
        for copy in copies:
            copy.wait()

    for q in range(group):
        for c in range(2):
            at = q * pair + c * block
            weight[at : at + block, :] = weight_refs[c][0, q * block : (q + 1) * block]
    projected = nt_dot(weight[...], rows[...])
    slot_ids = lax.broadcasted_iota(jnp.int32, (slots, tokens), 0).astype(F32)
    slot_rows = lax.broadcasted_iota(jnp.int32, (slots, pair), 0)
    for q in range(group):
        e = step * group + q
        slot_all, scale_all = slot_ref[e], scale_ref[e]
        for i in range(items):
            scale = scale_all[i : i + 1]
            pick = (slot_all[i : i + 1] == slot_ids).astype(BF16)
            own = projected[q * pair : (q + 1) * pair, i * tokens : (i + 1) * tokens]
            hidden = tn_dot(hidden_refs[i][q, 0], pick)
            grad = nt_dot(pick, (scale * own).astype(BF16))
            combine = jnp.sum(hidden * own, axis=0, keepdims=True)
            high = combine.astype(BF16).astype(F32)
            partial = jnp.concatenate([high, combine - high], axis=1)
            grad_refs[i][q] = jnp.where(slot_rows == slots - top_k, partial, grad).astype(BF16)
            scatter = (scale * hidden).astype(BF16)
            for half in range(2):
                at = pl.ds(pl.multiple_of(e * block, block), block)
                terms[half, at, i * tokens : (i + 1) * tokens] = scatter[half * block : (half + 1) * block]

    @pl.when(step == pl.num_programs(0) - 1)
    def _():
        height = terms.shape[1]
        row = lax.broadcasted_iota(jnp.int32, (height, height), 0)
        col = lax.broadcasted_iota(jnp.int32, (8, height), 1)
        shift = block.bit_length() - 1
        to = (jnp.bitwise_and(col, block - 1) * experts + jnp.right_shift(col, shift))[0:1]
        order = (row == to).astype(BF16)
        for half in range(2):
            scatter_ref[half] = jnp.dot(order, terms[half], preferred_element_type=F32).astype(BF16)


def project(index, items, weights, hidden, top_k, group=2):
    experts, sources, slots, pair = hidden[0].shape
    width = weights.shape[2]
    pieces = [piece for rows, _, _ in items for piece in rows]
    sizes = [p.shape[0] for p in pieces]
    count = sum(sizes)
    block = pair // 2
    return pl.pallas_call(
        functools.partial(project_kernel, top_k, sizes, len(items)),
        grid_spec=pltpu.PrefetchScalarGridSpec(
            num_scalar_prefetch=1,
            grid=(experts // group,),
            in_specs=[pl.BlockSpec(memory_space=pl.ANY)] * len(sizes)
            + [pl.BlockSpec((1, group * block, width), lambda e, idx, c=c: (c, e, 0)) for c in range(2)]
            + [
                pl.BlockSpec((group, 1, slots, pair), lambda e, idx, k=k: (e, idx[k], 0, 0))
                for _, _, k in items
            ],
            out_specs=[pl.BlockSpec((group, slots, pair), lambda e, idx: (e, 0, 0))] * len(items)
            + [pl.BlockSpec((2, experts * block, count), lambda e, idx: (0, 0, 0))],
            scratch_shapes=[
                pltpu.VMEM((count, width), BF16),
                pltpu.VMEM((group * pair, width), BF16),
                pltpu.VMEM((2, experts * block, count), BF16),
                pltpu.VMEM((experts, 8, block), F32),
                pltpu.VMEM((experts, 8, block), F32),
                pltpu.SemaphoreType.DMA((len(sizes),)),
            ],
        ),
        out_shape=[jax.ShapeDtypeStruct((experts, slots, pair), BF16)] * len(items)
        + [jax.ShapeDtypeStruct((2, experts * block, count), BF16)],
        compiler_params=pltpu.CompilerParams(vmem_limit_bytes=VMEM_BYTES),
        cost_estimate=pl.CostEstimate(
            flops=4 * count * width * experts * pair,
            bytes_accessed=2 * (count * width + weights.size),
            transcendentals=0,
        ),
    )(index, *pieces, weights, weights, *[hidden[m] for _, m, _ in items])


def fill_rows(pieces, rows):
    at = 0
    for piece in pieces:
        size = piece.shape[0]
        rows[at : at + size, :] = piece[...]
        at += size


def sum_terms(scatters, rows, half):
    total, at = None, 0
    for scatter in scatters:
        count = scatter.shape[2]
        term = jnp.dot(scatter[half], rows[at : at + count, :], preferred_element_type=F32)
        total = term if total is None else total + term
        at += count
    return total


def half_grad_kernel(terms, arrivals, last, *refs):
    scatters, arrived = refs[:terms], refs[terms : terms + arrivals]
    pieces, (out_ref, rows) = refs[terms + arrivals : -2], refs[-2:]
    fill_rows(pieces, rows)
    total = sum_terms(scatters, rows, 0)
    for array in arrived:
        total += array[...].astype(F32)
    if not last:
        out_ref[...] = total.astype(BF16)
        return
    out_ref[...] = total.reshape(out_ref.shape)


def half_grad(half, scatters, pieces, arrived, experts, tile, last):
    height = scatters[0].shape[1]
    width = pieces[0].shape[1]
    count = sum(p.shape[0] for p in pieces)
    in_specs = [pl.BlockSpec((1,) + a.shape[1:], lambda i: (half, 0, 0)) for a in scatters]
    in_specs += [pl.BlockSpec((height, tile), lambda i: (0, i)) for _ in arrived]
    in_specs += [pl.BlockSpec((p.shape[0], tile), lambda i: (0, i)) for p in pieces]
    scratch = [pltpu.VMEM((count, tile), BF16)]
    if last:
        out_spec = pl.BlockSpec((height // experts, experts, tile), lambda i: (0, 0, i))
        out_shape = jax.ShapeDtypeStruct((height // experts, experts, width), F32)
    else:
        out_spec = pl.BlockSpec((height, tile), lambda i: (0, i))
        out_shape = jax.ShapeDtypeStruct((height, width), BF16)
    return pl.pallas_call(
        functools.partial(half_grad_kernel, len(scatters), len(arrived), last),
        grid=(width // tile,),
        in_specs=in_specs,
        out_specs=out_spec,
        out_shape=out_shape,
        scratch_shapes=scratch,
        compiler_params=pltpu.CompilerParams(vmem_limit_bytes=VMEM_BYTES),
        cost_estimate=pl.CostEstimate(
            flops=2 * height * count * width,
            bytes_accessed=2 * count * (width + height) + 4 * height * width,
            transcendentals=0,
        ),
    )(*scatters, *arrived, *pieces)


def place_kernel(top_k, idx_ref, *refs):
    count = len(refs) - 3
    block = refs[0].shape[2] // 2
    pieces, (out_ref, sum_ref, out_sems) = refs[:count], refs[count:]
    experts, slots, pair = pieces[0].shape
    rows = 16
    slabs = count // 4
    stores = []
    for i in range(count):
        for half in range(2):
            column = pl.multiple_of(idx_ref[slabs + 2 * (i % 4) + half] * block, block)
            to = out_ref.at[idx_ref[i // 4], :, :, pl.ds(column, block)]
            part = pieces[i].at[:, :, half * block : (half + 1) * block]
            stores.append(pltpu.make_async_copy(part, to, out_sems.at[2 * i + half]))
    for copy in stores:
        copy.start()
    for k in range(slabs):
        for e in range(experts):
            total = sum(pieces[4 * k + m][e, slots - rows :].astype(F32) for m in range(4))
            row = total[rows - top_k : rows - top_k + 1]
            sum_ref[k * experts + e : k * experts + e + 1] = row[:, : pair // 2] + row[:, pair // 2 :]
    for copy in stores:
        copy.wait()


def place(index, pieces, top_k):
    experts, slots, pair = pieces[0].shape
    slabs = len(pieces) // 4
    return pl.pallas_call(
        functools.partial(place_kernel, top_k),
        grid_spec=pltpu.PrefetchScalarGridSpec(
            num_scalar_prefetch=1,
            grid=(1,),
            in_specs=[pl.BlockSpec((experts, slots, pair), lambda i, idx: (0, 0, 0))] * len(pieces),
            out_specs=[
                pl.BlockSpec(memory_space=pl.ANY),
                pl.BlockSpec((slabs * experts, pair // 2), lambda i, idx: (0, 0)),
            ],
            scratch_shapes=[
                pltpu.SemaphoreType.DMA((2 * len(pieces),)),
            ],
        ),
        out_shape=[
            jax.ShapeDtypeStruct((slabs, experts, slots, 4 * pair), BF16),
            jax.ShapeDtypeStruct((slabs * experts, pair // 2), F32),
        ],
        compiler_params=pltpu.CompilerParams(vmem_limit_bytes=48 * 2**20),
        cost_estimate=pl.CostEstimate(
            flops=0, bytes_accessed=4 * len(pieces) * experts * slots * pair, transcendentals=0
        ),
    )(index, *pieces)


def on_device_tokens(grad_out, routes, affinity, saved_hidden, down_proj):
    reps, sources = lax.axis_size("rep"), lax.axis_size("exp")
    block, experts, width = down_proj.shape
    tokens, top_k = routes.shape
    most, hidden_units = saved_hidden.shape[3:]
    pair = 2 * block
    me = lax.axis_index("exp")
    rep = lax.axis_index("rep")
    chip, core = lax.div(rep, 2), lax.rem(rep, 2)
    blocks = [2 * jnp.bitwise_xor(chip, m) + jnp.bitwise_xor(core, c) for m in range(4) for c in range(2)]

    def across(array, bits):
        return lax.ppermute(array, "rep", [(i, i ^ bits) for i in range(reps)])

    def around(array, shift):
        return lax.ppermute(array, "exp", [(i, (i + shift) % sources) for i in range(sources)])

    totals = jnp.sum(affinity, axis=-1, keepdims=True)
    shares = affinity / totals
    route_weight = (ROUTE_SCALE * shares).astype(BF16)
    meta = jnp.concatenate([routes.astype(BF16).T, route_weight.T], axis=1)
    fence = lax.optimization_barrier

    slabs = [lax.rem(me - step + sources, sources) for step in range(sources)]
    index = jnp.stack(slabs + [me * experts]).astype(jnp.int32)

    def kernel(items):
        *grads, scatter = project(index, items, weights, hidden, top_k)
        return grads, scatter

    def send_back(grads, chip_of):
        return [across(g, 2 * m) if m else g for g, m in zip(grads, chip_of)]

    x0, y0, next1 = across(grad_out, 2), across(grad_out, 4), around(grad_out, 1)
    held = jnp.transpose(saved_hidden.reshape(experts, sources, most, 8, block), (3, 0, 1, 2, 4))
    held = fence(held)
    held = [lax.dynamic_index_in_dim(held, b, axis=0, keepdims=False) for b in blocks]
    own_weight = jnp.transpose(down_proj, (1, 0, 2)).reshape(experts * block, width)
    last_meta, held, own_weight = fence((meta, held, own_weight))
    metas = [meta, around(meta, 1), around(meta, 2), around(last_meta, 3)]
    metas, x0, y0, next1, held, own_weight = fence((metas, x0, y0, next1, held, own_weight))

    xy0, x1, next2 = across(x0, 4), across(next1, 2), around(next1, 1)
    own3 = around(fence((grad_out, next2))[0], -1)
    partner_weight = across(own_weight, 1)
    metas = jnp.stack([metas[(sources - 1 - i) % sources] for i in range(2 * sources - 1)])
    metas = lax.dynamic_slice_in_dim(metas, sources - 1 - me, sources, axis=0)
    blank = jnp.zeros((experts, sources, SLOT_PAD - most - top_k, pair), BF16)
    metas = jnp.broadcast_to(metas[None], (experts, sources, top_k, pair))
    hidden = []
    for m in range(4):
        piece = jnp.concatenate([held[2 * m], held[2 * m + 1]], axis=3)
        hidden.append(jnp.concatenate([piece, blank, metas], axis=2))
    diagonal = across(hidden[3], 6)
    hidden = [
        hidden[0],
        across(fence((hidden[1], x1, diagonal))[0], 2),
        across(fence((hidden[2], xy0, diagonal))[0], 4),
        diagonal,
    ]
    weights = jnp.stack([own_weight, partner_weight])
    hidden, xy0, x1, next2, own3, weights, x0, y0, next1 = fence(
        (hidden, xy0, x1, next2, own3, weights, x0, y0, next1)
    )

    y1, x2, x3 = across(next1, 4), across(next2, 2), around(x0, -1)
    grads0, scatter0 = kernel([([grad_out], 0, 0), ([x0], 1, 0), ([y0], 2, 0), ([xy0], 3, 0)])
    y1, x2, x3, grads0, scatter0, y0, xy0, next2, x1 = fence(
        (y1, x2, x3, grads0, scatter0, y0, xy0, next2, x1)
    )

    xy1, y2, y3 = across(y1, 2), across(next2, 4), around(y0, -1)
    grads1, scatter1 = kernel(
        [([next1], 0, 1), ([x1], 1, 1), ([y1], 2, 1), ([next2], 0, 2), ([x2], 1, 2), ([x3], 1, 3)]
    )
    xy1, y2, y3, grads1, scatter1, xy0, x2, grads0 = fence((xy1, y2, y3, grads1, scatter1, xy0, x2, grads0))

    xy2, xy3 = across(x2, 4), around(xy0, -1)
    returned0 = send_back(grads0, (0, 1, 2, 3))
    returned1 = send_back(grads1, (0, 1, 2, 0, 1, 1))
    grads2, scatter2 = kernel([([xy1], 3, 1), ([y2], 2, 2), ([own3], 0, 3), ([y3], 2, 3)])
    first = [grad_out, x0, y0, xy0, next1, x1, y1, next2, x2, x3]
    mine, other = 0, 1
    partner = half_grad(other, [scatter0, scatter1], first, [], experts, 896, False)
    xy2, xy3, returned0, returned1, grads2, scatter2, partner = fence(
        (xy2, xy3, returned0, returned1, grads2, scatter2, partner)
    )

    partner = across(partner, 1)
    returned2 = send_back(grads2, (3, 2, 0, 2))
    grads3, scatter3 = kernel([([xy2], 3, 2), ([xy3], 3, 3)])
    late = [xy1, y2, own3, y3, xy2, xy3]
    later = half_grad(other, [scatter2, scatter3], late, [], experts, 896, False)
    partner, returned2, later, grads3, scatter3 = fence((partner, returned2, later, grads3, scatter3))
    later = across(later, 1)
    returned3 = send_back(grads3, (3, 3))
    returned = [
        *returned0,
        *returned1[:3],
        returned2[0],
        returned1[3],
        returned1[4],
        returned2[1],
        returned3[0],
        returned2[2],
        returned1[5],
        returned2[3],
        returned3[1],
    ]
    placed, combine = place(jnp.stack(slabs + blocks).astype(jnp.int32), returned, top_k)
    combine = combine.reshape(sources, experts, tokens)
    combines = [combine[0], around(combine[1], -1), around(combine[2], -2), around(combine[3], 1)]
    route_grad = 0.0
    expert_ids = jnp.arange(experts, dtype=routes.dtype)
    for step in range(sources):
        ids = lax.rem(me + step, sources) * experts + expert_ids
        named = routes.T[:, None, :] == ids[None, :, None]
        route_grad += jnp.sum(jnp.where(named, combines[step][None], 0.0), axis=1)
    hidden_grad = jnp.transpose(placed[:, :, :most], (1, 0, 2, 3)).reshape(saved_hidden.shape)
    route_grad = ROUTE_SCALE * route_grad.T
    affinity_grad = (route_grad - jnp.sum(route_grad * shares, axis=-1, keepdims=True)) / totals
    scatters = [scatter0, scatter1, scatter2, scatter3]
    down_grad = half_grad(mine, scatters, first + late, [partner, later], experts, 896, True)
    return (affinity_grad, hidden_grad, down_grad)


def on_device(grad_out, routes, affinity, saved_hidden, down_proj):
    reps, sources = lax.axis_size("rep"), lax.axis_size("exp")
    block, experts, width = down_proj.shape
    tokens, top_k = routes.shape
    most = saved_hidden.shape[3]
    fits = block == 128 and tokens == 128 and width % 3584 == 0 and reps == 8 and 8 % experts == 0
    fits = fits and sources == 4 and most + top_k <= SLOT_PAD and top_k <= 8
    if fits and sources * tokens <= 2 * block * experts:
        return on_device_tokens(grad_out, routes, affinity, saved_hidden, down_proj)
    return on_device_weights(grad_out, routes, affinity, saved_hidden, down_proj)


def solution(mesh):
    return jax.shard_map(
        on_device,
        mesh=mesh,
        in_specs=(
            P(("rep", "exp"), None),
            P(("rep", "exp"), None),
            P(("rep", "exp"), None),
            P("rep", "exp", None, None, None),
            P("rep", "exp", None),
        ),
        out_specs=(
            P(("rep", "exp"), None),
            P("rep", "exp", None, None, None),
            P("rep", "exp", None),
        ),
        check_vma=False,
    )
```

```python
import functools
import jax
import jax.numpy as jnp
from jax import lax
from jax.experimental import pallas as pl
from jax.experimental.pallas import tpu as pltpu
from jax.sharding import PartitionSpec as P

ROUTE_SCALE = 2.5


def pack_routes(grad_rows, route_ids, route_weight, expert_count, most):
    expert_ids = jnp.arange(expert_count, dtype=jnp.int32)
    naming = jnp.sum((route_ids[:, :, None] == expert_ids[None, None, :]).astype(jnp.int32), axis=1)
    before = jnp.cumsum(naming, axis=0) - naming
    slot_ids = jnp.take_along_axis(before, route_ids, axis=1)
    placed = (route_ids * most + slot_ids).reshape(-1)
    token_ids = jnp.repeat(jnp.arange(grad_rows.shape[0], dtype=jnp.int32), route_ids.shape[1])
    source = jnp.zeros((expert_count * most,), jnp.int32).at[placed].set(token_ids)
    filled = jnp.zeros((expert_count * most,), jnp.int32).at[placed].set(1)
    weights = (
        jnp.zeros((expert_count * most,), route_weight.dtype)
        .at[placed]
        .set(route_weight.reshape(-1))
    )
    fetched = jnp.take(grad_rows, source, axis=0)
    packed = jnp.where(filled[:, None] > 0, fetched, jnp.zeros_like(fetched))
    return (packed, weights, placed)


def on_device_weights(grad_out, routes, affinity, saved_hidden, down_proj):
    exp_devices = lax.axis_size("exp")
    local_experts = down_proj.shape[1]
    expert_count = exp_devices * local_experts
    most = saved_hidden.shape[3]
    width = grad_out.shape[1]
    hidden_units = saved_hidden.shape[4]
    row_count = exp_devices * most
    totals = jnp.sum(affinity, axis=-1, keepdims=True)
    shares = affinity / totals
    route_weight = (ROUTE_SCALE * shares).astype(jnp.bfloat16)
    packed, weights, placed = pack_routes(grad_out, routes, route_weight, expert_count, most)
    outgoing = packed.reshape(exp_devices, local_experts, 1, most, width)
    outgoing_weight = weights.reshape(exp_devices, local_experts, 1, most)
    received, received_weight = (
        lax.all_to_all(outgoing, "exp", split_axis=0, concat_axis=2, tiled=True),
        lax.all_to_all(outgoing_weight, "exp", split_axis=0, concat_axis=2, tiled=True),
    )
    received = received.reshape(local_experts, row_count, width)
    row_scale = received_weight.reshape(local_experts, row_count).astype(jnp.float32)
    hidden = saved_hidden.reshape(local_experts, row_count, hidden_units)
    gathered = lax.all_gather(down_proj, "rep", axis=0, tiled=True)
    projected = jnp.einsum("erd,hed->erh", received, gathered, preferred_element_type=jnp.float32)
    hidden_grad = (row_scale[:, :, None] * projected).astype(jnp.bfloat16)
    combine_grad = ROUTE_SCALE * jnp.sum(hidden.astype(jnp.float32) * projected, axis=-1)
    scaled = (row_scale[:, :, None] * received.astype(jnp.float32)).astype(jnp.bfloat16)
    grad_term = jnp.einsum("erh,erd->hed", hidden, scaled, preferred_element_type=jnp.float32)
    down_grad = lax.psum_scatter(
        grad_term.astype(jnp.bfloat16), "rep", scatter_dimension=0, tiled=True
    ).astype(jnp.float32)
    returned = lax.all_to_all(
        combine_grad.reshape(local_experts, exp_devices, most),
        "exp",
        split_axis=1,
        concat_axis=0,
        tiled=True,
    )
    route_grad = jnp.take(returned.reshape(-1), placed).reshape(routes.shape)
    affinity_grad = (route_grad - jnp.sum(route_grad * shares, axis=-1, keepdims=True)) / totals
    return (affinity_grad, hidden_grad.reshape(saved_hidden.shape), down_grad)


SLOT_PAD = 64
F32 = jnp.float32
BF16 = jnp.bfloat16
VMEM_BYTES = 30 * 2**20


def nt_dot(a, b):
    return lax.dot_general(a, b, (((1,), (1,)), ((), ())), preferred_element_type=F32)


def tn_dot(a, b):
    return lax.dot_general(a, b, (((0,), (0,)), ((), ())), preferred_element_type=F32)


def project_kernel(top_k, sizes, items, idx_ref, *refs):
    parts = len(sizes)
    pieces, weight_refs = refs[:parts], refs[parts : parts + 2]
    hidden_refs = refs[parts + 2 : parts + 2 + items]
    grad_refs = refs[parts + 2 + items : parts + 2 + 2 * items]
    scatter_ref, rows, weight, terms, slot_ref, scale_ref, sems = refs[parts + 2 + 2 * items :]
    step = pl.program_id(0)
    group, slots, pair = grad_refs[0].shape
    block = pair // 2
    tokens = rows.shape[0] // items
    experts = slot_ref.shape[0]

    @pl.when(step == 0)
    def _():
        copies, at = [], 0
        for i, size in enumerate(sizes):
            copies.append(pltpu.make_async_copy(pieces[i], rows.at[at : at + size], sems.at[i]))
            at += size
        for copy in copies:
            copy.start()
        metas = [hidden_refs[i][0, 0][slots - 8 :].astype(F32)[8 - top_k :] for i in range(items)]
        fill = jnp.full((8 - items, tokens), -1.0, F32)
        routes = [jnp.concatenate([m[k : k + 1, :tokens] for m in metas] + [fill], axis=0) for k in range(top_k)]
        weights = [jnp.concatenate([m[k : k + 1, tokens:] for m in metas] + [fill], axis=0) for k in range(top_k)]
        earlier = (
            lax.broadcasted_iota(jnp.int32, (tokens, tokens), 0)
            < lax.broadcasted_iota(jnp.int32, (tokens, tokens), 1)
        ).astype(BF16)
        every = []
        for e in range(experts):
            expert = (idx_ref[4] + e).astype(F32)
            named = jnp.zeros((8, tokens), F32)
            scale = jnp.zeros((8, tokens), F32)
            for k in range(top_k):
                hit = routes[k] == expert
                named = jnp.where(hit, 1.0, named)
                scale = jnp.where(hit, weights[k], scale)
            scale_ref[e] = scale
            every.append(named)
        named = jnp.concatenate(every, axis=0)
        before = jnp.dot(named.astype(BF16), earlier, preferred_element_type=F32)
        slot = jnp.where(named > 0, before, -1.0)
        for e in range(experts):
            slot_ref[e] = slot[e * 8 : (e + 1) * 8]
        for copy in copies:
            copy.wait()

    for q in range(group):
        for c in range(2):
            at = q * pair + c * block
            weight[at : at + block, :] = weight_refs[c][0, q * block : (q + 1) * block]
    projected = nt_dot(weight[...], rows[...])
    slot_ids = lax.broadcasted_iota(jnp.int32, (slots, tokens), 0).astype(F32)
    slot_rows = lax.broadcasted_iota(jnp.int32, (slots, pair), 0)
    for q in range(group):
        e = step * group + q
        slot_all, scale_all = slot_ref[e], scale_ref[e]
        for i in range(items):
            scale = scale_all[i : i + 1]
            pick = (slot_all[i : i + 1] == slot_ids).astype(BF16)
            own = projected[q * pair : (q + 1) * pair, i * tokens : (i + 1) * tokens]
            hidden = tn_dot(hidden_refs[i][q, 0], pick)
            grad = nt_dot(pick, (scale * own).astype(BF16))
            combine = jnp.sum(hidden * own, axis=0, keepdims=True)
            high = combine.astype(BF16).astype(F32)
            partial = jnp.concatenate([high, combine - high], axis=1)
            grad_refs[i][q] = jnp.where(slot_rows == slots - top_k, partial, grad).astype(BF16)
            scatter = (scale * hidden).astype(BF16)
            for half in range(2):
                at = pl.ds(pl.multiple_of(e * block, block), block)
                terms[half, at, i * tokens : (i + 1) * tokens] = scatter[half * block : (half + 1) * block]

    @pl.when(step == pl.num_programs(0) - 1)
    def _():
        height = terms.shape[1]
        row = lax.broadcasted_iota(jnp.int32, (height, height), 0)
        col = lax.broadcasted_iota(jnp.int32, (8, height), 1)
        shift = block.bit_length() - 1
        to = (jnp.bitwise_and(col, block - 1) * experts + jnp.right_shift(col, shift))[0:1]
        order = (row == to).astype(BF16)
        for half in range(2):
            scatter_ref[half] = jnp.dot(order, terms[half], preferred_element_type=F32).astype(BF16)


def project(index, items, weights, hidden, top_k, group=2):
    experts, sources, slots, pair = hidden[0].shape
    width = weights.shape[2]
    pieces = [piece for rows, _, _ in items for piece in rows]
    sizes = [p.shape[0] for p in pieces]
    count = sum(sizes)
    block = pair // 2
    return pl.pallas_call(
        functools.partial(project_kernel, top_k, sizes, len(items)),
        grid_spec=pltpu.PrefetchScalarGridSpec(
            num_scalar_prefetch=1,
            grid=(experts // group,),
            in_specs=[pl.BlockSpec(memory_space=pl.ANY)] * len(sizes)
            + [pl.BlockSpec((1, group * block, width), lambda e, idx, c=c: (c, e, 0)) for c in range(2)]
            + [
                pl.BlockSpec((group, 1, slots, pair), lambda e, idx, k=k: (e, idx[k], 0, 0))
                for _, _, k in items
            ],
            out_specs=[pl.BlockSpec((group, slots, pair), lambda e, idx: (e, 0, 0))] * len(items)
            + [pl.BlockSpec((2, experts * block, count), lambda e, idx: (0, 0, 0))],
            scratch_shapes=[
                pltpu.VMEM((count, width), BF16),
                pltpu.VMEM((group * pair, width), BF16),
                pltpu.VMEM((2, experts * block, count), BF16),
                pltpu.VMEM((experts, 8, block), F32),
                pltpu.VMEM((experts, 8, block), F32),
                pltpu.SemaphoreType.DMA((len(sizes),)),
            ],
        ),
        out_shape=[jax.ShapeDtypeStruct((experts, slots, pair), BF16)] * len(items)
        + [jax.ShapeDtypeStruct((2, experts * block, count), BF16)],
        compiler_params=pltpu.CompilerParams(vmem_limit_bytes=VMEM_BYTES),
        cost_estimate=pl.CostEstimate(
            flops=4 * count * width * experts * pair,
            bytes_accessed=2 * (count * width + weights.size),
            transcendentals=0,
        ),
    )(index, *pieces, weights, weights, *[hidden[m] for _, m, _ in items])


def fill_rows(pieces, rows):
    at = 0
    for piece in pieces:
        size = piece.shape[0]
        rows[at : at + size, :] = piece[...]
        at += size


def sum_terms(scatters, rows, half):
    total, at = None, 0
    for scatter in scatters:
        count = scatter.shape[2]
        term = jnp.dot(scatter[half], rows[at : at + count, :], preferred_element_type=F32)
        total = term if total is None else total + term
        at += count
    return total


def half_grad_kernel(terms, arrivals, last, *refs):
    scatters, arrived = refs[:terms], refs[terms : terms + arrivals]
    pieces, (out_ref, rows) = refs[terms + arrivals : -2], refs[-2:]
    fill_rows(pieces, rows)
    total = sum_terms(scatters, rows, 0)
    for array in arrived:
        total += array[...].astype(F32)
    if not last:
        out_ref[...] = total.astype(BF16)
        return
    out_ref[...] = total.reshape(out_ref.shape)


def half_grad(half, scatters, pieces, arrived, experts, tile, last):
    height = scatters[0].shape[1]
    width = pieces[0].shape[1]
    count = sum(p.shape[0] for p in pieces)
    in_specs = [pl.BlockSpec((1,) + a.shape[1:], lambda i: (half, 0, 0)) for a in scatters]
    in_specs += [pl.BlockSpec((height, tile), lambda i: (0, i)) for _ in arrived]
    in_specs += [pl.BlockSpec((p.shape[0], tile), lambda i: (0, i)) for p in pieces]
    scratch = [pltpu.VMEM((count, tile), BF16)]
    if last:
        out_spec = pl.BlockSpec((height // experts, experts, tile), lambda i: (0, 0, i))
        out_shape = jax.ShapeDtypeStruct((height // experts, experts, width), F32)
    else:
        out_spec = pl.BlockSpec((height, tile), lambda i: (0, i))
        out_shape = jax.ShapeDtypeStruct((height, width), BF16)
    return pl.pallas_call(
        functools.partial(half_grad_kernel, len(scatters), len(arrived), last),
        grid=(width // tile,),
        in_specs=in_specs,
        out_specs=out_spec,
        out_shape=out_shape,
        scratch_shapes=scratch,
        compiler_params=pltpu.CompilerParams(vmem_limit_bytes=2 * VMEM_BYTES if last else VMEM_BYTES),
        cost_estimate=pl.CostEstimate(
            flops=2 * height * count * width,
            bytes_accessed=2 * count * (width + height) + 4 * height * width,
            transcendentals=0,
        ),
    )(*scatters, *arrived, *pieces)


def place_kernel(top_k, idx_ref, *refs):
    count = len(refs) - 3
    block = refs[0].shape[2] // 2
    pieces, (out_ref, sum_ref, out_sems) = refs[:count], refs[count:]
    experts, slots, pair = pieces[0].shape
    rows = 16
    slabs = count // 4
    stores = []
    for i in range(count):
        for half in range(2):
            column = pl.multiple_of(idx_ref[slabs + 2 * (i % 4) + half] * block, block)
            to = out_ref.at[idx_ref[i // 4], :, :, pl.ds(column, block)]
            part = pieces[i].at[:, :, half * block : (half + 1) * block]
            stores.append(pltpu.make_async_copy(part, to, out_sems.at[2 * i + half]))
    for copy in stores:
        copy.start()
    for k in range(slabs):
        for e in range(experts):
            total = sum(pieces[4 * k + m][e, slots - rows :].astype(F32) for m in range(4))
            row = total[rows - top_k : rows - top_k + 1]
            sum_ref[k * experts + e : k * experts + e + 1] = row[:, : pair // 2] + row[:, pair // 2 :]
    for copy in stores:
        copy.wait()


def place(index, pieces, top_k):
    experts, slots, pair = pieces[0].shape
    slabs = len(pieces) // 4
    return pl.pallas_call(
        functools.partial(place_kernel, top_k),
        grid_spec=pltpu.PrefetchScalarGridSpec(
            num_scalar_prefetch=1,
            grid=(1,),
            in_specs=[pl.BlockSpec((experts, slots, pair), lambda i, idx: (0, 0, 0))] * len(pieces),
            out_specs=[
                pl.BlockSpec(memory_space=pl.ANY),
                pl.BlockSpec((slabs * experts, pair // 2), lambda i, idx: (0, 0)),
            ],
            scratch_shapes=[
                pltpu.SemaphoreType.DMA((2 * len(pieces),)),
            ],
        ),
        out_shape=[
            jax.ShapeDtypeStruct((slabs, experts, slots, 4 * pair), BF16),
            jax.ShapeDtypeStruct((slabs * experts, pair // 2), F32),
        ],
        compiler_params=pltpu.CompilerParams(vmem_limit_bytes=61 * 2**20),
        cost_estimate=pl.CostEstimate(
            flops=0, bytes_accessed=4 * len(pieces) * experts * slots * pair, transcendentals=0
        ),
    )(index, *pieces)


def on_device_tokens(grad_out, routes, affinity, saved_hidden, down_proj):
    reps, sources = lax.axis_size("rep"), lax.axis_size("exp")
    block, experts, width = down_proj.shape
    tokens, top_k = routes.shape
    most, hidden_units = saved_hidden.shape[3:]
    pair = 2 * block
    me = lax.axis_index("exp")
    rep = lax.axis_index("rep")
    chip, core = lax.div(rep, 2), lax.rem(rep, 2)
    blocks = [2 * jnp.bitwise_xor(chip, m) + jnp.bitwise_xor(core, c) for m in range(4) for c in range(2)]

    def across(array, bits):
        return lax.ppermute(array, "rep", [(i, i ^ bits) for i in range(reps)])

    def around(array, shift):
        return lax.ppermute(array, "exp", [(i, (i + shift) % sources) for i in range(sources)])

    totals = jnp.sum(affinity, axis=-1, keepdims=True)
    shares = affinity / totals
    route_weight = (ROUTE_SCALE * shares).astype(BF16)
    meta = jnp.concatenate([routes.astype(BF16).T, route_weight.T], axis=1)
    fence = lax.optimization_barrier

    slabs = [lax.rem(me - step + sources, sources) for step in range(sources)]
    index = jnp.stack(slabs + [me * experts]).astype(jnp.int32)

    def kernel(items):
        *grads, scatter = project(index, items, weights, hidden, top_k)
        return grads, scatter

    def send_back(grads, chip_of):
        return [across(g, 2 * m) if m else g for g, m in zip(grads, chip_of)]

    x0, y0, next1 = across(grad_out, 2), across(grad_out, 4), around(grad_out, 1)
    held = jnp.transpose(saved_hidden.reshape(experts, sources, most, 8, block), (3, 0, 1, 2, 4))
    held = fence(held)
    held = [lax.dynamic_index_in_dim(held, b, axis=0, keepdims=False) for b in blocks]
    own_weight = jnp.transpose(down_proj, (1, 0, 2)).reshape(experts * block, width)
    last_meta, held, own_weight = fence((meta, held, own_weight))
    metas = [meta, around(meta, 1), around(meta, 2), around(last_meta, 3)]
    metas, x0, y0, next1, held, own_weight = fence((metas, x0, y0, next1, held, own_weight))

    xy0, x1, next2 = across(x0, 4), across(next1, 2), around(next1, 1)
    own3 = around(fence((grad_out, next2))[0], -1)
    partner_weight = across(own_weight, 1)
    metas = jnp.stack([metas[(sources - 1 - i) % sources] for i in range(2 * sources - 1)])
    metas = lax.dynamic_slice_in_dim(metas, sources - 1 - me, sources, axis=0)
    blank = jnp.zeros((experts, sources, SLOT_PAD - most - top_k, pair), BF16)
    metas = jnp.broadcast_to(metas[None], (experts, sources, top_k, pair))
    hidden = []
    for m in range(4):
        piece = jnp.concatenate([held[2 * m], held[2 * m + 1]], axis=3)
        hidden.append(jnp.concatenate([piece, blank, metas], axis=2))
    diagonal = across(hidden[3], 6)
    hidden = [
        hidden[0],
        across(fence((hidden[1], x1, diagonal))[0], 2),
        across(fence((hidden[2], xy0, diagonal))[0], 4),
        diagonal,
    ]
    weights = jnp.stack([own_weight, partner_weight])
    hidden, xy0, x1, next2, own3, weights, x0, y0, next1 = fence(
        (hidden, xy0, x1, next2, own3, weights, x0, y0, next1)
    )

    y1, x2, x3 = across(next1, 4), across(next2, 2), around(x0, -1)
    grads0, scatter0 = kernel([([grad_out], 0, 0), ([x0], 1, 0), ([y0], 2, 0), ([xy0], 3, 0)])
    y1, x2, x3, grads0, scatter0, y0, xy0, next2, x1 = fence(
        (y1, x2, x3, grads0, scatter0, y0, xy0, next2, x1)
    )

    xy1, y2, y3 = across(y1, 2), across(next2, 4), around(y0, -1)
    grads1, scatter1 = kernel(
        [([next1], 0, 1), ([x1], 1, 1), ([y1], 2, 1), ([next2], 0, 2), ([x2], 1, 2), ([x3], 1, 3)]
    )
    xy1, y2, y3, grads1, scatter1, xy0, x2, grads0 = fence((xy1, y2, y3, grads1, scatter1, xy0, x2, grads0))

    xy2, xy3 = across(x2, 4), around(xy0, -1)
    returned0 = send_back(grads0, (0, 1, 2, 3))
    returned1 = send_back(grads1, (0, 1, 2, 0, 1, 1))
    grads2, scatter2 = kernel([([xy1], 3, 1), ([y2], 2, 2), ([own3], 0, 3), ([y3], 2, 3)])
    first = [grad_out, x0, y0, xy0, next1, x1, y1, next2, x2, x3]
    mine, other = 0, 1
    partner = half_grad(other, [scatter0, scatter1], first, [], experts, 896, False)
    xy2, xy3, returned0, returned1, grads2, scatter2, partner = fence(
        (xy2, xy3, returned0, returned1, grads2, scatter2, partner)
    )

    partner = across(partner, 1)
    returned2 = send_back(grads2, (3, 2, 0, 2))
    grads3, scatter3 = kernel([([xy2], 3, 2), ([xy3], 3, 3)])
    late = [xy1, y2, own3, y3, xy2, xy3]
    later = half_grad(other, [scatter2, scatter3], late, [], experts, 896, False)
    partner, returned2, later, grads3, scatter3 = fence((partner, returned2, later, grads3, scatter3))
    later = across(later, 1)
    returned3 = send_back(grads3, (3, 3))
    returned = [
        *returned0,
        *returned1[:3],
        returned2[0],
        returned1[3],
        returned1[4],
        returned2[1],
        returned3[0],
        returned2[2],
        returned1[5],
        returned2[3],
        returned3[1],
    ]
    placed, combine = place(jnp.stack(slabs + blocks).astype(jnp.int32), returned, top_k)
    combine = combine.reshape(sources, experts, tokens)
    combines = [combine[0], around(combine[1], -1), around(combine[2], -2), around(combine[3], 1)]
    route_grad = 0.0
    expert_ids = jnp.arange(experts, dtype=routes.dtype)
    for step in range(sources):
        ids = lax.rem(me + step, sources) * experts + expert_ids
        named = routes.T[:, None, :] == ids[None, :, None]
        route_grad += jnp.sum(jnp.where(named, combines[step][None], 0.0), axis=1)
    hidden_grad = jnp.transpose(placed[:, :, :most], (1, 0, 2, 3)).reshape(saved_hidden.shape)
    route_grad = ROUTE_SCALE * route_grad.T
    affinity_grad = (route_grad - jnp.sum(route_grad * shares, axis=-1, keepdims=True)) / totals
    scatters = [scatter0, scatter1, scatter2, scatter3]
    down_grad = half_grad(mine, scatters, first + late, [partner, later], experts, 896, True)
    return (affinity_grad, hidden_grad, down_grad)


def on_device(grad_out, routes, affinity, saved_hidden, down_proj):
    reps, sources = lax.axis_size("rep"), lax.axis_size("exp")
    block, experts, width = down_proj.shape
    tokens, top_k = routes.shape
    most = saved_hidden.shape[3]
    fits = block == 128 and tokens == 128 and width % 3584 == 0 and reps == 8 and 8 % experts == 0
    fits = fits and sources == 4 and most + top_k <= SLOT_PAD and top_k <= 8
    if fits and sources * tokens <= 2 * block * experts:
        return on_device_tokens(grad_out, routes, affinity, saved_hidden, down_proj)
    return on_device_weights(grad_out, routes, affinity, saved_hidden, down_proj)


def solution(mesh):
    return jax.shard_map(
        on_device,
        mesh=mesh,
        in_specs=(
            P(("rep", "exp"), None),
            P(("rep", "exp"), None),
            P(("rep", "exp"), None),
            P("rep", "exp", None, None, None),
            P("rep", "exp", None),
        ),
        out_specs=(
            P(("rep", "exp"), None),
            P("rep", "exp", None, None, None),
            P("rep", "exp", None),
        ),
        check_vma=False,
    )
```

```python
import functools
import jax
import jax.numpy as jnp
from jax import lax
from jax.experimental import pallas as pl
from jax.experimental.pallas import tpu as pltpu
from jax.sharding import PartitionSpec as P

ROUTE_SCALE = 2.5


def pack_routes(grad_rows, route_ids, route_weight, expert_count, most):
    expert_ids = jnp.arange(expert_count, dtype=jnp.int32)
    naming = jnp.sum((route_ids[:, :, None] == expert_ids[None, None, :]).astype(jnp.int32), axis=1)
    before = jnp.cumsum(naming, axis=0) - naming
    slot_ids = jnp.take_along_axis(before, route_ids, axis=1)
    placed = (route_ids * most + slot_ids).reshape(-1)
    token_ids = jnp.repeat(jnp.arange(grad_rows.shape[0], dtype=jnp.int32), route_ids.shape[1])
    source = jnp.zeros((expert_count * most,), jnp.int32).at[placed].set(token_ids)
    filled = jnp.zeros((expert_count * most,), jnp.int32).at[placed].set(1)
    weights = (
        jnp.zeros((expert_count * most,), route_weight.dtype)
        .at[placed]
        .set(route_weight.reshape(-1))
    )
    fetched = jnp.take(grad_rows, source, axis=0)
    packed = jnp.where(filled[:, None] > 0, fetched, jnp.zeros_like(fetched))
    return (packed, weights, placed)


def on_device_weights(grad_out, routes, affinity, saved_hidden, down_proj):
    exp_devices = lax.axis_size("exp")
    local_experts = down_proj.shape[1]
    expert_count = exp_devices * local_experts
    most = saved_hidden.shape[3]
    width = grad_out.shape[1]
    hidden_units = saved_hidden.shape[4]
    row_count = exp_devices * most
    totals = jnp.sum(affinity, axis=-1, keepdims=True)
    shares = affinity / totals
    route_weight = (ROUTE_SCALE * shares).astype(jnp.bfloat16)
    packed, weights, placed = pack_routes(grad_out, routes, route_weight, expert_count, most)
    outgoing = packed.reshape(exp_devices, local_experts, 1, most, width)
    outgoing_weight = weights.reshape(exp_devices, local_experts, 1, most)
    received, received_weight = (
        lax.all_to_all(outgoing, "exp", split_axis=0, concat_axis=2, tiled=True),
        lax.all_to_all(outgoing_weight, "exp", split_axis=0, concat_axis=2, tiled=True),
    )
    received = received.reshape(local_experts, row_count, width)
    row_scale = received_weight.reshape(local_experts, row_count).astype(jnp.float32)
    hidden = saved_hidden.reshape(local_experts, row_count, hidden_units)
    gathered = lax.all_gather(down_proj, "rep", axis=0, tiled=True)
    projected = jnp.einsum("erd,hed->erh", received, gathered, preferred_element_type=jnp.float32)
    hidden_grad = (row_scale[:, :, None] * projected).astype(jnp.bfloat16)
    combine_grad = ROUTE_SCALE * jnp.sum(hidden.astype(jnp.float32) * projected, axis=-1)
    scaled = (row_scale[:, :, None] * received.astype(jnp.float32)).astype(jnp.bfloat16)
    grad_term = jnp.einsum("erh,erd->hed", hidden, scaled, preferred_element_type=jnp.float32)
    down_grad = lax.psum_scatter(
        grad_term.astype(jnp.bfloat16), "rep", scatter_dimension=0, tiled=True
    ).astype(jnp.float32)
    returned = lax.all_to_all(
        combine_grad.reshape(local_experts, exp_devices, most),
        "exp",
        split_axis=1,
        concat_axis=0,
        tiled=True,
    )
    route_grad = jnp.take(returned.reshape(-1), placed).reshape(routes.shape)
    affinity_grad = (route_grad - jnp.sum(route_grad * shares, axis=-1, keepdims=True)) / totals
    return (affinity_grad, hidden_grad.reshape(saved_hidden.shape), down_grad)


SLOT_PAD = 64
F32 = jnp.float32
BF16 = jnp.bfloat16
VMEM_BYTES = 30 * 2**20


def nt_dot(a, b):
    return lax.dot_general(a, b, (((1,), (1,)), ((), ())), preferred_element_type=F32)


def tn_dot(a, b):
    return lax.dot_general(a, b, (((0,), (0,)), ((), ())), preferred_element_type=F32)


def project_kernel(top_k, sizes, items, idx_ref, *refs):
    parts = len(sizes)
    pieces, weight_refs = refs[:parts], refs[parts : parts + 2]
    hidden_refs = refs[parts + 2 : parts + 2 + items]
    grad_refs = refs[parts + 2 + items : parts + 2 + 2 * items]
    scatter_ref, rows, weight, terms, slot_ref, scale_ref, sems = refs[parts + 2 + 2 * items :]
    step = pl.program_id(0)
    group, slots, pair = grad_refs[0].shape
    block = pair // 2
    tokens = rows.shape[0] // items
    experts = slot_ref.shape[0]

    @pl.when(step == 0)
    def _():
        copies, at = [], 0
        for i, size in enumerate(sizes):
            copies.append(pltpu.make_async_copy(pieces[i], rows.at[at : at + size], sems.at[i]))
            at += size
        for copy in copies:
            copy.start()
        metas = [hidden_refs[i][0, 0][slots - 8 :].astype(F32)[8 - top_k :] for i in range(items)]
        fill = jnp.full((8 - items, tokens), -1.0, F32)
        routes = [jnp.concatenate([m[k : k + 1, :tokens] for m in metas] + [fill], axis=0) for k in range(top_k)]
        weights = [jnp.concatenate([m[k : k + 1, tokens:] for m in metas] + [fill], axis=0) for k in range(top_k)]
        earlier = (
            lax.broadcasted_iota(jnp.int32, (tokens, tokens), 0)
            < lax.broadcasted_iota(jnp.int32, (tokens, tokens), 1)
        ).astype(BF16)
        every = []
        for e in range(experts):
            expert = (idx_ref[4] + e).astype(F32)
            named = jnp.zeros((8, tokens), F32)
            scale = jnp.zeros((8, tokens), F32)
            for k in range(top_k):
                hit = routes[k] == expert
                named = jnp.where(hit, 1.0, named)
                scale = jnp.where(hit, weights[k], scale)
            scale_ref[e] = scale
            every.append(named)
        named = jnp.concatenate(every, axis=0)
        before = jnp.dot(named.astype(BF16), earlier, preferred_element_type=F32)
        slot = jnp.where(named > 0, before, -1.0)
        for e in range(experts):
            slot_ref[e] = slot[e * 8 : (e + 1) * 8]
        for copy in copies:
            copy.wait()

    for q in range(group):
        for c in range(2):
            at = q * pair + c * block
            weight[at : at + block, :] = weight_refs[c][0, q * block : (q + 1) * block]
    projected = nt_dot(weight[...], rows[...])
    slot_ids = lax.broadcasted_iota(jnp.int32, (slots, tokens), 0).astype(F32)
    slot_rows = lax.broadcasted_iota(jnp.int32, (slots, pair), 0)
    for q in range(group):
        e = step * group + q
        slot_all, scale_all = slot_ref[e], scale_ref[e]
        for i in range(items):
            scale = scale_all[i : i + 1]
            pick = (slot_all[i : i + 1] == slot_ids).astype(BF16)
            own = projected[q * pair : (q + 1) * pair, i * tokens : (i + 1) * tokens]
            hidden = tn_dot(hidden_refs[i][q, 0], pick)
            grad = nt_dot(pick, (scale * own).astype(BF16))
            combine = jnp.sum(hidden * own, axis=0, keepdims=True)
            high = combine.astype(BF16).astype(F32)
            partial = jnp.concatenate([high, combine - high], axis=1)
            grad_refs[i][q] = jnp.where(slot_rows == slots - top_k, partial, grad).astype(BF16)
            scatter = (scale * hidden).astype(BF16)
            for half in range(2):
                at = pl.ds(pl.multiple_of(e * block, block), block)
                terms[half, at, i * tokens : (i + 1) * tokens] = scatter[half * block : (half + 1) * block]

    @pl.when(step == pl.num_programs(0) - 1)
    def _():
        height = terms.shape[1]
        row = lax.broadcasted_iota(jnp.int32, (height, height), 0)
        col = lax.broadcasted_iota(jnp.int32, (8, height), 1)
        shift = block.bit_length() - 1
        to = (jnp.bitwise_and(col, block - 1) * experts + jnp.right_shift(col, shift))[0:1]
        order = (row == to).astype(BF16)
        for half in range(2):
            scatter_ref[half] = jnp.dot(order, terms[half], preferred_element_type=F32).astype(BF16)


def project(index, items, weights, hidden, top_k, group=2):
    experts, sources, slots, pair = hidden[0].shape
    width = weights.shape[2]
    pieces = [piece for rows, _, _ in items for piece in rows]
    sizes = [p.shape[0] for p in pieces]
    count = sum(sizes)
    block = pair // 2
    return pl.pallas_call(
        functools.partial(project_kernel, top_k, sizes, len(items)),
        grid_spec=pltpu.PrefetchScalarGridSpec(
            num_scalar_prefetch=1,
            grid=(experts // group,),
            in_specs=[pl.BlockSpec(memory_space=pl.ANY)] * len(sizes)
            + [pl.BlockSpec((1, group * block, width), lambda e, idx, c=c: (c, e, 0)) for c in range(2)]
            + [
                pl.BlockSpec((group, 1, slots, pair), lambda e, idx, k=k: (e, idx[k], 0, 0))
                for _, _, k in items
            ],
            out_specs=[pl.BlockSpec((group, slots, pair), lambda e, idx: (e, 0, 0))] * len(items)
            + [pl.BlockSpec((2, experts * block, count), lambda e, idx: (0, 0, 0))],
            scratch_shapes=[
                pltpu.VMEM((count, width), BF16),
                pltpu.VMEM((group * pair, width), BF16),
                pltpu.VMEM((2, experts * block, count), BF16),
                pltpu.VMEM((experts, 8, block), F32),
                pltpu.VMEM((experts, 8, block), F32),
                pltpu.SemaphoreType.DMA((len(sizes),)),
            ],
        ),
        out_shape=[jax.ShapeDtypeStruct((experts, slots, pair), BF16)] * len(items)
        + [jax.ShapeDtypeStruct((2, experts * block, count), BF16)],
        compiler_params=pltpu.CompilerParams(vmem_limit_bytes=VMEM_BYTES),
        cost_estimate=pl.CostEstimate(
            flops=4 * count * width * experts * pair,
            bytes_accessed=2 * (count * width + weights.size),
            transcendentals=0,
        ),
    )(index, *pieces, weights, weights, *[hidden[m] for _, m, _ in items])


def fill_rows(pieces, rows):
    at = 0
    for piece in pieces:
        size = piece.shape[0]
        rows[at : at + size, :] = piece[...]
        at += size


def sum_terms(scatters, rows, half):
    total, at = None, 0
    for scatter in scatters:
        count = scatter.shape[2]
        term = jnp.dot(scatter[half], rows[at : at + count, :], preferred_element_type=F32)
        total = term if total is None else total + term
        at += count
    return total


def half_grad_kernel(terms, arrivals, last, *refs):
    scatters, arrived = refs[:terms], refs[terms : terms + arrivals]
    pieces, (out_ref, rows) = refs[terms + arrivals : -2], refs[-2:]
    fill_rows(pieces, rows)
    total = sum_terms(scatters, rows, 0)
    for array in arrived:
        total += array[...].astype(F32)
    if not last:
        out_ref[...] = total.astype(out_ref.dtype)
        return
    out_ref[...] = total.reshape(out_ref.shape)


def half_grad(half, scatters, pieces, arrived, experts, tile, last, dtype=BF16):
    height = scatters[0].shape[1]
    width = pieces[0].shape[1]
    count = sum(p.shape[0] for p in pieces)
    in_specs = [pl.BlockSpec((1,) + a.shape[1:], lambda i: (half, 0, 0)) for a in scatters]
    in_specs += [pl.BlockSpec((height, tile), lambda i: (0, i)) for _ in arrived]
    in_specs += [pl.BlockSpec((p.shape[0], tile), lambda i: (0, i)) for p in pieces]
    scratch = [pltpu.VMEM((count, tile), BF16)]
    if last:
        out_spec = pl.BlockSpec((height // experts, experts, tile), lambda i: (0, 0, i))
        out_shape = jax.ShapeDtypeStruct((height // experts, experts, width), F32)
    else:
        out_spec = pl.BlockSpec((height, tile), lambda i: (0, i))
        out_shape = jax.ShapeDtypeStruct((height, width), dtype)
    return pl.pallas_call(
        functools.partial(half_grad_kernel, len(scatters), len(arrived), last),
        grid=(width // tile,),
        in_specs=in_specs,
        out_specs=out_spec,
        out_shape=out_shape,
        scratch_shapes=scratch,
        compiler_params=pltpu.CompilerParams(vmem_limit_bytes=2 * VMEM_BYTES if last else VMEM_BYTES),
        cost_estimate=pl.CostEstimate(
            flops=2 * height * count * width,
            bytes_accessed=2 * count * (width + height) + 4 * height * width,
            transcendentals=0,
        ),
    )(*scatters, *arrived, *pieces)


def place_kernel(top_k, idx_ref, *refs):
    count = len(refs) - 3
    block = refs[0].shape[2] // 2
    pieces, (out_ref, sum_ref, out_sems) = refs[:count], refs[count:]
    experts, slots, pair = pieces[0].shape
    rows = 16
    slabs = count // 4
    stores = []
    for i in range(count):
        for half in range(2):
            column = pl.multiple_of(idx_ref[slabs + 2 * (i % 4) + half] * block, block)
            to = out_ref.at[idx_ref[i // 4], :, :, pl.ds(column, block)]
            part = pieces[i].at[:, :, half * block : (half + 1) * block]
            stores.append(pltpu.make_async_copy(part, to, out_sems.at[2 * i + half]))
    for copy in stores:
        copy.start()
    for k in range(slabs):
        for e in range(experts):
            total = sum(pieces[4 * k + m][e, slots - rows :].astype(F32) for m in range(4))
            row = total[rows - top_k : rows - top_k + 1]
            sum_ref[k * experts + e : k * experts + e + 1] = row[:, : pair // 2] + row[:, pair // 2 :]
    for copy in stores:
        copy.wait()


def place(index, pieces, top_k):
    experts, slots, pair = pieces[0].shape
    slabs = len(pieces) // 4
    return pl.pallas_call(
        functools.partial(place_kernel, top_k),
        grid_spec=pltpu.PrefetchScalarGridSpec(
            num_scalar_prefetch=1,
            grid=(1,),
            in_specs=[pl.BlockSpec((experts, slots, pair), lambda i, idx: (0, 0, 0))] * len(pieces),
            out_specs=[
                pl.BlockSpec(memory_space=pl.ANY),
                pl.BlockSpec((slabs * experts, pair // 2), lambda i, idx: (0, 0)),
            ],
            scratch_shapes=[
                pltpu.SemaphoreType.DMA((2 * len(pieces),)),
            ],
        ),
        out_shape=[
            jax.ShapeDtypeStruct((slabs, experts, slots, 4 * pair), BF16),
            jax.ShapeDtypeStruct((slabs * experts, pair // 2), F32),
        ],
        compiler_params=pltpu.CompilerParams(vmem_limit_bytes=61 * 2**20),
        cost_estimate=pl.CostEstimate(
            flops=0, bytes_accessed=4 * len(pieces) * experts * slots * pair, transcendentals=0
        ),
    )(index, *pieces)


def on_device_tokens(grad_out, routes, affinity, saved_hidden, down_proj):
    reps, sources = lax.axis_size("rep"), lax.axis_size("exp")
    block, experts, width = down_proj.shape
    tokens, top_k = routes.shape
    most, hidden_units = saved_hidden.shape[3:]
    pair = 2 * block
    me = lax.axis_index("exp")
    rep = lax.axis_index("rep")
    chip, core = lax.div(rep, 2), lax.rem(rep, 2)
    blocks = [2 * jnp.bitwise_xor(chip, m) + jnp.bitwise_xor(core, c) for m in range(4) for c in range(2)]

    def across(array, bits):
        return lax.ppermute(array, "rep", [(i, i ^ bits) for i in range(reps)])

    def around(array, shift):
        return lax.ppermute(array, "exp", [(i, (i + shift) % sources) for i in range(sources)])

    totals = jnp.sum(affinity, axis=-1, keepdims=True)
    shares = affinity / totals
    route_weight = (ROUTE_SCALE * shares).astype(BF16)
    meta = jnp.concatenate([routes.astype(BF16).T, route_weight.T], axis=1)
    fence = lax.optimization_barrier

    slabs = [lax.rem(me - step + sources, sources) for step in range(sources)]
    index = jnp.stack(slabs + [me * experts]).astype(jnp.int32)

    def kernel(items):
        *grads, scatter = project(index, items, weights, hidden, top_k)
        return grads, scatter

    def send_back(grads, chip_of):
        return [across(g, 2 * m) if m else g for g, m in zip(grads, chip_of)]

    x0, y0, next1 = across(grad_out, 2), across(grad_out, 4), around(grad_out, 1)
    held = jnp.transpose(saved_hidden.reshape(experts, sources, most, 8, block), (3, 0, 1, 2, 4))
    held = fence(held)
    held = [lax.dynamic_index_in_dim(held, b, axis=0, keepdims=False) for b in blocks]
    own_weight = jnp.transpose(down_proj, (1, 0, 2)).reshape(experts * block, width)
    last_meta, held, own_weight = fence((meta, held, own_weight))
    metas = [meta, around(meta, 1), around(meta, 2), around(last_meta, 3)]
    metas, x0, y0, next1, held, own_weight = fence((metas, x0, y0, next1, held, own_weight))

    xy0, x1, next2 = across(x0, 4), across(next1, 2), around(next1, 1)
    own3 = around(fence((grad_out, next2))[0], -1)
    partner_weight = across(own_weight, 1)
    metas = jnp.stack([metas[(sources - 1 - i) % sources] for i in range(2 * sources - 1)])
    metas = lax.dynamic_slice_in_dim(metas, sources - 1 - me, sources, axis=0)
    blank = jnp.zeros((experts, sources, SLOT_PAD - most - top_k, pair), BF16)
    metas = jnp.broadcast_to(metas[None], (experts, sources, top_k, pair))
    hidden = []
    for m in range(4):
        piece = jnp.concatenate([held[2 * m], held[2 * m + 1]], axis=3)
        hidden.append(jnp.concatenate([piece, blank, metas], axis=2))
    diagonal = across(hidden[3], 6)
    hidden = [
        hidden[0],
        across(fence((hidden[1], x1, diagonal))[0], 2),
        across(fence((hidden[2], xy0, diagonal))[0], 4),
        diagonal,
    ]
    weights = jnp.stack([own_weight, partner_weight])
    hidden, xy0, x1, next2, own3, weights, x0, y0, next1 = fence(
        (hidden, xy0, x1, next2, own3, weights, x0, y0, next1)
    )

    y1, x2, x3 = across(next1, 4), across(next2, 2), around(x0, -1)
    grads0, scatter0 = kernel([([grad_out], 0, 0), ([x0], 1, 0), ([y0], 2, 0), ([xy0], 3, 0)])
    y1, x2, x3, grads0, scatter0, y0, xy0, next2, x1 = fence(
        (y1, x2, x3, grads0, scatter0, y0, xy0, next2, x1)
    )

    xy1, y2, y3 = across(y1, 2), across(next2, 4), around(y0, -1)
    grads1, scatter1 = kernel(
        [([next1], 0, 1), ([x1], 1, 1), ([y1], 2, 1), ([next2], 0, 2), ([x2], 1, 2), ([x3], 1, 3)]
    )
    xy1, y2, y3, grads1, scatter1, xy0, x2, grads0 = fence((xy1, y2, y3, grads1, scatter1, xy0, x2, grads0))

    xy2, xy3 = across(x2, 4), around(xy0, -1)
    returned0 = send_back(grads0, (0, 1, 2, 3))
    returned1 = send_back(grads1, (0, 1, 2, 0, 1, 1))
    grads2, scatter2 = kernel([([xy1], 3, 1), ([y2], 2, 2), ([own3], 0, 3), ([y3], 2, 3)])
    first = [grad_out, x0, y0, xy0, next1, x1, y1, next2, x2, x3]
    mine, other = 0, 1
    xy2, xy3, returned0, returned1, grads2, scatter2 = fence(
        (xy2, xy3, returned0, returned1, grads2, scatter2)
    )

    returned2 = send_back(grads2, (3, 2, 0, 2))
    grads3, scatter3 = kernel([([xy2], 3, 2), ([xy3], 3, 3)])
    late = [xy1, y2, own3, y3, xy2, xy3]
    scatters = [scatter0, scatter1, scatter2, scatter3]
    later = half_grad(other, scatters, first + late, [], experts, 896, False)
    returned2, later, grads3, scatter0 = fence((returned2, later, grads3, scatter0))
    early = half_grad(mine, [scatter0, scatter1], first, [], experts, 896, False, F32)
    later = across(later, 1)
    returned3 = send_back(grads3, (3, 3))
    returned3, early = fence((returned3, early))
    returned = [
        *returned0,
        *returned1[:3],
        returned2[0],
        returned1[3],
        returned1[4],
        returned2[1],
        returned3[0],
        returned2[2],
        returned1[5],
        returned2[3],
        returned3[1],
    ]
    placed, combine = place(jnp.stack(slabs + blocks).astype(jnp.int32), returned, top_k)
    combine = combine.reshape(sources, experts, tokens)
    combines = [combine[0], around(combine[1], -1), around(combine[2], -2), around(combine[3], 1)]
    route_grad = 0.0
    expert_ids = jnp.arange(experts, dtype=routes.dtype)
    for step in range(sources):
        ids = lax.rem(me + step, sources) * experts + expert_ids
        named = routes.T[:, None, :] == ids[None, :, None]
        route_grad += jnp.sum(jnp.where(named, combines[step][None], 0.0), axis=1)
    hidden_grad = jnp.transpose(placed[:, :, :most], (1, 0, 2, 3)).reshape(saved_hidden.shape)
    route_grad = ROUTE_SCALE * route_grad.T
    affinity_grad = (route_grad - jnp.sum(route_grad * shares, axis=-1, keepdims=True)) / totals
    down_grad = half_grad(mine, [scatter2, scatter3], late, [later, early], experts, 896, True)
    return (affinity_grad, hidden_grad, down_grad)


def on_device(grad_out, routes, affinity, saved_hidden, down_proj):
    reps, sources = lax.axis_size("rep"), lax.axis_size("exp")
    block, experts, width = down_proj.shape
    tokens, top_k = routes.shape
    most = saved_hidden.shape[3]
    fits = block == 128 and tokens == 128 and width % 3584 == 0 and reps == 8 and 8 % experts == 0
    fits = fits and sources == 4 and most + top_k <= SLOT_PAD and top_k <= 8
    if fits and sources * tokens <= 2 * block * experts:
        return on_device_tokens(grad_out, routes, affinity, saved_hidden, down_proj)
    return on_device_weights(grad_out, routes, affinity, saved_hidden, down_proj)


def solution(mesh):
    return jax.shard_map(
        on_device,
        mesh=mesh,
        in_specs=(
            P(("rep", "exp"), None),
            P(("rep", "exp"), None),
            P(("rep", "exp"), None),
            P("rep", "exp", None, None, None),
            P("rep", "exp", None),
        ),
        out_specs=(
            P(("rep", "exp"), None),
            P("rep", "exp", None, None, None),
            P("rep", "exp", None),
        ),
        check_vma=False,
    )
```

```python
import functools
import jax
import jax.numpy as jnp
from jax import lax
from jax.experimental import pallas as pl
from jax.experimental.pallas import tpu as pltpu
from jax.sharding import PartitionSpec as P

ROUTE_SCALE = 2.5


def pack_routes(grad_rows, route_ids, route_weight, expert_count, most):
    expert_ids = jnp.arange(expert_count, dtype=jnp.int32)
    naming = jnp.sum((route_ids[:, :, None] == expert_ids[None, None, :]).astype(jnp.int32), axis=1)
    before = jnp.cumsum(naming, axis=0) - naming
    slot_ids = jnp.take_along_axis(before, route_ids, axis=1)
    placed = (route_ids * most + slot_ids).reshape(-1)
    token_ids = jnp.repeat(jnp.arange(grad_rows.shape[0], dtype=jnp.int32), route_ids.shape[1])
    source = jnp.zeros((expert_count * most,), jnp.int32).at[placed].set(token_ids)
    filled = jnp.zeros((expert_count * most,), jnp.int32).at[placed].set(1)
    weights = (
        jnp.zeros((expert_count * most,), route_weight.dtype)
        .at[placed]
        .set(route_weight.reshape(-1))
    )
    fetched = jnp.take(grad_rows, source, axis=0)
    packed = jnp.where(filled[:, None] > 0, fetched, jnp.zeros_like(fetched))
    return (packed, weights, placed)


def on_device_weights(grad_out, routes, affinity, saved_hidden, down_proj):
    exp_devices = lax.axis_size("exp")
    local_experts = down_proj.shape[1]
    expert_count = exp_devices * local_experts
    most = saved_hidden.shape[3]
    width = grad_out.shape[1]
    hidden_units = saved_hidden.shape[4]
    row_count = exp_devices * most
    totals = jnp.sum(affinity, axis=-1, keepdims=True)
    shares = affinity / totals
    route_weight = (ROUTE_SCALE * shares).astype(jnp.bfloat16)
    packed, weights, placed = pack_routes(grad_out, routes, route_weight, expert_count, most)
    outgoing = packed.reshape(exp_devices, local_experts, 1, most, width)
    outgoing_weight = weights.reshape(exp_devices, local_experts, 1, most)
    received, received_weight = (
        lax.all_to_all(outgoing, "exp", split_axis=0, concat_axis=2, tiled=True),
        lax.all_to_all(outgoing_weight, "exp", split_axis=0, concat_axis=2, tiled=True),
    )
    received = received.reshape(local_experts, row_count, width)
    row_scale = received_weight.reshape(local_experts, row_count).astype(jnp.float32)
    hidden = saved_hidden.reshape(local_experts, row_count, hidden_units)
    gathered = lax.all_gather(down_proj, "rep", axis=0, tiled=True)
    projected = jnp.einsum("erd,hed->erh", received, gathered, preferred_element_type=jnp.float32)
    hidden_grad = (row_scale[:, :, None] * projected).astype(jnp.bfloat16)
    combine_grad = ROUTE_SCALE * jnp.sum(hidden.astype(jnp.float32) * projected, axis=-1)
    scaled = (row_scale[:, :, None] * received.astype(jnp.float32)).astype(jnp.bfloat16)
    grad_term = jnp.einsum("erh,erd->hed", hidden, scaled, preferred_element_type=jnp.float32)
    down_grad = lax.psum_scatter(
        grad_term.astype(jnp.bfloat16), "rep", scatter_dimension=0, tiled=True
    ).astype(jnp.float32)
    returned = lax.all_to_all(
        combine_grad.reshape(local_experts, exp_devices, most),
        "exp",
        split_axis=1,
        concat_axis=0,
        tiled=True,
    )
    route_grad = jnp.take(returned.reshape(-1), placed).reshape(routes.shape)
    affinity_grad = (route_grad - jnp.sum(route_grad * shares, axis=-1, keepdims=True)) / totals
    return (affinity_grad, hidden_grad.reshape(saved_hidden.shape), down_grad)


SLOT_PAD = 64
F32 = jnp.float32
BF16 = jnp.bfloat16
VMEM_BYTES = 30 * 2**20


def nt_dot(a, b):
    return lax.dot_general(a, b, (((1,), (1,)), ((), ())), preferred_element_type=F32)


def tn_dot(a, b):
    return lax.dot_general(a, b, (((0,), (0,)), ((), ())), preferred_element_type=F32)


def project_kernel(top_k, sizes, items, idx_ref, *refs):
    parts = len(sizes)
    pieces, weight_refs = refs[:parts], refs[parts : parts + 2]
    hidden_refs = refs[parts + 2 : parts + 2 + items]
    grad_refs = refs[parts + 2 + items : parts + 2 + 2 * items]
    scatter_ref, rows, weight, terms, slot_ref, scale_ref, sems = refs[parts + 2 + 2 * items :]
    step = pl.program_id(0)
    group, slots, pair = grad_refs[0].shape
    block = pair // 2
    tokens = rows.shape[0] // items
    experts = slot_ref.shape[0]

    @pl.when(step == 0)
    def _():
        copies, at = [], 0
        for i, size in enumerate(sizes):
            copies.append(pltpu.make_async_copy(pieces[i], rows.at[at : at + size], sems.at[i]))
            at += size
        for copy in copies:
            copy.start()
        metas = [hidden_refs[i][0, 0][slots - 8 :].astype(F32)[8 - top_k :] for i in range(items)]
        fill = jnp.full((8 - items, tokens), -1.0, F32)
        routes = [jnp.concatenate([m[k : k + 1, :tokens] for m in metas] + [fill], axis=0) for k in range(top_k)]
        weights = [jnp.concatenate([m[k : k + 1, tokens:] for m in metas] + [fill], axis=0) for k in range(top_k)]
        earlier = (
            lax.broadcasted_iota(jnp.int32, (tokens, tokens), 0)
            < lax.broadcasted_iota(jnp.int32, (tokens, tokens), 1)
        ).astype(BF16)
        every = []
        for e in range(experts):
            expert = (idx_ref[4] + e).astype(F32)
            named = jnp.zeros((8, tokens), F32)
            scale = jnp.zeros((8, tokens), F32)
            for k in range(top_k):
                hit = routes[k] == expert
                named = jnp.where(hit, 1.0, named)
                scale = jnp.where(hit, weights[k], scale)
            scale_ref[e] = scale
            every.append(named)
        named = jnp.concatenate(every, axis=0)
        before = jnp.dot(named.astype(BF16), earlier, preferred_element_type=F32)
        slot = jnp.where(named > 0, before, -1.0)
        for e in range(experts):
            slot_ref[e] = slot[e * 8 : (e + 1) * 8]
        for copy in copies:
            copy.wait()

    for q in range(group):
        for c in range(2):
            at = q * pair + c * block
            weight[at : at + block, :] = weight_refs[c][0, q * block : (q + 1) * block]
    projected = nt_dot(weight[...], rows[...])
    slot_ids = lax.broadcasted_iota(jnp.int32, (slots, tokens), 0).astype(F32)
    slot_rows = lax.broadcasted_iota(jnp.int32, (slots, pair), 0)
    for q in range(group):
        e = step * group + q
        slot_all, scale_all = slot_ref[e], scale_ref[e]
        for i in range(items):
            scale = scale_all[i : i + 1]
            pick = (slot_all[i : i + 1] == slot_ids).astype(BF16)
            own = projected[q * pair : (q + 1) * pair, i * tokens : (i + 1) * tokens]
            hidden = tn_dot(hidden_refs[i][q, 0], pick)
            grad = nt_dot(pick, (scale * own).astype(BF16))
            combine = jnp.sum(hidden * own, axis=0, keepdims=True)
            high = combine.astype(BF16).astype(F32)
            partial = jnp.concatenate([high, combine - high], axis=1)
            grad_refs[i][q] = jnp.where(slot_rows == slots - top_k, partial, grad).astype(BF16)
            scatter = (scale * hidden).astype(BF16)
            for half in range(2):
                at = pl.ds(pl.multiple_of(e * block, block), block)
                terms[half, at, i * tokens : (i + 1) * tokens] = scatter[half * block : (half + 1) * block]

    @pl.when(step == pl.num_programs(0) - 1)
    def _():
        height = terms.shape[1]
        row = lax.broadcasted_iota(jnp.int32, (height, height), 0)
        col = lax.broadcasted_iota(jnp.int32, (8, height), 1)
        shift = block.bit_length() - 1
        to = (jnp.bitwise_and(col, block - 1) * experts + jnp.right_shift(col, shift))[0:1]
        order = (row == to).astype(BF16)
        for half in range(2):
            scatter_ref[half] = jnp.dot(order, terms[half], preferred_element_type=F32).astype(BF16)


def project(index, items, weights, hidden, top_k, group=2):
    experts, sources, slots, pair = hidden[0].shape
    width = weights.shape[2]
    pieces = [piece for rows, _, _ in items for piece in rows]
    sizes = [p.shape[0] for p in pieces]
    count = sum(sizes)
    block = pair // 2
    return pl.pallas_call(
        functools.partial(project_kernel, top_k, sizes, len(items)),
        grid_spec=pltpu.PrefetchScalarGridSpec(
            num_scalar_prefetch=1,
            grid=(experts // group,),
            in_specs=[pl.BlockSpec(memory_space=pl.ANY)] * len(sizes)
            + [pl.BlockSpec((1, group * block, width), lambda e, idx, c=c: (c, e, 0)) for c in range(2)]
            + [
                pl.BlockSpec((group, 1, slots, pair), lambda e, idx, k=k: (e, idx[k], 0, 0))
                for _, _, k in items
            ],
            out_specs=[pl.BlockSpec((group, slots, pair), lambda e, idx: (e, 0, 0))] * len(items)
            + [pl.BlockSpec((2, experts * block, count), lambda e, idx: (0, 0, 0))],
            scratch_shapes=[
                pltpu.VMEM((count, width), BF16),
                pltpu.VMEM((group * pair, width), BF16),
                pltpu.VMEM((2, experts * block, count), BF16),
                pltpu.VMEM((experts, 8, block), F32),
                pltpu.VMEM((experts, 8, block), F32),
                pltpu.SemaphoreType.DMA((len(sizes),)),
            ],
        ),
        out_shape=[jax.ShapeDtypeStruct((experts, slots, pair), BF16)] * len(items)
        + [jax.ShapeDtypeStruct((2, experts * block, count), BF16)],
        compiler_params=pltpu.CompilerParams(vmem_limit_bytes=VMEM_BYTES),
        cost_estimate=pl.CostEstimate(
            flops=4 * count * width * experts * pair,
            bytes_accessed=2 * (count * width + weights.size),
            transcendentals=0,
        ),
    )(index, *pieces, weights, weights, *[hidden[m] for _, m, _ in items])


def fill_rows(pieces, rows):
    at = 0
    for piece in pieces:
        size = piece.shape[0]
        rows[at : at + size, :] = piece[...]
        at += size


def sum_terms(scatters, rows, half):
    total, at = None, 0
    for scatter in scatters:
        count = scatter.shape[2]
        term = jnp.dot(scatter[half], rows[at : at + count, :], preferred_element_type=F32)
        total = term if total is None else total + term
        at += count
    return total


def half_grad_kernel(terms, arrivals, last, *refs):
    scatters, arrived = refs[:terms], refs[terms : terms + arrivals]
    pieces, (out_ref, rows) = refs[terms + arrivals : -2], refs[-2:]
    fill_rows(pieces, rows)
    total = sum_terms(scatters, rows, 0)
    for array in arrived:
        total += array[...].astype(F32)
    if not last:
        out_ref[...] = total.astype(BF16)
        return
    out_ref[...] = total.reshape(out_ref.shape)


def half_grad(half, scatters, pieces, arrived, experts, tile, last):
    height = scatters[0].shape[1]
    width = pieces[0].shape[1]
    count = sum(p.shape[0] for p in pieces)
    in_specs = [pl.BlockSpec((1,) + a.shape[1:], lambda i: (half, 0, 0)) for a in scatters]
    in_specs += [pl.BlockSpec((height, tile), lambda i: (0, i)) for _ in arrived]
    in_specs += [pl.BlockSpec((p.shape[0], tile), lambda i: (0, i)) for p in pieces]
    scratch = [pltpu.VMEM((count, tile), BF16)]
    if last:
        out_spec = pl.BlockSpec((height // experts, experts, tile), lambda i: (0, 0, i))
        out_shape = jax.ShapeDtypeStruct((height // experts, experts, width), F32)
    else:
        out_spec = pl.BlockSpec((height, tile), lambda i: (0, i))
        out_shape = jax.ShapeDtypeStruct((height, width), BF16)
    return pl.pallas_call(
        functools.partial(half_grad_kernel, len(scatters), len(arrived), last),
        grid=(width // tile,),
        in_specs=in_specs,
        out_specs=out_spec,
        out_shape=out_shape,
        scratch_shapes=scratch,
        compiler_params=pltpu.CompilerParams(vmem_limit_bytes=2 * VMEM_BYTES if last else VMEM_BYTES),
        cost_estimate=pl.CostEstimate(
            flops=2 * height * count * width,
            bytes_accessed=2 * count * (width + height) + 4 * height * width,
            transcendentals=0,
        ),
    )(*scatters, *arrived, *pieces)


def place_kernel(top_k, idx_ref, *refs):
    count = len(refs) - 3
    block = refs[0].shape[2] // 2
    pieces, (out_ref, sum_ref, out_sems) = refs[:count], refs[count:]
    experts, slots, pair = pieces[0].shape
    rows = 16
    slabs = count // 4
    stores = []
    for i in range(count):
        for half in range(2):
            column = pl.multiple_of(idx_ref[slabs + 2 * (i % 4) + half] * block, block)
            to = out_ref.at[idx_ref[i // 4], :, :, pl.ds(column, block)]
            part = pieces[i].at[:, :, half * block : (half + 1) * block]
            stores.append(pltpu.make_async_copy(part, to, out_sems.at[2 * i + half]))
    for copy in stores:
        copy.start()
    for k in range(slabs):
        for e in range(experts):
            total = sum(pieces[4 * k + m][e, slots - rows :].astype(F32) for m in range(4))
            row = total[rows - top_k : rows - top_k + 1]
            sum_ref[k * experts + e : k * experts + e + 1] = row[:, : pair // 2] + row[:, pair // 2 :]
    for copy in stores:
        copy.wait()


def place(index, pieces, top_k):
    experts, slots, pair = pieces[0].shape
    slabs = len(pieces) // 4
    return pl.pallas_call(
        functools.partial(place_kernel, top_k),
        grid_spec=pltpu.PrefetchScalarGridSpec(
            num_scalar_prefetch=1,
            grid=(1,),
            in_specs=[pl.BlockSpec((experts, slots, pair), lambda i, idx: (0, 0, 0))] * len(pieces),
            out_specs=[
                pl.BlockSpec(memory_space=pl.ANY),
                pl.BlockSpec((slabs * experts, pair // 2), lambda i, idx: (0, 0)),
            ],
            scratch_shapes=[
                pltpu.SemaphoreType.DMA((2 * len(pieces),)),
            ],
        ),
        out_shape=[
            jax.ShapeDtypeStruct((slabs, experts, slots, 4 * pair), BF16),
            jax.ShapeDtypeStruct((slabs * experts, pair // 2), F32),
        ],
        compiler_params=pltpu.CompilerParams(vmem_limit_bytes=61 * 2**20),
        cost_estimate=pl.CostEstimate(
            flops=0, bytes_accessed=4 * len(pieces) * experts * slots * pair, transcendentals=0
        ),
    )(index, *pieces)


def on_device_tokens(grad_out, routes, affinity, saved_hidden, down_proj):
    reps, sources = lax.axis_size("rep"), lax.axis_size("exp")
    block, experts, width = down_proj.shape
    tokens, top_k = routes.shape
    most, hidden_units = saved_hidden.shape[3:]
    pair = 2 * block
    me = lax.axis_index("exp")
    rep = lax.axis_index("rep")
    chip, core = lax.div(rep, 2), lax.rem(rep, 2)
    blocks = [2 * jnp.bitwise_xor(chip, m) + jnp.bitwise_xor(core, c) for m in range(4) for c in range(2)]

    def across(array, bits):
        return lax.ppermute(array, "rep", [(i, i ^ bits) for i in range(reps)])

    def around(array, shift):
        return lax.ppermute(array, "exp", [(i, (i + shift) % sources) for i in range(sources)])

    totals = jnp.sum(affinity, axis=-1, keepdims=True)
    shares = affinity / totals
    route_weight = (ROUTE_SCALE * shares).astype(BF16)
    meta = jnp.concatenate([routes.astype(BF16).T, route_weight.T], axis=1)
    fence = lax.optimization_barrier

    slabs = [lax.rem(me - step + sources, sources) for step in range(sources)]
    index = jnp.stack(slabs + [me * experts]).astype(jnp.int32)

    def kernel(items):
        *grads, scatter = project(index, items, weights, hidden, top_k)
        return grads, scatter

    def send_back(grads, chip_of):
        return [across(g, 2 * m) if m else g for g, m in zip(grads, chip_of)]

    x0, y0, next1 = across(grad_out, 2), across(grad_out, 4), around(grad_out, 1)
    held = jnp.transpose(saved_hidden.reshape(experts, sources, most, 8, block), (3, 0, 1, 2, 4))
    held = fence(held)
    held = [lax.dynamic_index_in_dim(held, b, axis=0, keepdims=False) for b in blocks]
    own_weight = jnp.transpose(down_proj, (1, 0, 2)).reshape(experts * block, width)
    last_meta, held, own_weight = fence((meta, held, own_weight))
    metas = [meta, around(meta, 1), around(meta, 2), around(last_meta, 3)]
    metas, x0, y0, next1, held, own_weight = fence((metas, x0, y0, next1, held, own_weight))

    xy0, x1, next2 = across(x0, 4), across(next1, 2), around(next1, 1)
    own3 = around(fence((grad_out, next2))[0], -1)
    partner_weight = across(own_weight, 1)
    metas = jnp.stack([metas[(sources - 1 - i) % sources] for i in range(2 * sources - 1)])
    metas = lax.dynamic_slice_in_dim(metas, sources - 1 - me, sources, axis=0)
    blank = jnp.zeros((experts, sources, SLOT_PAD - most - top_k, pair), BF16)
    metas = jnp.broadcast_to(metas[None], (experts, sources, top_k, pair))
    hidden = []
    for m in range(4):
        piece = jnp.concatenate([held[2 * m], held[2 * m + 1]], axis=3)
        hidden.append(jnp.concatenate([piece, blank, metas], axis=2))
    diagonal = across(hidden[3], 6)
    hidden = [
        hidden[0],
        across(fence((hidden[1], x1, diagonal))[0], 2),
        across(fence((hidden[2], xy0, diagonal))[0], 4),
        diagonal,
    ]
    weights = jnp.stack([own_weight, partner_weight])
    hidden, xy0, x1, next2, own3, weights, x0, y0, next1 = fence(
        (hidden, xy0, x1, next2, own3, weights, x0, y0, next1)
    )

    y1, x2, x3 = across(next1, 4), across(next2, 2), around(x0, -1)
    grads0, scatter0 = kernel([([grad_out], 0, 0), ([x0], 1, 0), ([y0], 2, 0), ([xy0], 3, 0)])
    y1, x2, x3, grads0, scatter0, y0, xy0, next2, x1 = fence(
        (y1, x2, x3, grads0, scatter0, y0, xy0, next2, x1)
    )

    xy1, y2, y3 = across(y1, 2), across(next2, 4), around(y0, -1)
    grads1, scatter1 = kernel(
        [([next1], 0, 1), ([x1], 1, 1), ([y1], 2, 1), ([next2], 0, 2), ([x2], 1, 2), ([x3], 1, 3)]
    )
    xy1, y2, y3, grads1, scatter1, xy0, x2, grads0 = fence((xy1, y2, y3, grads1, scatter1, xy0, x2, grads0))

    xy2, xy3 = across(x2, 4), around(xy0, -1)
    returned0 = send_back(grads0, (0, 1, 2, 3))
    returned1 = send_back(grads1, (0, 1, 2, 0, 1, 1))
    grads2, scatter2 = kernel([([xy1], 3, 1), ([y2], 2, 2), ([own3], 0, 3), ([y3], 2, 3)])
    first = [grad_out, x0, y0, xy0, next1, x1, y1, next2, x2, x3]
    mine, other = 0, 1
    partner = half_grad(other, [scatter0, scatter1], first, [], experts, 896, False)
    xy2, xy3, returned0, returned1, grads2, scatter2, partner = fence(
        (xy2, xy3, returned0, returned1, grads2, scatter2, partner)
    )

    partner = across(partner, 1)
    returned2 = send_back(grads2, (3, 2, 0, 2))
    grads3, scatter3 = kernel([([xy2], 3, 2), ([xy3], 3, 3)])
    late = [xy1, y2, own3, y3, xy2, xy3]
    later = half_grad(other, [scatter2, scatter3], late, [], experts, 896, False)
    returned3 = send_back(grads3, (3, 3))
    partner, returned2, returned3, later = fence((partner, returned2, returned3, later))
    later = across(later, 1)
    returned = [
        *returned0,
        *returned1[:3],
        returned2[0],
        returned1[3],
        returned1[4],
        returned2[1],
        returned3[0],
        returned2[2],
        returned1[5],
        returned2[3],
        returned3[1],
    ]
    placed, combine = place(jnp.stack(slabs + blocks).astype(jnp.int32), returned, top_k)
    combine = combine.reshape(sources, experts, tokens)
    combines = [combine[0], around(combine[1], -1), around(combine[2], -2), around(combine[3], 1)]
    route_grad = 0.0
    expert_ids = jnp.arange(experts, dtype=routes.dtype)
    for step in range(sources):
        ids = lax.rem(me + step, sources) * experts + expert_ids
        named = routes.T[:, None, :] == ids[None, :, None]
        route_grad += jnp.sum(jnp.where(named, combines[step][None], 0.0), axis=1)
    hidden_grad = jnp.transpose(placed[:, :, :most], (1, 0, 2, 3)).reshape(saved_hidden.shape)
    route_grad = ROUTE_SCALE * route_grad.T
    affinity_grad = (route_grad - jnp.sum(route_grad * shares, axis=-1, keepdims=True)) / totals
    scatters = [scatter0, scatter1, scatter2, scatter3]
    down_grad = half_grad(mine, scatters, first + late, [partner, later], experts, 896, True)
    return (affinity_grad, hidden_grad, down_grad)


def on_device(grad_out, routes, affinity, saved_hidden, down_proj):
    reps, sources = lax.axis_size("rep"), lax.axis_size("exp")
    block, experts, width = down_proj.shape
    tokens, top_k = routes.shape
    most = saved_hidden.shape[3]
    fits = block == 128 and tokens == 128 and width % 3584 == 0 and reps == 8 and 8 % experts == 0
    fits = fits and sources == 4 and most + top_k <= SLOT_PAD and top_k <= 8
    if fits and sources * tokens <= 2 * block * experts:
        return on_device_tokens(grad_out, routes, affinity, saved_hidden, down_proj)
    return on_device_weights(grad_out, routes, affinity, saved_hidden, down_proj)


def solution(mesh):
    return jax.shard_map(
        on_device,
        mesh=mesh,
        in_specs=(
            P(("rep", "exp"), None),
            P(("rep", "exp"), None),
            P(("rep", "exp"), None),
            P("rep", "exp", None, None, None),
            P("rep", "exp", None),
        ),
        out_specs=(
            P(("rep", "exp"), None),
            P("rep", "exp", None, None, None),
            P("rep", "exp", None),
        ),
        check_vma=False,
    )
```

```python
import functools
import jax
import jax.numpy as jnp
from jax import lax
from jax.experimental import pallas as pl
from jax.experimental.pallas import tpu as pltpu
from jax.sharding import PartitionSpec as P

ROUTE_SCALE = 2.5


def pack_routes(grad_rows, route_ids, route_weight, expert_count, most):
    expert_ids = jnp.arange(expert_count, dtype=jnp.int32)
    naming = jnp.sum((route_ids[:, :, None] == expert_ids[None, None, :]).astype(jnp.int32), axis=1)
    before = jnp.cumsum(naming, axis=0) - naming
    slot_ids = jnp.take_along_axis(before, route_ids, axis=1)
    placed = (route_ids * most + slot_ids).reshape(-1)
    token_ids = jnp.repeat(jnp.arange(grad_rows.shape[0], dtype=jnp.int32), route_ids.shape[1])
    source = jnp.zeros((expert_count * most,), jnp.int32).at[placed].set(token_ids)
    filled = jnp.zeros((expert_count * most,), jnp.int32).at[placed].set(1)
    weights = (
        jnp.zeros((expert_count * most,), route_weight.dtype)
        .at[placed]
        .set(route_weight.reshape(-1))
    )
    fetched = jnp.take(grad_rows, source, axis=0)
    packed = jnp.where(filled[:, None] > 0, fetched, jnp.zeros_like(fetched))
    return (packed, weights, placed)


def on_device_weights(grad_out, routes, affinity, saved_hidden, down_proj):
    exp_devices = lax.axis_size("exp")
    local_experts = down_proj.shape[1]
    expert_count = exp_devices * local_experts
    most = saved_hidden.shape[3]
    width = grad_out.shape[1]
    hidden_units = saved_hidden.shape[4]
    row_count = exp_devices * most
    totals = jnp.sum(affinity, axis=-1, keepdims=True)
    shares = affinity / totals
    route_weight = (ROUTE_SCALE * shares).astype(jnp.bfloat16)
    packed, weights, placed = pack_routes(grad_out, routes, route_weight, expert_count, most)
    outgoing = packed.reshape(exp_devices, local_experts, 1, most, width)
    outgoing_weight = weights.reshape(exp_devices, local_experts, 1, most)
    received, received_weight = (
        lax.all_to_all(outgoing, "exp", split_axis=0, concat_axis=2, tiled=True),
        lax.all_to_all(outgoing_weight, "exp", split_axis=0, concat_axis=2, tiled=True),
    )
    received = received.reshape(local_experts, row_count, width)
    row_scale = received_weight.reshape(local_experts, row_count).astype(jnp.float32)
    hidden = saved_hidden.reshape(local_experts, row_count, hidden_units)
    gathered = lax.all_gather(down_proj, "rep", axis=0, tiled=True)
    projected = jnp.einsum("erd,hed->erh", received, gathered, preferred_element_type=jnp.float32)
    hidden_grad = (row_scale[:, :, None] * projected).astype(jnp.bfloat16)
    combine_grad = ROUTE_SCALE * jnp.sum(hidden.astype(jnp.float32) * projected, axis=-1)
    scaled = (row_scale[:, :, None] * received.astype(jnp.float32)).astype(jnp.bfloat16)
    grad_term = jnp.einsum("erh,erd->hed", hidden, scaled, preferred_element_type=jnp.float32)
    down_grad = lax.psum_scatter(
        grad_term.astype(jnp.bfloat16), "rep", scatter_dimension=0, tiled=True
    ).astype(jnp.float32)
    returned = lax.all_to_all(
        combine_grad.reshape(local_experts, exp_devices, most),
        "exp",
        split_axis=1,
        concat_axis=0,
        tiled=True,
    )
    route_grad = jnp.take(returned.reshape(-1), placed).reshape(routes.shape)
    affinity_grad = (route_grad - jnp.sum(route_grad * shares, axis=-1, keepdims=True)) / totals
    return (affinity_grad, hidden_grad.reshape(saved_hidden.shape), down_grad)


SLOT_PAD = 64
F32 = jnp.float32
BF16 = jnp.bfloat16
VMEM_BYTES = 30 * 2**20


def nt_dot(a, b):
    return lax.dot_general(a, b, (((1,), (1,)), ((), ())), preferred_element_type=F32)


def tn_dot(a, b):
    return lax.dot_general(a, b, (((0,), (0,)), ((), ())), preferred_element_type=F32)


def project_kernel(top_k, sizes, items, idx_ref, *refs):
    parts = len(sizes)
    pieces, weight_refs = refs[:parts], refs[parts : parts + 2]
    hidden_refs = refs[parts + 2 : parts + 2 + items]
    grad_refs = refs[parts + 2 + items : parts + 2 + 2 * items]
    scatter_ref, rows, weight, terms, slot_ref, scale_ref, sems = refs[parts + 2 + 2 * items :]
    step = pl.program_id(0)
    group, slots, pair = grad_refs[0].shape
    block = pair // 2
    tokens = rows.shape[0] // items
    experts = slot_ref.shape[0]

    @pl.when(step == 0)
    def _():
        copies, at = [], 0
        for i, size in enumerate(sizes):
            copies.append(pltpu.make_async_copy(pieces[i], rows.at[at : at + size], sems.at[i]))
            at += size
        for copy in copies:
            copy.start()
        metas = [hidden_refs[i][0, 0][slots - 8 :].astype(F32)[8 - top_k :] for i in range(items)]
        fill = jnp.full((8 - items, tokens), -1.0, F32)
        routes = [jnp.concatenate([m[k : k + 1, :tokens] for m in metas] + [fill], axis=0) for k in range(top_k)]
        weights = [jnp.concatenate([m[k : k + 1, tokens:] for m in metas] + [fill], axis=0) for k in range(top_k)]
        earlier = (
            lax.broadcasted_iota(jnp.int32, (tokens, tokens), 0)
            < lax.broadcasted_iota(jnp.int32, (tokens, tokens), 1)
        ).astype(BF16)
        every = []
        for e in range(experts):
            expert = (idx_ref[4] + e).astype(F32)
            named = jnp.zeros((8, tokens), F32)
            scale = jnp.zeros((8, tokens), F32)
            for k in range(top_k):
                hit = routes[k] == expert
                named = jnp.where(hit, 1.0, named)
                scale = jnp.where(hit, weights[k], scale)
            scale_ref[e] = scale
            every.append(named)
        named = jnp.concatenate(every, axis=0)
        before = jnp.dot(named.astype(BF16), earlier, preferred_element_type=F32)
        slot = jnp.where(named > 0, before, -1.0)
        for e in range(experts):
            slot_ref[e] = slot[e * 8 : (e + 1) * 8]
        for copy in copies:
            copy.wait()

    for q in range(group):
        for c in range(2):
            at = q * pair + c * block
            weight[at : at + block, :] = weight_refs[c][0, q * block : (q + 1) * block]
    projected = nt_dot(weight[...], rows[...])
    slot_ids = lax.broadcasted_iota(jnp.int32, (slots, tokens), 0).astype(F32)
    slot_rows = lax.broadcasted_iota(jnp.int32, (slots, pair), 0)
    for q in range(group):
        e = step * group + q
        slot_all, scale_all = slot_ref[e], scale_ref[e]
        for i in range(items):
            scale = scale_all[i : i + 1]
            pick = (slot_all[i : i + 1] == slot_ids).astype(BF16)
            own = projected[q * pair : (q + 1) * pair, i * tokens : (i + 1) * tokens]
            hidden = tn_dot(hidden_refs[i][q, 0], pick)
            grad = nt_dot(pick, (scale * own).astype(BF16))
            combine = jnp.sum(hidden * own, axis=0, keepdims=True)
            high = combine.astype(BF16).astype(F32)
            partial = jnp.concatenate([high, combine - high], axis=1)
            grad_refs[i][q] = jnp.where(slot_rows == slots - top_k, partial, grad).astype(BF16)
            scatter = (scale * hidden).astype(BF16)
            for half in range(2):
                at = pl.ds(pl.multiple_of(e * block, block), block)
                terms[half, at, i * tokens : (i + 1) * tokens] = scatter[half * block : (half + 1) * block]

    @pl.when(step == pl.num_programs(0) - 1)
    def _():
        height = terms.shape[1]
        row = lax.broadcasted_iota(jnp.int32, (height, height), 0)
        col = lax.broadcasted_iota(jnp.int32, (8, height), 1)
        shift = block.bit_length() - 1
        to = (jnp.bitwise_and(col, block - 1) * experts + jnp.right_shift(col, shift))[0:1]
        order = (row == to).astype(BF16)
        for half in range(2):
            scatter_ref[half] = jnp.dot(order, terms[half], preferred_element_type=F32).astype(BF16)


def project(index, items, weights, hidden, top_k, group=2):
    experts, sources, slots, pair = hidden[0].shape
    width = weights.shape[2]
    pieces = [piece for rows, _, _ in items for piece in rows]
    sizes = [p.shape[0] for p in pieces]
    count = sum(sizes)
    block = pair // 2
    return pl.pallas_call(
        functools.partial(project_kernel, top_k, sizes, len(items)),
        grid_spec=pltpu.PrefetchScalarGridSpec(
            num_scalar_prefetch=1,
            grid=(experts // group,),
            in_specs=[pl.BlockSpec(memory_space=pl.ANY)] * len(sizes)
            + [pl.BlockSpec((1, group * block, width), lambda e, idx, c=c: (c, e, 0)) for c in range(2)]
            + [
                pl.BlockSpec((group, 1, slots, pair), lambda e, idx, k=k: (e, idx[k], 0, 0))
                for _, _, k in items
            ],
            out_specs=[pl.BlockSpec((group, slots, pair), lambda e, idx: (e, 0, 0))] * len(items)
            + [pl.BlockSpec((2, experts * block, count), lambda e, idx: (0, 0, 0))],
            scratch_shapes=[
                pltpu.VMEM((count, width), BF16),
                pltpu.VMEM((group * pair, width), BF16),
                pltpu.VMEM((2, experts * block, count), BF16),
                pltpu.VMEM((experts, 8, block), F32),
                pltpu.VMEM((experts, 8, block), F32),
                pltpu.SemaphoreType.DMA((len(sizes),)),
            ],
        ),
        out_shape=[jax.ShapeDtypeStruct((experts, slots, pair), BF16)] * len(items)
        + [jax.ShapeDtypeStruct((2, experts * block, count), BF16)],
        compiler_params=pltpu.CompilerParams(vmem_limit_bytes=VMEM_BYTES),
        cost_estimate=pl.CostEstimate(
            flops=4 * count * width * experts * pair,
            bytes_accessed=2 * (count * width + weights.size),
            transcendentals=0,
        ),
    )(index, *pieces, weights, weights, *[hidden[m] for _, m, _ in items])


def fill_rows(pieces, rows):
    at = 0
    for piece in pieces:
        size = piece.shape[0]
        rows[at : at + size, :] = piece[...]
        at += size


def sum_terms(scatters, rows, half):
    total, at = None, 0
    for scatter in scatters:
        count = scatter.shape[2]
        term = jnp.dot(scatter[half], rows[at : at + count, :], preferred_element_type=F32)
        total = term if total is None else total + term
        at += count
    return total


def half_grad_kernel(terms, arrivals, last, *refs):
    scatters, arrived = refs[:terms], refs[terms : terms + arrivals]
    pieces, (out_ref, rows) = refs[terms + arrivals : -2], refs[-2:]
    fill_rows(pieces, rows)
    total = sum_terms(scatters, rows, 0)
    for array in arrived:
        total += array[...].astype(F32)
    if not last:
        out_ref[...] = total.astype(BF16)
        return
    out_ref[...] = total.reshape(out_ref.shape)


def half_grad(half, scatters, pieces, arrived, experts, tile, last):
    height = scatters[0].shape[1]
    width = pieces[0].shape[1]
    count = sum(p.shape[0] for p in pieces)
    in_specs = [pl.BlockSpec((1,) + a.shape[1:], lambda i: (half, 0, 0)) for a in scatters]
    in_specs += [pl.BlockSpec((height, tile), lambda i: (0, i)) for _ in arrived]
    in_specs += [pl.BlockSpec((p.shape[0], tile), lambda i: (0, i)) for p in pieces]
    scratch = [pltpu.VMEM((count, tile), BF16)]
    if last:
        out_spec = pl.BlockSpec((height // experts, experts, tile), lambda i: (0, 0, i))
        out_shape = jax.ShapeDtypeStruct((height // experts, experts, width), F32)
    else:
        out_spec = pl.BlockSpec((height, tile), lambda i: (0, i))
        out_shape = jax.ShapeDtypeStruct((height, width), BF16)
    return pl.pallas_call(
        functools.partial(half_grad_kernel, len(scatters), len(arrived), last),
        grid=(width // tile,),
        in_specs=in_specs,
        out_specs=out_spec,
        out_shape=out_shape,
        scratch_shapes=scratch,
        compiler_params=pltpu.CompilerParams(vmem_limit_bytes=2 * VMEM_BYTES if last else VMEM_BYTES),
        cost_estimate=pl.CostEstimate(
            flops=2 * height * count * width,
            bytes_accessed=2 * count * (width + height) + 4 * height * width,
            transcendentals=0,
        ),
    )(*scatters, *arrived, *pieces)


def place_kernel(top_k, idx_ref, *refs):
    count = len(refs) - 3
    block = refs[0].shape[2] // 2
    pieces, (out_ref, sum_ref, out_sems) = refs[:count], refs[count:]
    experts, slots, pair = pieces[0].shape
    rows = 16
    slabs = count // 4
    stores = []
    for i in range(count):
        for half in range(2):
            column = pl.multiple_of(idx_ref[slabs + 2 * (i % 4) + half] * block, block)
            to = out_ref.at[idx_ref[i // 4], :, :, pl.ds(column, block)]
            part = pieces[i].at[:, :, half * block : (half + 1) * block]
            stores.append(pltpu.make_async_copy(part, to, out_sems.at[2 * i + half]))
    for copy in stores:
        copy.start()
    for k in range(slabs):
        for e in range(experts):
            total = sum(pieces[4 * k + m][e, slots - rows :].astype(F32) for m in range(4))
            row = total[rows - top_k : rows - top_k + 1]
            sum_ref[k * experts + e : k * experts + e + 1] = row[:, : pair // 2] + row[:, pair // 2 :]
    for copy in stores:
        copy.wait()


def place(index, pieces, top_k):
    experts, slots, pair = pieces[0].shape
    slabs = len(pieces) // 4
    return pl.pallas_call(
        functools.partial(place_kernel, top_k),
        grid_spec=pltpu.PrefetchScalarGridSpec(
            num_scalar_prefetch=1,
            grid=(1,),
            in_specs=[pl.BlockSpec((experts, slots, pair), lambda i, idx: (0, 0, 0))] * len(pieces),
            out_specs=[
                pl.BlockSpec(memory_space=pl.ANY),
                pl.BlockSpec((slabs * experts, pair // 2), lambda i, idx: (0, 0)),
            ],
            scratch_shapes=[
                pltpu.SemaphoreType.DMA((2 * len(pieces),)),
            ],
        ),
        out_shape=[
            jax.ShapeDtypeStruct((slabs, experts, slots, 4 * pair), BF16),
            jax.ShapeDtypeStruct((slabs * experts, pair // 2), F32),
        ],
        compiler_params=pltpu.CompilerParams(vmem_limit_bytes=61 * 2**20),
        cost_estimate=pl.CostEstimate(
            flops=0, bytes_accessed=4 * len(pieces) * experts * slots * pair, transcendentals=0
        ),
    )(index, *pieces)


def on_device_tokens(grad_out, routes, affinity, saved_hidden, down_proj):
    reps, sources = lax.axis_size("rep"), lax.axis_size("exp")
    block, experts, width = down_proj.shape
    tokens, top_k = routes.shape
    most, hidden_units = saved_hidden.shape[3:]
    pair = 2 * block
    me = lax.axis_index("exp")
    rep = lax.axis_index("rep")
    chip, core = lax.div(rep, 2), lax.rem(rep, 2)
    blocks = [2 * jnp.bitwise_xor(chip, m) + jnp.bitwise_xor(core, c) for m in range(4) for c in range(2)]

    def across(array, bits):
        return lax.ppermute(array, "rep", [(i, i ^ bits) for i in range(reps)])

    def around(array, shift):
        return lax.ppermute(array, "exp", [(i, (i + shift) % sources) for i in range(sources)])

    totals = jnp.sum(affinity, axis=-1, keepdims=True)
    shares = affinity / totals
    route_weight = (ROUTE_SCALE * shares).astype(BF16)
    meta = jnp.concatenate([routes.astype(BF16).T, route_weight.T], axis=1)
    fence = lax.optimization_barrier

    slabs = [lax.rem(me - step + sources, sources) for step in range(sources)]
    index = jnp.stack(slabs + [me * experts]).astype(jnp.int32)

    def kernel(items):
        *grads, scatter = project(index, items, weights, hidden, top_k)
        return grads, scatter

    def send_back(grads, chip_of):
        return [across(g, 2 * m) if m else g for g, m in zip(grads, chip_of)]

    x0, y0, next1 = across(grad_out, 2), across(grad_out, 4), around(grad_out, 1)
    held = jnp.transpose(saved_hidden.reshape(experts, sources, most, 8, block), (3, 0, 1, 2, 4))
    held = fence(held)
    held = [lax.dynamic_index_in_dim(held, b, axis=0, keepdims=False) for b in blocks]
    own_weight = jnp.transpose(down_proj, (1, 0, 2)).reshape(experts * block, width)
    last_meta, held, own_weight = fence((meta, held, own_weight))
    metas = [meta, around(meta, 1), around(meta, 2), around(last_meta, 3)]
    metas, x0, y0, next1, held, own_weight = fence((metas, x0, y0, next1, held, own_weight))

    xy0, x1, next2 = across(x0, 4), across(next1, 2), around(next1, 1)
    own3 = around(fence((grad_out, next2))[0], -1)
    partner_weight = across(own_weight, 1)
    metas = jnp.stack([metas[(sources - 1 - i) % sources] for i in range(2 * sources - 1)])
    metas = lax.dynamic_slice_in_dim(metas, sources - 1 - me, sources, axis=0)
    blank = jnp.zeros((experts, sources, SLOT_PAD - most - top_k, pair), BF16)
    metas = jnp.broadcast_to(metas[None], (experts, sources, top_k, pair))
    hidden = []
    for m in range(4):
        piece = jnp.concatenate([held[2 * m], held[2 * m + 1]], axis=3)
        hidden.append(jnp.concatenate([piece, blank, metas], axis=2))
    diagonal = across(hidden[3], 6)
    hidden = [
        hidden[0],
        across(fence((hidden[1], x1, diagonal))[0], 2),
        across(fence((hidden[2], xy0, diagonal))[0], 4),
        diagonal,
    ]
    weights = jnp.stack([own_weight, partner_weight])
    hidden, xy0, x1, next2, own3, weights, x0, y0, next1 = fence(
        (hidden, xy0, x1, next2, own3, weights, x0, y0, next1)
    )

    y1, x2, x3 = across(next1, 4), across(next2, 2), around(x0, -1)
    grads0, scatter0 = kernel([([grad_out], 0, 0), ([x0], 1, 0), ([y0], 2, 0), ([xy0], 3, 0)])
    y1, x2, x3, grads0, scatter0, y0, xy0, next2, x1 = fence(
        (y1, x2, x3, grads0, scatter0, y0, xy0, next2, x1)
    )

    xy1, y2, y3 = across(y1, 2), across(next2, 4), around(y0, -1)
    grads1, scatter1 = kernel(
        [([next1], 0, 1), ([x1], 1, 1), ([y1], 2, 1), ([next2], 0, 2), ([x2], 1, 2), ([x3], 1, 3)]
    )
    xy1, y2, y3, grads1, scatter1, xy0, x2, grads0 = fence((xy1, y2, y3, grads1, scatter1, xy0, x2, grads0))

    xy2, xy3 = across(x2, 4), around(xy0, -1)
    returned0 = send_back(grads0, (0, 1, 2, 3))
    returned1 = send_back(grads1, (0, 1, 2, 0, 1, 1))
    grads2, scatter2 = kernel([([xy1], 3, 1), ([y2], 2, 2), ([own3], 0, 3), ([y3], 2, 3)])
    first = [grad_out, x0, y0, xy0, next1, x1, y1, next2, x2, x3]
    mine, other = 0, 1
    partner = half_grad(other, [scatter0, scatter1], first, [], experts, 896, False)
    xy2, xy3, returned0, returned1, grads2, scatter2, partner = fence(
        (xy2, xy3, returned0, returned1, grads2, scatter2, partner)
    )

    partner = across(partner, 1)
    returned2 = send_back(grads2, (3, 2, 0, 2))
    grads3, scatter3 = kernel([([xy2], 3, 2), ([xy3], 3, 3)])
    late = [xy1, y2, own3, y3, xy2, xy3]
    later = half_grad(other, [scatter2, scatter3], late, [], experts, 896, False)
    returned3 = send_back(grads3, (3, 3))
    partner, returned2, returned3, later = fence((partner, returned2, returned3, later))
    later = across(later, 1)
    returned = [
        *returned0,
        *returned1[:3],
        returned2[0],
        returned1[3],
        returned1[4],
        returned2[1],
        returned3[0],
        returned2[2],
        returned1[5],
        returned2[3],
        returned3[1],
    ]
    placed, combine = place(jnp.stack(slabs + blocks).astype(jnp.int32), returned, top_k)
    combine = combine.reshape(sources, experts, tokens)
    combines = [combine[0], around(combine[1], -1), around(combine[2], -2), around(combine[3], 1)]
    route_grad = 0.0
    expert_ids = jnp.arange(experts, dtype=routes.dtype)
    for step in range(sources):
        ids = lax.rem(me + step, sources) * experts + expert_ids
        named = routes.T[:, None, :] == ids[None, :, None]
        route_grad += jnp.sum(jnp.where(named, combines[step][None], 0.0), axis=1)
    hidden_grad = jnp.transpose(placed[:, :, :most], (1, 0, 2, 3)).reshape(saved_hidden.shape)
    route_grad = ROUTE_SCALE * route_grad.T
    affinity_grad = (route_grad - jnp.sum(route_grad * shares, axis=-1, keepdims=True)) / totals
    scatters = [scatter0, scatter1, scatter2, scatter3]
    down_grad = half_grad(mine, scatters, first + late, [partner, later], experts, 512, True)
    return (affinity_grad, hidden_grad, down_grad)


def on_device(grad_out, routes, affinity, saved_hidden, down_proj):
    reps, sources = lax.axis_size("rep"), lax.axis_size("exp")
    block, experts, width = down_proj.shape
    tokens, top_k = routes.shape
    most = saved_hidden.shape[3]
    fits = block == 128 and tokens == 128 and width % 3584 == 0 and reps == 8 and 8 % experts == 0
    fits = fits and sources == 4 and most + top_k <= SLOT_PAD and top_k <= 8
    if fits and sources * tokens <= 2 * block * experts:
        return on_device_tokens(grad_out, routes, affinity, saved_hidden, down_proj)
    return on_device_weights(grad_out, routes, affinity, saved_hidden, down_proj)


def solution(mesh):
    return jax.shard_map(
        on_device,
        mesh=mesh,
        in_specs=(
            P(("rep", "exp"), None),
            P(("rep", "exp"), None),
            P(("rep", "exp"), None),
            P("rep", "exp", None, None, None),
            P("rep", "exp", None),
        ),
        out_specs=(
            P(("rep", "exp"), None),
            P("rep", "exp", None, None, None),
            P("rep", "exp", None),
        ),
        check_vma=False,
    )
```
